512 devices in a mesh: section: 8 (over y, core), dp: 64 (over z, x).
Axes of the slice: x: 4, y: 4, z: 16, core: 2. Of those that a mesh axis runs over, the one named last changes fastest.
Arguments:
- source_tokens: bfloat16 [16384, 2048], P('dp'), may hold values from -6 to 6
- send_counts: int32 [64, 64], replicated, may hold values from 0 to 4, as said below
- doc_segments: int32 [256, 32], P('dp'), may hold values from 0 to 7, never falling along the last dimension, each value on 1 to 16 neighbouring positions
- out_cotangent: bfloat16 [8192, 2048], P('dp'), may hold values from -0.01953125 to 0.01953125
- norm_gain: float32 [8, 2048], P('section'), may hold values from 0.25 to 1.75
- query_weight: bfloat16 [8, 2048, 1024], P('section', 'dp'), may hold values from -0.125 to 0.125
- frozen_key_matrix: bfloat16 [8, 2048, 256], P('section', 'dp'), may hold values from -0.125 to 0.125
- frozen_value_matrix: bfloat16 [8, 2048, 256], P('section', 'dp'), may hold values from -0.125 to 0.125
- out_weight: bfloat16 [8, 1024, 2048], P('section', 'dp'), may hold values from -0.1875 to 0.1875
- adapter_down: bfloat16 [8, 2, 2048, 16], P('section'), may hold values from -0.125 to 0.125
- adapter_up_maps: bfloat16 [8, 16, 1280], P('section'), may hold values from -0.1875 to 0.1875
Outputs:
- down_grads: float32 [8, 2, 2048, 16], P('section')
- up_grads: float32 [8, 16, 1280], P('section')
The draws below stay inside these ranges and needn't reach their ends.
Inputs may be any that keep to these rules, and one draw needn't show every extreme that they name: `send_counts`: entry [s, d] counts tokens from replica s to replica d. Every column holds exactly one entry 4 and at least one entry 0; every column sums to at most 128, and some column sums to exactly that. `doc_segments`: segment ids never fall along a micro-batch; a segment spans at most 16 positions.
All inputs are finite; a program needn't handle non-finite values.
Results may differ from the reference program's by a relative error of at most 0.035.
Values may be sent and summed in bfloat16 or wider, within the bound.
No kernel may reach another device: no remote copies, remote signals or barrier semaphores. Data moves between devices by JAX's collectives and lax.ppermute only.
A program may use at most 64 MiB of HBM per device.

```python
import math
import jax
import jax.numpy as jnp
import numpy as np
from jax import lax

MODEL_WIDTH = 2048
QUERY_HEADS = 16
KEY_VALUE_HEADS = 4
HEAD_SIZE = 64
ADAPTER_RANK = 16
M = 4
TOK = 32
REPLICAS = 64
SECTION_COUNT = 8
CAP = 4


def draw_send_counts(key, part):
    key = jax.random.fold_in(key, 7)
    keys_all = jax.random.split(key, 5)
    half_cap = CAP // 2
    first_pick = jax.random.randint(keys_all[0], (REPLICAS, REPLICAS), 0, half_cap + 1)
    second_pick = jax.random.randint(keys_all[1], (REPLICAS, REPLICAS), 0, half_cap + 1)
    counts = jnp.minimum(first_pick, second_pick)
    full_column = jax.random.randint(keys_all[2], (), 0, REPLICAS)
    columns = jnp.arange(REPLICAS)
    counts = jnp.where(columns[None, :] == full_column, half_cap, counts)
    heavy_row = jax.random.randint(keys_all[3], (REPLICAS,), 0, REPLICAS)
    empty_row = (heavy_row + jax.random.randint(keys_all[4], (REPLICAS,), 1, REPLICAS)) % REPLICAS
    sources = jnp.arange(REPLICAS)[:, None]
    counts = jnp.where(sources == heavy_row[None, :], CAP, counts)
    counts = jnp.where(sources == empty_row[None, :], 0, counts)
    return counts.astype(jnp.int32)


def steps_of(rng, shape, cuts, smallest, top_value):
    factor_of, own = 1.0, jax.random.fold_in(rng, 6)
    for axis_at, blocks in cuts:
        steps = jnp.exp(jax.random.uniform(jax.random.fold_in(own, axis_at), (blocks,), jnp.float32, smallest / len(cuts), top_value / len(cuts)))
        factor_of = factor_of * jnp.repeat(steps, shape[axis_at] // blocks).reshape([-1 if axis == axis_at else 1 for axis in range(len(shape))])
    return factor_of


def length_profile(number_of, total, reach, slope):
    portions = [(1 << 20) // math.isqrt(rank ** slope) + 1 for rank in range(2, number_of + 1)]
    spare, given = total - reach - (number_of - 1), [1] * (number_of - 1)
    while spare > 0:
        movable = [i for i in range(number_of - 1) if given[i] < reach]
        mass, budget = sum([portions[i] for i in movable]), spare
        for i in movable:
            addition = min(reach - given[i], max(1, budget * portions[i] // mass), spare)
            given[i] = given[i] + addition
            spare = spare - addition
    return np.array([reach] + given)


def ragged(stream_key, number_of, total, reach, skew):
    if number_of == 2:
        one = jax.random.randint(stream_key, (), max(1, total - reach), min(reach, total - 1) + 1)
        return jnp.stack([one, total - one])
    lengths = jnp.asarray(length_profile(number_of, total, reach, skew), jnp.int32)
    pairs = (number_of - 1) // 2
    giver, taker = lengths[1:1 + 2 * pairs:2], lengths[2:2 + 2 * pairs:2]
    margin = jnp.minimum(giver - 1, reach - taker)
    moved = jax.random.randint(jax.random.fold_in(stream_key, 1), (pairs,), 0, 1 << 20) % (margin + 1)
    lengths = lengths.at[1:1 + 2 * pairs:2].set(giver - moved).at[2:2 + 2 * pairs:2].set(taker + moved)
    return lengths[jax.random.permutation(jax.random.fold_in(stream_key, 2), number_of)]


def scatter_about(rng, dims, deviation, limit, shards=(), kind=jnp.bfloat16):
    drawn = deviation * jax.random.normal(rng, dims, jnp.float32)
    if shards:
        drawn = drawn * steps_of(rng, dims, shards, -0.22, 0.18)
    return jnp.clip(drawn, -limit, limit).astype(kind)


def setup_inputs(seed: int = 0) -> dict:
    seeds = jax.random.split(jax.random.key(seed), 12)
    return {
        "source_tokens": scatter_about(seeds[0], (REPLICAS * 2 * M * TOK, MODEL_WIDTH), 1.0, 6.0, ((0, 64),)),
        "send_counts": draw_send_counts(jax.random.fold_in(seeds[11], 71), 0),
        "doc_segments": jax.vmap(lambda own: jnp.searchsorted(jnp.cumsum(ragged(own, TOK // 4, TOK, TOK // 2, 2)), jnp.arange(TOK), side="right"))(jax.random.split(seeds[2], (REPLICAS * M))).reshape((REPLICAS * M, TOK)).astype(jnp.int32),
        "out_cotangent": scatter_about(seeds[3], (REPLICAS * M * TOK, MODEL_WIDTH), ((64 * M * TOK * REPLICAS) ** -0.5), 0.01953125, ((0, 64),)),
        "norm_gain": jnp.clip(1.0 + 0.15 * jax.random.normal(seeds[4], (SECTION_COUNT, MODEL_WIDTH), jnp.float32), 0.25, 1.75),
        "query_weight": scatter_about(seeds[5], (SECTION_COUNT, MODEL_WIDTH, QUERY_HEADS * HEAD_SIZE), MODEL_WIDTH ** -0.5, 0.125, ((0, 8), (1, 64))),
        "frozen_key_matrix": scatter_about(seeds[6], (SECTION_COUNT, MODEL_WIDTH, KEY_VALUE_HEADS * HEAD_SIZE), MODEL_WIDTH ** -0.5, 0.125, ((0, 8), (1, 64))),
        "frozen_value_matrix": scatter_about(seeds[7], (SECTION_COUNT, MODEL_WIDTH, KEY_VALUE_HEADS * HEAD_SIZE), MODEL_WIDTH ** -0.5, 0.125, ((0, 8), (1, 64))),
        "out_weight": scatter_about(seeds[8], (SECTION_COUNT, QUERY_HEADS * HEAD_SIZE, MODEL_WIDTH), (QUERY_HEADS * HEAD_SIZE) ** -0.5, 0.1875, ((0, 8), (1, 64))),
        "adapter_down": scatter_about(seeds[9], (SECTION_COUNT, 2, MODEL_WIDTH, ADAPTER_RANK), MODEL_WIDTH ** -0.5, 0.125, ((0, 8),)),
        "adapter_up_maps": scatter_about(seeds[10], (SECTION_COUNT, ADAPTER_RANK, QUERY_HEADS * HEAD_SIZE + KEY_VALUE_HEADS * HEAD_SIZE), (ADAPTER_RANK * 64) ** -0.5, 0.1875, ((0, 8),)),
    }


ROPE_BASE = 500000.0
ADAPTER_SCALE = 2.0
NORM_EPS = 1e-05

def widen_heads(tensor):
    return lax.optimization_barrier(tensor).astype(jnp.float32)

def doc_layout(seg_row, valid_row):
    token_row_count = seg_row.shape[0]
    places = jnp.arange(token_row_count, dtype=jnp.int32)
    same_doc = seg_row[:, None] == seg_row[None, :]
    before = places[None, :] < places[:, None]
    position = lax.optimization_barrier(jnp.sum(jnp.where(same_doc & before, 1.0, 0.0).astype(jnp.float32), axis=1))
    causal = places[None, :] <= places[:, None]
    paired = same_doc & valid_row[:, None] & valid_row[None, :]
    allowed = causal & (paired | (places[None, :] == places[:, None]))
    frequency = ROPE_BASE ** (-2.0 * jnp.arange(HEAD_SIZE // 2, dtype=jnp.float32) / HEAD_SIZE)
    angles = position[:, None] * frequency[None, :]
    return (jnp.cos(angles)[:, None, :], jnp.sin(angles)[:, None, :], allowed)

def normalize(hidden, gain_row):
    energy = lax.optimization_barrier(jnp.mean(hidden * hidden, axis=-1, keepdims=True))
    return (hidden * lax.rsqrt(energy + NORM_EPS) * gain_row).astype(jnp.bfloat16)

def rotary_apply(tensor, cosine_table, sine_table):
    middle = tensor.shape[-1] // 2
    leading = tensor[..., :middle]
    trailing = tensor[..., middle:]
    return jnp.concatenate([leading * cosine_table - trailing * sine_table, trailing * cosine_table + leading * sine_table], axis=-1)

def project(normed_hidden, adapter, frozen, cosine_table, sine_table):
    w_query, key_projection_weight, w_value = frozen
    down_pair, up_pair = adapter
    split_at = QUERY_HEADS * HEAD_SIZE
    token_row_count = normed_hidden.shape[0]
    low_query = jnp.dot(normed_hidden, down_pair[0], preferred_element_type=jnp.float32).astype(jnp.bfloat16)
    low_value = jnp.dot(normed_hidden, down_pair[1], preferred_element_type=jnp.float32).astype(jnp.bfloat16)
    query_rows = jnp.dot(normed_hidden, w_query, preferred_element_type=jnp.float32) + ADAPTER_SCALE * jnp.dot(low_query, up_pair[:, :split_at], preferred_element_type=jnp.float32)
    query_rows = rotary_apply(query_rows.reshape(token_row_count, QUERY_HEADS, HEAD_SIZE), cosine_table, sine_table).astype(jnp.bfloat16)
    key_head_rows = rotary_apply(jnp.dot(normed_hidden, key_projection_weight, preferred_element_type=jnp.float32).reshape(token_row_count, KEY_VALUE_HEADS, HEAD_SIZE), cosine_table, sine_table).astype(jnp.bfloat16)
    value_head_rows = jnp.dot(normed_hidden, w_value, preferred_element_type=jnp.float32) + ADAPTER_SCALE * jnp.dot(low_value, up_pair[:, split_at:], preferred_element_type=jnp.float32)
    value_head_rows = value_head_rows.astype(jnp.bfloat16).reshape(token_row_count, KEY_VALUE_HEADS, HEAD_SIZE)
    return (query_rows, key_head_rows, value_head_rows)

def attend(query_rows, key_head_rows, value_head_rows, allowed):
    token_row_count = query_rows.shape[0]
    grouped_queries = widen_heads(query_rows).reshape(token_row_count, KEY_VALUE_HEADS, QUERY_HEADS // KEY_VALUE_HEADS, HEAD_SIZE)
    scores = jnp.einsum('qhgd,khd->hgqk', grouped_queries, widen_heads(key_head_rows)) * HEAD_SIZE ** (-0.5)
    weights = jnp.where(allowed[None, None], jnp.exp(scores), 0.0)
    shares = (weights / lax.optimization_barrier(jnp.sum(weights, axis=-1, keepdims=True))).astype(jnp.bfloat16)
    blended = jnp.einsum('hgqk,khd->qhgd', widen_heads(shares), widen_heads(value_head_rows))
    return blended.reshape(token_row_count, QUERY_HEADS * HEAD_SIZE).astype(jnp.bfloat16)

def finish(hidden, blended, w_out):
    return (hidden + jnp.dot(blended, w_out, preferred_element_type=jnp.float32)).astype(jnp.bfloat16)

def section_apply(tokens, adapter, frozen, gain_row, cosine_table, sine_table, allowed):
    hidden = tokens.astype(jnp.float32)
    normed_hidden = normalize(hidden, gain_row)
    query_rows, key_head_rows, value_head_rows = project(normed_hidden, adapter, frozen[:3], cosine_table, sine_table)
    return finish(hidden, attend(query_rows, key_head_rows, value_head_rows, allowed), frozen[3])

def reference(source_tokens, send_counts, doc_segments, out_cotangent, norm_gain, query_weight, frozen_key_matrix, frozen_value_matrix, out_weight, adapter_down, adapter_up_maps):
    per_source = source_tokens.shape[0] // REPLICAS
    anchor = source_tokens.reshape(REPLICAS, per_source, MODEL_WIDTH)
    send_start = (jnp.cumsum(send_counts, axis=1) - send_counts).astype(jnp.int32)
    recv_end = jnp.cumsum(send_counts, axis=0).astype(jnp.int32)
    recv_start = (recv_end - send_counts).astype(jnp.int32)
    places = jnp.arange(M * TOK, dtype=jnp.int32)

    def arrange(target):
        end_rows = recv_end[:, target]
        starts = recv_start[:, target]
        source_of = jnp.minimum(lax.optimization_barrier(jnp.sum((end_rows[None, :] <= places[:, None]).astype(jnp.int32), axis=1)), REPLICAS - 1).astype(jnp.int32)
        offset = (places - starts[source_of]).astype(jnp.int32)
        filled = places < end_rows[REPLICAS - 1]
        row_of = jnp.where(filled, send_start[source_of, target] + offset, 0).astype(jnp.int32)
        picked = anchor[source_of, row_of]
        return (jnp.where(filled[:, None], picked, jnp.zeros_like(picked)), filled)
    streams, filled = lax.map(arrange, jnp.arange(REPLICAS, dtype=jnp.int32))
    tokens = streams.reshape(REPLICAS * M, TOK, MODEL_WIDTH)
    cosine_table, sine_table, allowed = jax.vmap(doc_layout)(doc_segments, filled.reshape(REPLICAS * M, TOK))
    section_inputs = []
    for section_index in range(SECTION_COUNT):
        section_inputs.append(tokens)
        adapter = (adapter_down[section_index], adapter_up_maps[section_index])
        frozen = (query_weight[section_index], frozen_key_matrix[section_index], frozen_value_matrix[section_index], out_weight[section_index])
        tokens = jax.vmap(section_apply, in_axes=(0, None, None, None, 0, 0, 0))(tokens, adapter, frozen, norm_gain[section_index], cosine_table, sine_table, allowed)
    cotangent = out_cotangent.reshape(REPLICAS * M, TOK, MODEL_WIDTH)
    down_list = []
    up_list = []
    for section_index in range(SECTION_COUNT - 1, -1, -1):
        adapter = (adapter_down[section_index], adapter_up_maps[section_index])
        frozen = (query_weight[section_index], frozen_key_matrix[section_index], frozen_value_matrix[section_index], out_weight[section_index])
        gain_row = norm_gain[section_index]

        def pullback(inputs, upstream, cos_one, sin_one, allow_one):

            def apply_section(inside, params):
                return section_apply(inside, params, frozen, gain_row, cos_one, sin_one, allow_one)
            unused, puller = jax.vjp(apply_section, inputs, adapter)
            return puller(upstream)
        cotangent, adapter_grad = jax.vmap(pullback)(section_inputs[section_index], cotangent, cosine_table, sine_table, allowed)
        down_list.append(lax.optimization_barrier(jnp.sum(adapter_grad[0].astype(jnp.float32), axis=0)))
        up_list.append(lax.optimization_barrier(jnp.sum(adapter_grad[1].astype(jnp.float32), axis=0)))
    return (jnp.stack(down_list[::-1]), jnp.stack(up_list[::-1]))
```

```python
import functools

import jax
import jax.numpy as jnp
from jax import lax
from jax.experimental import pallas as pl
from jax.experimental.pallas import tpu as pltpu
from jax.sharding import PartitionSpec as P

QUERY_HEADS = 16
KEY_VALUE_HEADS = 4
GROUP = QUERY_HEADS // KEY_VALUE_HEADS
HEAD_SIZE = 64
QUERY_WIDTH = QUERY_HEADS * HEAD_SIZE
KEY_WIDTH = KEY_VALUE_HEADS * HEAD_SIZE
RANK = 16
LANES = 128

ROPE_BASE = 500000.0
ADAPTER_SCALE = 2.0
NORM_EPS = 1e-05
SCORE_SCALE = HEAD_SIZE ** (-0.5)

X_CHIPS = 4

F32 = jnp.float32
BF16 = jnp.bfloat16
VMEM_LIMIT = 40 * 1024 * 1024


def dot(a, b):
    return jnp.dot(a, b, preferred_element_type=F32)


def dot_nt(a, b):
    return lax.dot_general(a, b, (((1,), (1,)), ((), ())), preferred_element_type=F32)


def dot_tn(a, b):
    return lax.dot_general(a, b, (((0,), (0,)), ((), ())), preferred_element_type=F32)


def lanes_of(rows, width):
    return lax.broadcasted_iota(jnp.int32, (rows, width), 1)


def rope(t, cosine, signed_sine):
    rows, width = t.shape
    copies = width // LANES
    wide_cos = jnp.concatenate([cosine] * copies, axis=1)
    wide_sin = jnp.concatenate([signed_sine] * copies, axis=1)
    half = HEAD_SIZE // 2
    leading = (lanes_of(rows, width) % HEAD_SIZE) < half
    partner = jnp.where(leading, pltpu.roll(t, width - half, 1), pltpu.roll(t, half, 1))
    return t * wide_cos + partner * wide_sin


def expand(turned, head):
    rows, width = turned[0].shape
    block = lanes_of(rows, width) // HEAD_SIZE
    zero = jnp.zeros((), turned[0].dtype)
    parts = [
        jnp.where(block == g, turned[(g - head) % KEY_VALUE_HEADS], zero) for g in range(GROUP)
    ]
    return jnp.concatenate(parts, axis=0)


def turns_of(t):
    width = t.shape[1]
    wide = t.astype(F32)
    return [t] + [
        pltpu.roll(wide, j * HEAD_SIZE, 1).astype(t.dtype) for j in range(1, KEY_VALUE_HEADS)
    ]


def fold(products):
    rows = products[0].shape[0] // GROUP
    width = products[0].shape[1]
    block = lanes_of(rows, width) // HEAD_SIZE
    total = None
    for h, product in enumerate(products):
        diagonal = None
        for g in range(GROUP):
            part = jnp.where(block == g, product[g * rows : (g + 1) * rows], 0.0)
            diagonal = part if diagonal is None else diagonal + part
        pair = diagonal + pltpu.roll(diagonal, HEAD_SIZE, 1)
        whole = pair + pltpu.roll(pair, 2 * HEAD_SIZE, 1)
        kept = jnp.where(block == h, whole, 0.0)
        total = kept if total is None else total + kept
    return total


def forward_kernel(
    x_ref, gain_ref, wqkv_ref, wout_ref, down_ref, upq_ref, upv_ref, cos_ref, sin_ref, mask_ref,
    y_ref, q_ref, k_ref, v_ref, p_ref, low_ref, n_ref,
):
    hidden = x_ref[...].astype(F32)
    energy = jnp.mean(hidden * hidden, axis=-1, keepdims=True)
    n = (hidden * lax.rsqrt(energy + NORM_EPS) * gain_ref[...]).astype(BF16)
    n_ref[...] = n
    cosine, sine = cos_ref[...], sin_ref[...]
    low = dot(n, down_ref[...]).astype(BF16)
    low_ref[...] = low
    k = rope(dot(n, wqkv_ref[:, QUERY_WIDTH : QUERY_WIDTH + KEY_WIDTH]), cosine, sine).astype(BF16)
    k_ref[...] = k
    v = dot(n, wqkv_ref[:, QUERY_WIDTH + KEY_WIDTH :]) + ADAPTER_SCALE * dot(low, upv_ref[...])
    v = v.astype(BF16)
    v_ref[...] = v
    k_turns, v_turns = turns_of(k), turns_of(v)
    allowed = mask_ref[...] > 0.0
    tokens = hidden.shape[0]
    width = GROUP * HEAD_SIZE
    blended = []
    for h in range(KEY_VALUE_HEADS):
        at = slice(h * width, (h + 1) * width)
        q = dot(n, wqkv_ref[:, at]) + ADAPTER_SCALE * dot(low, upq_ref[:, at])
        q = rope(q, cosine, sine).astype(BF16)
        q_ref[:, at] = q
        scores = dot_nt(q, expand(k_turns, h)) * SCORE_SCALE
        shares = []
        for g in range(GROUP):
            weights = jnp.where(allowed, jnp.exp(scores[:, g * tokens : (g + 1) * tokens]), 0.0)
            shares.append((weights / jnp.sum(weights, axis=-1, keepdims=True)).astype(BF16))
        shares = jnp.concatenate(shares, axis=1)
        p_ref[:, h * GROUP * tokens : (h + 1) * GROUP * tokens] = shares
        blended.append(dot(shares, expand(v_turns, h)).astype(BF16))
    blended = jnp.concatenate(blended, axis=1)
    y_ref[...] = (hidden + dot(blended, wout_ref[...])).astype(BF16)


def backward_kernel(
    c_ref, x_ref, gain_ref, wqkv_ref, wout_ref, down_ref, upq_ref, upv_ref, cos_ref, sin_ref,
    q_ref, k_ref, v_ref, p_ref,
    out_ref, dq_ref, dv_ref, dlow_ref,
):
    c = c_ref[...]
    tokens = c.shape[0]
    width = GROUP * HEAD_SIZE
    cosine, sine = cos_ref[...], sin_ref[...]
    k_turns, v_turns = turns_of(k_ref[...]), turns_of(v_ref[...])
    dn = None
    dlow = None
    dk_products, dv_products = [], []
    for h in range(KEY_VALUE_HEADS):
        at = slice(h * width, (h + 1) * width)
        dblended = dot_nt(c, wout_ref[at, :]).astype(BF16)
        shares = p_ref[:, h * GROUP * tokens : (h + 1) * GROUP * tokens]
        dshares = dot_nt(dblended, expand(v_turns, h))
        dscores = []
        for g in range(GROUP):
            span = slice(g * tokens, (g + 1) * tokens)
            p = shares[:, span].astype(F32)
            dp = dshares[:, span]
            pdp = p * dp
            dscores.append(
                ((pdp - p * jnp.sum(pdp, axis=-1, keepdims=True)) * SCORE_SCALE).astype(BF16)
            )
        dscores = jnp.concatenate(dscores, axis=1)
        dq = dot(dscores, expand(k_turns, h))
        dq = rope(dq, cosine, -sine).astype(BF16)
        dq_ref[:, at] = dq
        part = dot_nt(dq, upq_ref[:, at])
        dlow = part if dlow is None else dlow + part
        part = dot_nt(dq, wqkv_ref[:, at])
        dn = part if dn is None else dn + part
        dv_products.append(dot_tn(shares, dblended))
        dk_products.append(dot_tn(dscores, q_ref[:, at]))
    dk = rope(fold(dk_products), cosine, -sine).astype(BF16)
    dv = fold(dv_products).astype(BF16)
    dv_ref[...] = dv
    dlow = (ADAPTER_SCALE * (dlow + dot_nt(dv, upv_ref[...]))).astype(BF16)
    dlow_ref[...] = dlow
    dn = dn + dot_nt(dk, wqkv_ref[:, QUERY_WIDTH : QUERY_WIDTH + KEY_WIDTH])
    dn = dn + dot_nt(dv, wqkv_ref[:, QUERY_WIDTH + KEY_WIDTH :])
    dn = dn + dot_nt(dlow, down_ref[...])
    hidden = x_ref[...].astype(F32)
    energy = jnp.mean(hidden * hidden, axis=-1, keepdims=True)
    scale = lax.rsqrt(energy + NORM_EPS)
    dy = dn * gain_ref[...]
    along = jnp.mean(hidden * dy, axis=-1, keepdims=True)
    dh = scale * dy - hidden * (scale * scale * scale * along)
    out_ref[...] = (c.astype(F32) + dh).astype(BF16)


def grads_kernel(n_ref, low_ref, dq_ref, dv_ref, dlow_ref, g_ref):
    g_ref[...] = jnp.zeros_like(g_ref)
    g_ref[0 : 2 * RANK, :] = dot_tn(dlow_ref[...], n_ref[...])[: 2 * RANK]
    low = low_ref[...]
    up_q = ADAPTER_SCALE * dot_tn(low, dq_ref[...])
    up_v = ADAPTER_SCALE * dot_tn(low, dv_ref[...])
    g_ref[2 * RANK : 3 * RANK, 0:QUERY_WIDTH] = up_q[:RANK]
    g_ref[2 * RANK : 3 * RANK, QUERY_WIDTH : QUERY_WIDTH + KEY_WIDTH] = up_v[RANK : 2 * RANK]


def call(kernel, outs, *args):
    return pl.pallas_call(
        kernel,
        out_shape=[jax.ShapeDtypeStruct(shape, dtype) for shape, dtype in outs],
        in_specs=[pl.BlockSpec(memory_space=pltpu.VMEM)] * len(args),
        out_specs=[pl.BlockSpec(memory_space=pltpu.VMEM)] * len(outs),
        compiler_params=pltpu.CompilerParams(vmem_limit_bytes=VMEM_LIMIT),
    )(*args)


def z_route(replicas, distance):
    return [(i, (i + distance * X_CHIPS) % replicas) for i in range(replicas)]


def x_route(replicas, distance):
    return [
        (i, i // X_CHIPS * X_CHIPS + (i % X_CHIPS + distance) % X_CHIPS) for i in range(replicas)
    ]


def ring(piece, route, count, place, put, split):
    put(place, None, piece)
    ahead = behind = piece
    for step in range(1, count // 2):
        ahead = lax.ppermute(ahead, "dp", route(1))
        behind = lax.ppermute(behind, "dp", route(-1))
        put((place - step) % count, None, ahead)
        put((place + step) % count, None, behind)
    step = count // 2
    ahead = lax.ppermute(split(ahead)[0], "dp", route(1))
    behind = lax.ppermute(split(behind)[1], "dp", route(-1))
    put((place - step) % count, 0, ahead)
    put((place + step) % count, 1, behind)


def gather_weights(shard, replica, replicas):
    rows, columns = shard.shape
    z_count = replicas // X_CHIPS
    z, x = replica // X_CHIPS, replica % X_CHIPS
    line = [jnp.zeros((X_CHIPS, rows, columns), shard.dtype)]

    def put_line(at, part, data):
        start = rows // 2 if part == 1 else 0
        line[0] = lax.dynamic_update_slice(line[0], data[None], (at, start, 0))

    ring(
        shard,
        functools.partial(x_route, replicas),
        X_CHIPS,
        x,
        put_line,
        lambda t: (t[: rows // 2], t[rows // 2 :]),
    )
    qkv_width = QUERY_WIDTH + 2 * KEY_WIDTH
    half = rows // 2
    qkv = [jnp.zeros((z_count, X_CHIPS, rows, qkv_width), shard.dtype)]
    out = [jnp.zeros((z_count, X_CHIPS, half, 2 * QUERY_WIDTH), shard.dtype)]

    def put_plane(at, part, data):
        start = X_CHIPS // 2 if part == 1 else 0
        qkv[0] = lax.dynamic_update_slice(qkv[0], data[None, :, :, :qkv_width], (at, start, 0, 0))
        left = data[None, :, :half, qkv_width:]
        right = data[None, :, half:, qkv_width:]
        out[0] = lax.dynamic_update_slice(
            out[0], jnp.concatenate([left, right], axis=-1), (at, start, 0, 0)
        )

    ring(
        line[0],
        functools.partial(z_route, replicas),
        z_count,
        z,
        put_plane,
        lambda t: (t[: X_CHIPS // 2], t[X_CHIPS // 2 :]),
    )
    return (
        qkv[0].reshape(replicas * rows, qkv_width),
        out[0].reshape(replicas * half, 2 * QUERY_WIDTH),
    )


def sum_over_replicas(grads, replica, replicas):
    rows, columns = grads.shape
    z_count = replicas // X_CHIPS
    x = replica % X_CHIPS
    part_width = columns // X_CHIPS
    parts = grads.reshape(rows, X_CHIPS, part_width).transpose(1, 0, 2)
    sent = parts.astype(BF16)
    total = lax.dynamic_index_in_dim(parts, x, 0, keepdims=False)
    for distance in range(1, X_CHIPS):
        piece = lax.dynamic_index_in_dim(sent, (x + distance) % X_CHIPS, 0, keepdims=False)
        total = total + lax.ppermute(piece, "dp", x_route(replicas, distance)).astype(F32)
    low_count = 4
    sent = total.astype(BF16)
    for distance in range(1, low_count):
        route = []
        for i in range(replicas):
            zi, xi = i // X_CHIPS, i % X_CHIPS
            to = zi // low_count * low_count + (zi % low_count + distance) % low_count
            route.append((i, to * X_CHIPS + xi))
        total = total + lax.ppermute(sent, "dp", route).astype(F32)
    sent = total.astype(BF16)
    for distance in range(1, z_count // low_count):
        route = z_route(replicas, distance * low_count)
        total = total + lax.ppermute(sent, "dp", route).astype(F32)
    sent = total.astype(BF16)
    whole = jnp.zeros((X_CHIPS, rows, part_width), F32)
    whole = lax.dynamic_update_slice(whole, total[None], (x, 0, 0))
    for distance in range(1, X_CHIPS):
        piece = lax.ppermute(sent, "dp", x_route(replicas, distance)).astype(F32)
        whole = lax.dynamic_update_slice(whole, piece[None], ((x - distance) % X_CHIPS, 0, 0))
    return whole.transpose(1, 0, 2).reshape(rows, columns)


def exchange_tokens(source_tokens, send_counts, replica, replicas, stream_count):
    slot_count = source_tokens.shape[0] // replicas
    features = source_tokens.shape[1]
    sent_counts = lax.dynamic_index_in_dim(send_counts, replica, 0, keepdims=False)
    send_start = jnp.cumsum(sent_counts) - sent_counts
    slot_ids = jnp.arange(slot_count, dtype=jnp.int32)
    occupied = slot_ids[None, :] < sent_counts[:, None]
    pick_rows = jnp.where(occupied, send_start[:, None] + slot_ids[None, :], -1).reshape(-1)
    own_rows = jnp.arange(source_tokens.shape[0], dtype=jnp.int32)
    choose = (pick_rows[:, None] == own_rows[None, :]).astype(BF16)
    packed = dot(choose, source_tokens).astype(BF16).reshape(replicas, slot_count, features)
    arrived = lax.all_to_all(packed, "dp", split_axis=0, concat_axis=0, tiled=True)
    incoming = lax.dynamic_index_in_dim(send_counts, replica, 1, keepdims=False)
    end_rows = jnp.cumsum(incoming)
    starts = end_rows - incoming
    places = jnp.arange(stream_count, dtype=jnp.int32)
    slot_place = starts[:, None] + slot_ids[None, :]
    slot_place = jnp.where(slot_ids[None, :] < incoming[:, None], slot_place, -1).reshape(-1)
    choose = (places[:, None] == slot_place[None, :]).astype(BF16)
    stream = dot(choose, arrived.reshape(replicas * slot_count, features)).astype(BF16)
    return stream, places < end_rows[replicas - 1]


def layout(segments, filled):
    micro_count, token_count = segments.shape
    tokens = micro_count * token_count
    segment = segments.reshape(tokens)
    places = jnp.arange(tokens, dtype=jnp.int32)
    sequence = places // token_count
    same = (segment[:, None] == segment[None, :]) & (sequence[:, None] == sequence[None, :])
    before = places[None, :] < places[:, None]
    position = jnp.sum(jnp.where(same & before, 1.0, 0.0).astype(F32), axis=1)
    alone = places[None, :] == places[:, None]
    allowed = (before & same & filled[:, None] & filled[None, :]) | alone
    half = HEAD_SIZE // 2
    frequency = ROPE_BASE ** (-2.0 * jnp.arange(half, dtype=F32) / HEAD_SIZE)
    angles = position[:, None] * frequency[None, :]
    cosine, sine = jnp.cos(angles), jnp.sin(angles)
    heads = LANES // HEAD_SIZE
    return (
        jnp.concatenate([cosine, cosine] * heads, axis=1),
        jnp.concatenate([-sine, sine] * heads, axis=1),
        allowed.astype(F32),
    )


def local(
    source_tokens,
    send_counts,
    doc_segments,
    out_cotangent,
    norm_gain,
    query_weight,
    frozen_key_matrix,
    frozen_value_matrix,
    out_weight,
    adapter_down,
    adapter_up_maps,
):
    replicas = lax.axis_size("dp")
    sections = lax.axis_size("section")
    replica = lax.axis_index("dp")
    section = lax.axis_index("section")
    features = source_tokens.shape[1]
    tokens = doc_segments.shape[0] * doc_segments.shape[1]

    half = out_weight.shape[2] // 2
    out_rows = jnp.concatenate([out_weight[0, :, :half], out_weight[0, :, half:]], axis=0)
    shard = jnp.concatenate(
        [query_weight[0], frozen_key_matrix[0], frozen_value_matrix[0], out_rows], axis=1
    )
    stream, filled = exchange_tokens(source_tokens, send_counts, replica, replicas, tokens)
    cosine, sine, allowed = layout(doc_segments, filled)
    wqkv, wout = gather_weights(shard, replica, replicas)
    gain = norm_gain[0].reshape(1, features)
    spare = LANES - 2 * RANK
    down = jnp.concatenate(
        [adapter_down[0, 0], adapter_down[0, 1], jnp.zeros((features, spare), BF16)], axis=1
    )
    up = adapter_up_maps[0]
    up_q = jnp.concatenate([up[:, :QUERY_WIDTH], jnp.zeros((LANES - RANK, QUERY_WIDTH), BF16)])
    up_v = jnp.concatenate(
        [
            jnp.zeros((RANK, KEY_WIDTH), BF16),
            up[:, QUERY_WIDTH:],
            jnp.zeros((spare, KEY_WIDTH), BF16),
        ]
    )

    saved_shapes = [
        ((tokens, QUERY_WIDTH), BF16),
        ((tokens, KEY_WIDTH), BF16),
        ((tokens, KEY_WIDTH), BF16),
        ((tokens, QUERY_HEADS * tokens), BF16),
        ((tokens, LANES), BF16),
        ((tokens, features), BF16),
    ]
    x = stream
    saved = tuple(jnp.zeros(shape, dtype) for shape, dtype in saved_shapes)
    for turn in range(sections):

        def run(x, saved):
            made = call(
                forward_kernel,
                [((tokens, features), BF16)] + saved_shapes,
                x, gain, wqkv, wout, down, up_q, up_v, cosine, sine, allowed,
            )
            return made[0], tuple(made[1:])

        y, saved = lax.cond(section == turn, run, lambda x, saved: (x, saved), x, saved)
        if turn + 1 < sections:
            came = lax.ppermute(y, "section", [(turn, turn + 1)])
            x = jnp.where(section == turn + 1, came, x)

    q, k, v, shares, low, normed = saved
    c = out_cotangent
    kept = (
        jnp.zeros((tokens, QUERY_WIDTH), BF16),
        jnp.zeros((tokens, KEY_WIDTH), BF16),
        jnp.zeros((tokens, LANES), BF16),
    )
    for turn in range(sections - 1, -1, -1):

        def run_back(c, kept):
            made = call(
                backward_kernel,
                [((tokens, features), BF16)] + [(t.shape, t.dtype) for t in kept],
                c, x, gain, wqkv, wout, down, up_q, up_v, cosine, sine, q, k, v, shares,
            )
            return made[0], tuple(made[1:])

        back, kept = lax.cond(section == turn, run_back, lambda c, kept: (c, kept), c, kept)
        if turn > 0:
            came = lax.ppermute(back, "section", [(turn, turn - 1)])
            c = jnp.where(section == turn - 1, came, c)

    (grads,) = call(
        grads_kernel, [((3 * RANK, features), F32)], normed, low, kept[0], kept[1], kept[2]
    )
    grads = sum_over_replicas(grads, replica, replicas)
    down_grads = grads[: 2 * RANK].reshape(2, RANK, features).transpose(0, 2, 1)
    up_grads = grads[2 * RANK :, : QUERY_WIDTH + KEY_WIDTH]
    return (down_grads[None], up_grads[None])


def solution(mesh):
    placed = (
        P("dp", None),
        P(),
        P("dp", None),
        P("dp", None),
        P("section", None),
        P("section", "dp", None),
        P("section", "dp", None),
        P("section", "dp", None),
        P("section", "dp", None),
        P("section", None, None, None),
        P("section", None, None),
    )
    return jax.shard_map(
        local,
        mesh=mesh,
        in_specs=placed,
        out_specs=(P("section", None, None, None), P("section", None, None)),
        check_vma=False,
    )
```

```python
import functools

import jax
import jax.numpy as jnp
from jax import lax
from jax.experimental import pallas as pl
from jax.experimental.pallas import tpu as pltpu
from jax.sharding import PartitionSpec as P

QUERY_HEADS = 16
KEY_VALUE_HEADS = 4
GROUP = QUERY_HEADS // KEY_VALUE_HEADS
HEAD_SIZE = 64
QUERY_WIDTH = QUERY_HEADS * HEAD_SIZE
KEY_WIDTH = KEY_VALUE_HEADS * HEAD_SIZE
RANK = 16
LANES = 128

ROPE_BASE = 500000.0
ADAPTER_SCALE = 2.0
NORM_EPS = 1e-05
SCORE_SCALE = HEAD_SIZE ** (-0.5)

X_CHIPS = 4

F32 = jnp.float32
BF16 = jnp.bfloat16
VMEM_LIMIT = 20 * 1024 * 1024
CUTS = (2, 5, 8)


def dot(a, b):
    return jnp.dot(a, b, preferred_element_type=F32)


def dot_nt(a, b):
    return lax.dot_general(a, b, (((1,), (1,)), ((), ())), preferred_element_type=F32)


def dot_tn(a, b):
    return lax.dot_general(a, b, (((0,), (0,)), ((), ())), preferred_element_type=F32)


def lanes_of(rows, width):
    return lax.broadcasted_iota(jnp.int32, (rows, width), 1)


def rope(t, cosine, signed_sine):
    rows, width = t.shape
    copies = width // LANES
    wide_cos = jnp.concatenate([cosine] * copies, axis=1)
    wide_sin = jnp.concatenate([signed_sine] * copies, axis=1)
    half = HEAD_SIZE // 2
    leading = (lanes_of(rows, width) % HEAD_SIZE) < half
    partner = jnp.where(leading, pltpu.roll(t, width - half, 1), pltpu.roll(t, half, 1))
    return t * wide_cos + partner * wide_sin


def expand(turned, head):
    rows, width = turned[0].shape
    block = lanes_of(rows, width) // HEAD_SIZE
    zero = jnp.zeros((), turned[0].dtype)
    parts = [
        jnp.where(block == g, turned[(g - head) % KEY_VALUE_HEADS], zero) for g in range(GROUP)
    ]
    return jnp.concatenate(parts, axis=0)


def turns_of(t):
    width = t.shape[1]
    wide = t.astype(F32)
    return [t] + [
        pltpu.roll(wide, j * HEAD_SIZE, 1).astype(t.dtype) for j in range(1, KEY_VALUE_HEADS)
    ]


def fold(products):
    rows = products[0].shape[0] // GROUP
    width = products[0].shape[1]
    block = lanes_of(rows, width) // HEAD_SIZE
    total = None
    for h, product in enumerate(products):
        diagonal = None
        for g in range(GROUP):
            part = jnp.where(block == g, product[g * rows : (g + 1) * rows], 0.0)
            diagonal = part if diagonal is None else diagonal + part
        pair = diagonal + pltpu.roll(diagonal, HEAD_SIZE, 1)
        whole = pair + pltpu.roll(pair, 2 * HEAD_SIZE, 1)
        kept = jnp.where(block == h, whole, 0.0)
        total = kept if total is None else total + kept
    return total


def forward_kernel(
    x_ref, gain_ref, wqkv_ref, wout_ref, down_ref, upq_ref, upv_ref, cos_ref, sin_ref, mask_ref,
    y_ref, kept_x_ref, q_ref, k_ref, v_ref, p_ref, low_ref, n_ref,
):
    kept_x_ref[...] = x_ref[...]
    hidden = x_ref[...].astype(F32)
    energy = jnp.mean(hidden * hidden, axis=-1, keepdims=True)
    n = (hidden * lax.rsqrt(energy + NORM_EPS) * gain_ref[...]).astype(BF16)
    n_ref[...] = n
    cosine, sine = cos_ref[...], sin_ref[...]
    low = dot(n, down_ref[...]).astype(BF16)
    low_ref[...] = low
    k = rope(dot(n, wqkv_ref[:, QUERY_WIDTH : QUERY_WIDTH + KEY_WIDTH]), cosine, sine).astype(BF16)
    k_ref[...] = k
    v = dot(n, wqkv_ref[:, QUERY_WIDTH + KEY_WIDTH :]) + ADAPTER_SCALE * dot(low, upv_ref[...])
    v = v.astype(BF16)
    v_ref[...] = v
    k_turns, v_turns = turns_of(k), turns_of(v)
    allowed = mask_ref[...] > 0.0
    tokens = hidden.shape[0]
    width = GROUP * HEAD_SIZE
    blended = []
    for h in range(KEY_VALUE_HEADS):
        at = slice(h * width, (h + 1) * width)
        q = dot(n, wqkv_ref[:, at]) + ADAPTER_SCALE * dot(low, upq_ref[:, at])
        q = rope(q, cosine, sine).astype(BF16)
        q_ref[:, at] = q
        scores = dot_nt(q, expand(k_turns, h)) * SCORE_SCALE
        shares = []
        for g in range(GROUP):
            weights = jnp.where(allowed, jnp.exp(scores[:, g * tokens : (g + 1) * tokens]), 0.0)
            shares.append((weights / jnp.sum(weights, axis=-1, keepdims=True)).astype(BF16))
        shares = jnp.concatenate(shares, axis=1)
        p_ref[:, h * GROUP * tokens : (h + 1) * GROUP * tokens] = shares
        blended.append(dot(shares, expand(v_turns, h)).astype(BF16))
    blended = jnp.concatenate(blended, axis=1)
    y_ref[...] = (hidden + dot(blended, wout_ref[...])).astype(BF16)


def backward_kernel(
    c_ref, x_ref, gain_ref, wqkv_ref, wout_ref, down_ref, upq_ref, upv_ref, cos_ref, sin_ref,
    q_ref, k_ref, v_ref, p_ref,
    out_ref, dq_ref, dv_ref, dlow_ref,
):
    c = c_ref[...]
    tokens = c.shape[0]
    width = GROUP * HEAD_SIZE
    cosine, sine = cos_ref[...], sin_ref[...]
    k_turns, v_turns = turns_of(k_ref[...]), turns_of(v_ref[...])
    dn = None
    dlow = None
    dk_products, dv_products = [], []
    for h in range(KEY_VALUE_HEADS):
        at = slice(h * width, (h + 1) * width)
        dblended = dot_nt(c, wout_ref[at, :]).astype(BF16)
        shares = p_ref[:, h * GROUP * tokens : (h + 1) * GROUP * tokens]
        dshares = dot_nt(dblended, expand(v_turns, h))
        dscores = []
        for g in range(GROUP):
            span = slice(g * tokens, (g + 1) * tokens)
            p = shares[:, span].astype(F32)
            dp = dshares[:, span]
            pdp = p * dp
            dscores.append(
                ((pdp - p * jnp.sum(pdp, axis=-1, keepdims=True)) * SCORE_SCALE).astype(BF16)
            )
        dscores = jnp.concatenate(dscores, axis=1)
        dq = dot(dscores, expand(k_turns, h))
        dq = rope(dq, cosine, -sine).astype(BF16)
        dq_ref[:, at] = dq
        part = dot_nt(dq, upq_ref[:, at])
        dlow = part if dlow is None else dlow + part
        part = dot_nt(dq, wqkv_ref[:, at])
        dn = part if dn is None else dn + part
        dv_products.append(dot_tn(shares, dblended))
        dk_products.append(dot_tn(dscores, q_ref[:, at]))
    dk = rope(fold(dk_products), cosine, -sine).astype(BF16)
    dv = fold(dv_products).astype(BF16)
    dv_ref[...] = dv
    dlow = (ADAPTER_SCALE * (dlow + dot_nt(dv, upv_ref[...]))).astype(BF16)
    dlow_ref[...] = dlow
    dn = dn + dot_nt(dk, wqkv_ref[:, QUERY_WIDTH : QUERY_WIDTH + KEY_WIDTH])
    dn = dn + dot_nt(dv, wqkv_ref[:, QUERY_WIDTH + KEY_WIDTH :])
    dn = dn + dot_nt(dlow, down_ref[...])
    hidden = x_ref[...].astype(F32)
    energy = jnp.mean(hidden * hidden, axis=-1, keepdims=True)
    scale = lax.rsqrt(energy + NORM_EPS)
    dy = dn * gain_ref[...]
    along = jnp.mean(hidden * dy, axis=-1, keepdims=True)
    dh = scale * dy - hidden * (scale * scale * scale * along)
    out_ref[...] = (c.astype(F32) + dh).astype(BF16)


def grads_kernel(n_ref, low_ref, dq_ref, dv_ref, dlow_ref, g_ref):
    g_ref[...] = jnp.zeros_like(g_ref)
    g_ref[0 : 2 * RANK, :] = dot_tn(dlow_ref[...], n_ref[...])[: 2 * RANK]
    low = low_ref[...]
    up_q = ADAPTER_SCALE * dot_tn(low, dq_ref[...])
    up_v = ADAPTER_SCALE * dot_tn(low, dv_ref[...])
    g_ref[2 * RANK : 3 * RANK, 0:QUERY_WIDTH] = up_q[:RANK]
    g_ref[2 * RANK : 3 * RANK, QUERY_WIDTH : QUERY_WIDTH + KEY_WIDTH] = up_v[RANK : 2 * RANK]


def call(kernel, outs, *args):
    return pl.pallas_call(
        kernel,
        out_shape=[jax.ShapeDtypeStruct(shape, dtype) for shape, dtype in outs],
        in_specs=[pl.BlockSpec(memory_space=pltpu.VMEM)] * len(args),
        out_specs=[pl.BlockSpec(memory_space=pltpu.VMEM)] * len(outs),
        compiler_params=pltpu.CompilerParams(vmem_limit_bytes=VMEM_LIMIT),
    )(*args)


def z_route(replicas, distance):
    return [(i, (i + distance * X_CHIPS) % replicas) for i in range(replicas)]


def x_route(replicas, distance):
    return [
        (i, i // X_CHIPS * X_CHIPS + (i % X_CHIPS + distance) % X_CHIPS) for i in range(replicas)
    ]


def gather_weights(shard, replica, replicas):
    rows, columns = shard.shape
    z_count = replicas // X_CHIPS
    z, x = replica // X_CHIPS, replica % X_CHIPS
    along_z = functools.partial(z_route, replicas)
    along_x = functools.partial(x_route, replicas)
    qkv_width = QUERY_WIDTH + 2 * KEY_WIDTH
    half = rows // 2
    qkv = jnp.zeros((z_count, X_CHIPS, rows, qkv_width), shard.dtype)
    out = jnp.zeros((z_count, X_CHIPS, half, 2 * QUERY_WIDTH), shard.dtype)

    def put(qkv, out, z_at, x_at, data):
        qkv = lax.dynamic_update_slice(qkv, data[None, None, :, :qkv_width], (z_at, x_at, 0, 0))
        sides = [data[:half, qkv_width:], data[half:, qkv_width:]]
        sides = jnp.concatenate(sides, axis=-1)[None, None]
        return qkv, lax.dynamic_update_slice(out, sides, (z_at, x_at, 0, 0))

    ahead = behind = shard
    fresh = [(z, shard)]
    late = None
    for step in range(1, z_count // 2 + 1):
        if step < z_count // 2:
            ahead = lax.ppermute(ahead, "dp", along_z(1))
            behind = lax.ppermute(behind, "dp", along_z(-1))
            fresh += [((z - step) % z_count, ahead), ((z + step) % z_count, behind)]
        else:
            upper = lax.ppermute(ahead[:half], "dp", along_z(1))
            lower = lax.ppermute(behind[half:], "dp", along_z(-1))
            fresh.append(((z + step) % z_count, jnp.concatenate([upper, lower], axis=0)))
        if step not in CUTS:
            continue
        chunk = jnp.stack([data for _, data in fresh])
        right = lax.ppermute(chunk, "dp", along_x(1))
        left = lax.ppermute(chunk, "dp", along_x(-1))
        far_upper = lax.ppermute(right[:, :half], "dp", along_x(1))
        far_lower = lax.ppermute(left[:, half:], "dp", along_x(-1))
        for i, (z_at, data) in enumerate(fresh):
            far = jnp.concatenate([far_upper[i], far_lower[i]], axis=0)
            qkv, out = put(qkv, out, z_at, x, data)
            qkv, out = put(qkv, out, z_at, (x - 1) % X_CHIPS, right[i])
            qkv, out = put(qkv, out, z_at, (x + 1) % X_CHIPS, left[i])
            qkv, out = put(qkv, out, z_at, (x + 2) % X_CHIPS, far)
        fresh = []
        if step == CUTS[1]:
            late = left
    return (
        qkv.reshape(replicas * rows, qkv_width),
        out.reshape(replicas * half, 2 * QUERY_WIDTH),
        late,
    )


def sum_over_replicas(grads, replica, replicas):
    rows, columns = grads.shape
    z_count = replicas // X_CHIPS
    x = replica % X_CHIPS
    part_width = columns // X_CHIPS
    parts = grads.reshape(rows, X_CHIPS, part_width).transpose(1, 0, 2)
    sent = parts.astype(BF16)
    total = lax.dynamic_index_in_dim(parts, x, 0, keepdims=False)
    for distance in range(1, X_CHIPS):
        piece = lax.dynamic_index_in_dim(sent, (x + distance) % X_CHIPS, 0, keepdims=False)
        total = total + lax.ppermute(piece, "dp", x_route(replicas, distance)).astype(F32)
    low_count = 4
    sent = total.astype(BF16)
    for distance in range(1, low_count):
        route = []
        for i in range(replicas):
            zi, xi = i // X_CHIPS, i % X_CHIPS
            to = zi // low_count * low_count + (zi % low_count + distance) % low_count
            route.append((i, to * X_CHIPS + xi))
        total = total + lax.ppermute(sent, "dp", route).astype(F32)
    sent = total.astype(BF16)
    for distance in range(1, z_count // low_count):
        route = z_route(replicas, distance * low_count)
        total = total + lax.ppermute(sent, "dp", route).astype(F32)
    sent = total.astype(BF16)
    whole = jnp.zeros((X_CHIPS, rows, part_width), F32)
    whole = lax.dynamic_update_slice(whole, total[None], (x, 0, 0))
    for distance in range(1, X_CHIPS):
        piece = lax.ppermute(sent, "dp", x_route(replicas, distance)).astype(F32)
        whole = lax.dynamic_update_slice(whole, piece[None], ((x - distance) % X_CHIPS, 0, 0))
    return whole.transpose(1, 0, 2).reshape(rows, columns)


def exchange_tokens(source_tokens, send_counts, replica, replicas, stream_count, late):
    slot_count = source_tokens.shape[0] // replicas
    features = source_tokens.shape[1]
    sent_counts = lax.dynamic_index_in_dim(send_counts, replica, 0, keepdims=False)
    send_start = jnp.cumsum(sent_counts) - sent_counts
    slot_ids = jnp.arange(slot_count, dtype=jnp.int32)
    occupied = slot_ids[None, :] < sent_counts[:, None]
    pick_rows = jnp.where(occupied, send_start[:, None] + slot_ids[None, :], -1).reshape(-1)
    own_rows = jnp.arange(source_tokens.shape[0], dtype=jnp.int32)
    choose = (pick_rows[:, None] == own_rows[None, :]).astype(BF16)
    packed = dot(choose, source_tokens).astype(BF16).reshape(replicas, slot_count, features)
    packed, _ = lax.optimization_barrier((packed, late))
    arrived = lax.all_to_all(packed, "dp", split_axis=0, concat_axis=0, tiled=True)
    incoming = lax.dynamic_index_in_dim(send_counts, replica, 1, keepdims=False)
    end_rows = jnp.cumsum(incoming)
    starts = end_rows - incoming
    places = jnp.arange(stream_count, dtype=jnp.int32)
    slot_place = starts[:, None] + slot_ids[None, :]
    slot_place = jnp.where(slot_ids[None, :] < incoming[:, None], slot_place, -1).reshape(-1)
    choose = (places[:, None] == slot_place[None, :]).astype(BF16)
    stream = dot(choose, arrived.reshape(replicas * slot_count, features)).astype(BF16)
    return stream, places < end_rows[replicas - 1]


def layout(segments, filled):
    micro_count, token_count = segments.shape
    tokens = micro_count * token_count
    segment = segments.reshape(tokens)
    places = jnp.arange(tokens, dtype=jnp.int32)
    sequence = places // token_count
    same = (segment[:, None] == segment[None, :]) & (sequence[:, None] == sequence[None, :])
    before = places[None, :] < places[:, None]
    position = jnp.sum(jnp.where(same & before, 1.0, 0.0).astype(F32), axis=1)
    alone = places[None, :] == places[:, None]
    allowed = (before & same & filled[:, None] & filled[None, :]) | alone
    half = HEAD_SIZE // 2
    frequency = ROPE_BASE ** (-2.0 * jnp.arange(half, dtype=F32) / HEAD_SIZE)
    angles = position[:, None] * frequency[None, :]
    cosine, sine = jnp.cos(angles), jnp.sin(angles)
    heads = LANES // HEAD_SIZE
    return (
        jnp.concatenate([cosine, cosine] * heads, axis=1),
        jnp.concatenate([-sine, sine] * heads, axis=1),
        allowed.astype(F32),
    )


def local(
    source_tokens,
    send_counts,
    doc_segments,
    out_cotangent,
    norm_gain,
    query_weight,
    frozen_key_matrix,
    frozen_value_matrix,
    out_weight,
    adapter_down,
    adapter_up_maps,
):
    replicas = lax.axis_size("dp")
    sections = lax.axis_size("section")
    replica = lax.axis_index("dp")
    section = lax.axis_index("section")
    features = source_tokens.shape[1]
    tokens = doc_segments.shape[0] * doc_segments.shape[1]

    half = out_weight.shape[2] // 2
    out_rows = jnp.concatenate([out_weight[0, :, :half], out_weight[0, :, half:]], axis=0)
    shard = jnp.concatenate(
        [query_weight[0], frozen_key_matrix[0], frozen_value_matrix[0], out_rows], axis=1
    )
    wqkv, wout, late = gather_weights(shard, replica, replicas)
    stream, filled = exchange_tokens(source_tokens, send_counts, replica, replicas, tokens, late)
    cosine, sine, allowed = layout(doc_segments, filled)
    gain = norm_gain[0].reshape(1, features)
    spare = LANES - 2 * RANK
    down = jnp.concatenate(
        [adapter_down[0, 0], adapter_down[0, 1], jnp.zeros((features, spare), BF16)], axis=1
    )
    up = adapter_up_maps[0]
    up_q = jnp.concatenate([up[:, :QUERY_WIDTH], jnp.zeros((LANES - RANK, QUERY_WIDTH), BF16)])
    up_v = jnp.concatenate(
        [
            jnp.zeros((RANK, KEY_WIDTH), BF16),
            up[:, QUERY_WIDTH:],
            jnp.zeros((spare, KEY_WIDTH), BF16),
        ]
    )

    saved_shapes = [
        ((tokens, features), BF16),
        ((tokens, QUERY_WIDTH), BF16),
        ((tokens, KEY_WIDTH), BF16),
        ((tokens, KEY_WIDTH), BF16),
        ((tokens, QUERY_HEADS * tokens), BF16),
        ((tokens, LANES), BF16),
        ((tokens, features), BF16),
    ]
    x = stream
    saved = tuple(jnp.zeros(shape, dtype) for shape, dtype in saved_shapes)
    for turn in range(sections):

        def run(x, saved):
            made = call(
                forward_kernel,
                [((tokens, features), BF16)] + saved_shapes,
                x, gain, wqkv, wout, down, up_q, up_v, cosine, sine, allowed,
            )
            return made[0], tuple(made[1:])

        y, saved = lax.cond(section == turn, run, lambda x, saved: (x, saved), x, saved)
        if turn + 1 < sections:
            x = lax.ppermute(y, "section", [(turn, turn + 1)])

    x, q, k, v, shares, low, normed = saved
    c = out_cotangent
    kept = (
        jnp.zeros((tokens, QUERY_WIDTH), BF16),
        jnp.zeros((tokens, KEY_WIDTH), BF16),
        jnp.zeros((tokens, LANES), BF16),
    )
    for turn in range(sections - 1, -1, -1):

        def run_back(c, kept):
            made = call(
                backward_kernel,
                [((tokens, features), BF16)] + [(t.shape, t.dtype) for t in kept],
                c, x, gain, wqkv, wout, down, up_q, up_v, cosine, sine, q, k, v, shares,
            )
            return made[0], tuple(made[1:])

        back, kept = lax.cond(section == turn, run_back, lambda c, kept: (c, kept), c, kept)
        if turn > 0:
            c = lax.ppermute(back, "section", [(turn, turn - 1)])

    (grads,) = call(
        grads_kernel, [((3 * RANK, features), F32)], normed, low, kept[0], kept[1], kept[2]
    )
    grads = sum_over_replicas(grads, replica, replicas)
    down_grads = grads[: 2 * RANK].reshape(2, RANK, features).transpose(0, 2, 1)
    up_grads = grads[2 * RANK :, : QUERY_WIDTH + KEY_WIDTH]
    return (down_grads[None], up_grads[None])


def solution(mesh):
    placed = (
        P("dp", None),
        P(),
        P("dp", None),
        P("dp", None),
        P("section", None),
        P("section", "dp", None),
        P("section", "dp", None),
        P("section", "dp", None),
        P("section", "dp", None),
        P("section", None, None, None),
        P("section", None, None),
    )
    return jax.shard_map(
        local,
        mesh=mesh,
        in_specs=placed,
        out_specs=(P("section", None, None, None), P("section", None, None)),
        check_vma=False,
    )
```

```python
import functools

import jax
import jax.numpy as jnp
from jax import lax
from jax.experimental import pallas as pl
from jax.experimental.pallas import tpu as pltpu
from jax.sharding import PartitionSpec as P

QUERY_HEADS = 16
KEY_VALUE_HEADS = 4
GROUP = QUERY_HEADS // KEY_VALUE_HEADS
HEAD_SIZE = 64
QUERY_WIDTH = QUERY_HEADS * HEAD_SIZE
KEY_WIDTH = KEY_VALUE_HEADS * HEAD_SIZE
RANK = 16
LANES = 128

ROPE_BASE = 500000.0
ADAPTER_SCALE = 2.0
NORM_EPS = 1e-05
SCORE_SCALE = HEAD_SIZE ** (-0.5)

X_CHIPS = 4

F32 = jnp.float32
BF16 = jnp.bfloat16
VMEM_LIMIT = 32 * 1024 * 1024
CUTS = (2, 5, 8)


def dot(a, b):
    return jnp.dot(a, b, preferred_element_type=F32)


def dot_nt(a, b):
    return lax.dot_general(a, b, (((1,), (1,)), ((), ())), preferred_element_type=F32)


def dot_tn(a, b):
    return lax.dot_general(a, b, (((0,), (0,)), ((), ())), preferred_element_type=F32)


def lanes_of(rows, width):
    return lax.broadcasted_iota(jnp.int32, (rows, width), 1)


def rope(t, cosine, signed_sine):
    rows, width = t.shape
    copies = width // LANES
    wide_cos = jnp.concatenate([cosine] * copies, axis=1)
    wide_sin = jnp.concatenate([signed_sine] * copies, axis=1)
    half = HEAD_SIZE // 2
    leading = (lanes_of(rows, width) % HEAD_SIZE) < half
    partner = jnp.where(leading, pltpu.roll(t, width - half, 1), pltpu.roll(t, half, 1))
    return t * wide_cos + partner * wide_sin


def expand(turned, head):
    rows, width = turned[0].shape
    block = lanes_of(rows, width) // HEAD_SIZE
    zero = jnp.zeros((), turned[0].dtype)
    parts = [
        jnp.where(block == g, turned[(g - head) % KEY_VALUE_HEADS], zero) for g in range(GROUP)
    ]
    return jnp.concatenate(parts, axis=0)


def turns_of(t):
    width = t.shape[1]
    wide = t.astype(F32)
    return [t] + [
        pltpu.roll(wide, j * HEAD_SIZE, 1).astype(t.dtype) for j in range(1, KEY_VALUE_HEADS)
    ]


def fold(products):
    rows = products[0].shape[0] // GROUP
    width = products[0].shape[1]
    block = lanes_of(rows, width) // HEAD_SIZE
    total = None
    for h, product in enumerate(products):
        diagonal = None
        for g in range(GROUP):
            part = jnp.where(block == g, product[g * rows : (g + 1) * rows], 0.0)
            diagonal = part if diagonal is None else diagonal + part
        pair = diagonal + pltpu.roll(diagonal, HEAD_SIZE, 1)
        whole = pair + pltpu.roll(pair, 2 * HEAD_SIZE, 1)
        kept = jnp.where(block == h, whole, 0.0)
        total = kept if total is None else total + kept
    return total


def load(copies):
    for copy in copies:
        copy.start()


def forward_kernel(
    last,
    x_hbm, gain_ref, wqkv_hbm, wout_hbm, down_ref, upq_ref, upv_ref, cos_ref, sin_ref, mask_ref,
    y_ref, x_ref, q_ref, k_ref, v_ref, p_ref, low_ref, n_ref,
    wqkv, wout, sems,
):
    width = GROUP * HEAD_SIZE
    head_at = [pl.ds(h * width, width) for h in range(KEY_VALUE_HEADS)]
    key_at = pl.ds(QUERY_WIDTH, 2 * KEY_WIDTH)
    get_x = pltpu.make_async_copy(x_hbm, x_ref, sems.at[0])
    get_kv = pltpu.make_async_copy(wqkv_hbm.at[:, key_at], wqkv.at[:, key_at], sems.at[1])
    get_q = [
        pltpu.make_async_copy(wqkv_hbm.at[:, at], wqkv.at[:, at], sems.at[2 + h])
        for h, at in enumerate(head_at)
    ]
    get_out = pltpu.make_async_copy(wout_hbm, wout, sems.at[2 + KEY_VALUE_HEADS])
    load([get_x, get_kv] + get_q + ([] if last else [get_out]))
    get_x.wait()
    hidden = x_ref[...].astype(F32)
    energy = jnp.mean(hidden * hidden, axis=-1, keepdims=True)
    n = (hidden * lax.rsqrt(energy + NORM_EPS) * gain_ref[...]).astype(BF16)
    n_ref[...] = n
    cosine, sine = cos_ref[...], sin_ref[...]
    low = dot(n, down_ref[...]).astype(BF16)
    low_ref[...] = low
    get_kv.wait()
    kv = dot(n, wqkv[:, key_at])
    k = rope(kv[:, :KEY_WIDTH], cosine, sine).astype(BF16)
    k_ref[...] = k
    v = kv[:, KEY_WIDTH:] + ADAPTER_SCALE * dot(low, upv_ref[...])
    v = v.astype(BF16)
    v_ref[...] = v
    k_turns, v_turns = turns_of(k), turns_of(v)
    allowed = mask_ref[...] > 0.0
    tokens = hidden.shape[0]
    blended = []
    for h, at in enumerate(head_at):
        get_q[h].wait()
        q = dot(n, wqkv[:, at]) + ADAPTER_SCALE * dot(low, upq_ref[:, at])
        q = rope(q, cosine, sine).astype(BF16)
        q_ref[:, at] = q
        scores = dot_nt(q, expand(k_turns, h)) * SCORE_SCALE
        shares = []
        for g in range(GROUP):
            weights = jnp.where(allowed, jnp.exp(scores[:, g * tokens : (g + 1) * tokens]), 0.0)
            shares.append((weights / jnp.sum(weights, axis=-1, keepdims=True)).astype(BF16))
        shares = jnp.concatenate(shares, axis=1)
        p_ref[:, h * GROUP * tokens : (h + 1) * GROUP * tokens] = shares
        if not last:
            blended.append(dot(shares, expand(v_turns, h)).astype(BF16))
    if last:
        y_ref[...] = jnp.zeros_like(y_ref)
        return
    get_out.wait()
    y_ref[...] = (hidden + dot(jnp.concatenate(blended, axis=1), wout[...])).astype(BF16)


def backward_kernel(
    first,
    c_hbm, x_ref, gain_ref, wqkv_hbm, wout_hbm, down_ref, upq_ref, upv_ref, cos_ref, sin_ref,
    q_ref, k_ref, v_ref, p_ref,
    out_ref, dq_ref, dv_ref, dlow_ref,
    c_ref, wqkv, wout, sems,
):
    width = GROUP * HEAD_SIZE
    head_at = [pl.ds(h * width, width) for h in range(KEY_VALUE_HEADS)]
    key_at = pl.ds(QUERY_WIDTH, 2 * KEY_WIDTH)
    get_c = pltpu.make_async_copy(c_hbm, c_ref, sems.at[0])
    get_out = [
        pltpu.make_async_copy(wout_hbm.at[at, :], wout.at[at, :], sems.at[1 + h])
        for h, at in enumerate(head_at)
    ]
    get_q = [
        pltpu.make_async_copy(
            wqkv_hbm.at[:, at], wqkv.at[:, at], sems.at[1 + KEY_VALUE_HEADS + h]
        )
        for h, at in enumerate(head_at)
    ]
    get_kv = pltpu.make_async_copy(
        wqkv_hbm.at[:, key_at], wqkv.at[:, key_at], sems.at[1 + 2 * KEY_VALUE_HEADS]
    )
    load([get_c])
    for h in range(KEY_VALUE_HEADS):
        load([get_out[h]] + ([] if first else [get_q[h]]))
    if not first:
        load([get_kv])
    k_turns, v_turns = turns_of(k_ref[...]), turns_of(v_ref[...])
    cosine, sine = cos_ref[...], sin_ref[...]
    get_c.wait()
    c = c_ref[...]
    tokens = c.shape[0]
    dn = None
    dlow = None
    dk_products, dv_products = [], []
    for h, at in enumerate(head_at):
        get_out[h].wait()
        dblended = dot_nt(c, wout[at, :]).astype(BF16)
        shares = p_ref[:, h * GROUP * tokens : (h + 1) * GROUP * tokens]
        dshares = dot_nt(dblended, expand(v_turns, h))
        dscores = []
        for g in range(GROUP):
            span = slice(g * tokens, (g + 1) * tokens)
            p = shares[:, span].astype(F32)
            dp = dshares[:, span]
            pdp = p * dp
            dscores.append(
                ((pdp - p * jnp.sum(pdp, axis=-1, keepdims=True)) * SCORE_SCALE).astype(BF16)
            )
        dscores = jnp.concatenate(dscores, axis=1)
        dq = dot(dscores, expand(k_turns, h))
        dq = rope(dq, cosine, -sine).astype(BF16)
        dq_ref[:, at] = dq
        part = dot_nt(dq, upq_ref[:, at])
        dlow = part if dlow is None else dlow + part
        dv_products.append(dot_tn(shares, dblended))
        if not first:
            dk_products.append(dot_tn(dscores, q_ref[:, at]))
            get_q[h].wait()
            part = dot_nt(dq, wqkv[:, at])
            dn = part if dn is None else dn + part
    dv = fold(dv_products).astype(BF16)
    dv_ref[...] = dv
    dlow = (ADAPTER_SCALE * (dlow + dot_nt(dv, upv_ref[...]))).astype(BF16)
    dlow_ref[...] = dlow
    if first:
        out_ref[...] = jnp.zeros_like(out_ref)
        return
    dk = rope(fold(dk_products), cosine, -sine).astype(BF16)
    get_kv.wait()
    dn = dn + dot_nt(jnp.concatenate([dk, dv], axis=1), wqkv[:, key_at])
    dn = dn + dot_nt(dlow, down_ref[...])
    hidden = x_ref[...].astype(F32)
    energy = jnp.mean(hidden * hidden, axis=-1, keepdims=True)
    scale = lax.rsqrt(energy + NORM_EPS)
    dy = dn * gain_ref[...]
    along = jnp.mean(hidden * dy, axis=-1, keepdims=True)
    dh = scale * dy - hidden * (scale * scale * scale * along)
    out_ref[...] = (c.astype(F32) + dh).astype(BF16)


def grads_kernel(n_ref, low_ref, dq_ref, dv_ref, dlow_ref, g_ref):
    part = g_ref.shape[2]
    down = dot_tn(dlow_ref[...], n_ref[...])[: 2 * RANK].astype(BF16)
    low = low_ref[...]
    up_q = ADAPTER_SCALE * dot_tn(low, dq_ref[...])[:RANK]
    up_v = ADAPTER_SCALE * dot_tn(low, dv_ref[...])[RANK : 2 * RANK]
    spare = jnp.zeros((RANK, g_ref.shape[0] * part - QUERY_WIDTH - KEY_WIDTH), F32)
    up = jnp.concatenate([up_q, up_v, spare], axis=1).astype(BF16)
    for i in range(g_ref.shape[0]):
        at = slice(i * part, (i + 1) * part)
        g_ref[i, 0 : 2 * RANK, :] = down[:, at]
        g_ref[i, 2 * RANK : 3 * RANK, :] = up[:, at]


def place_kernel(offsets, place_ref, *refs):
    own, right, left, far_upper, far_lower = refs[:5]
    qkv, out, sems = refs[-3:]
    z_count, x_count, rows, qkv_width = qkv.shape
    half, width = rows // 2, out.shape[3] // 2
    z, x = place_ref[0], place_ref[1]
    ends = []
    for i, offset in enumerate(offsets):
        z_at = lax.rem(z + (offset + z_count), z_count)
        for source, turn in ((own, 0), (right, x_count - 1), (left, 1)):
            x_at = lax.rem(x + turn, x_count)
            ends += [
                (source.at[i, :, pl.ds(0, qkv_width)], qkv.at[z_at, x_at]),
                (
                    source.at[i, pl.ds(0, half), pl.ds(qkv_width, width)],
                    out.at[z_at, x_at, :, pl.ds(0, width)],
                ),
                (
                    source.at[i, pl.ds(half, half), pl.ds(qkv_width, width)],
                    out.at[z_at, x_at, :, pl.ds(width, width)],
                ),
            ]
        x_at = lax.rem(x + 2, x_count)
        for source, side in ((far_upper, 0), (far_lower, 1)):
            ends += [
                (
                    source.at[i, :, pl.ds(0, qkv_width)],
                    qkv.at[z_at, x_at, pl.ds(side * half, half)],
                ),
                (
                    source.at[i, :, pl.ds(qkv_width, width)],
                    out.at[z_at, x_at, :, pl.ds(side * width, width)],
                ),
            ]
    copies = [pltpu.make_async_copy(a, b, sems.at[j]) for j, (a, b) in enumerate(ends)]
    load(copies)
    for copy in copies:
        copy.wait()


def place(offsets, at, pieces, kept, shapes):
    anywhere = pl.BlockSpec(memory_space=pl.ANY)
    first_kept = 1 + len(pieces)
    return pl.pallas_call(
        functools.partial(place_kernel, offsets),
        out_shape=[jax.ShapeDtypeStruct(shape, BF16) for shape in shapes],
        in_specs=[pl.BlockSpec(memory_space=pltpu.SMEM)] + [anywhere] * (len(pieces) + len(kept)),
        out_specs=[anywhere] * len(shapes),
        scratch_shapes=[pltpu.SemaphoreType.DMA((13 * len(offsets),))],
        input_output_aliases={first_kept + i: i for i in range(len(kept))},
    )(at, *pieces, *kept)


def call(kernel, outs, args, from_hbm=(), scratch=()):
    return pl.pallas_call(
        kernel,
        out_shape=[jax.ShapeDtypeStruct(shape, dtype) for shape, dtype in outs],
        in_specs=[
            pl.BlockSpec(memory_space=pl.ANY if i in from_hbm else pltpu.VMEM)
            for i in range(len(args))
        ],
        out_specs=[pl.BlockSpec(memory_space=pltpu.VMEM)] * len(outs),
        scratch_shapes=list(scratch),
        compiler_params=pltpu.CompilerParams(vmem_limit_bytes=VMEM_LIMIT),
    )(*args)


def z_route(replicas, distance):
    return [(i, (i + distance * X_CHIPS) % replicas) for i in range(replicas)]


def x_route(replicas, distance):
    return [
        (i, i // X_CHIPS * X_CHIPS + (i % X_CHIPS + distance) % X_CHIPS) for i in range(replicas)
    ]


def gather_weights(shard, replica, replicas):
    rows, columns = shard.shape
    z_count = replicas // X_CHIPS
    z, x = replica // X_CHIPS, replica % X_CHIPS
    along_z = functools.partial(z_route, replicas)
    along_x = functools.partial(x_route, replicas)
    qkv_width = QUERY_WIDTH + 2 * KEY_WIDTH
    half = rows // 2
    shapes = [
        (z_count, X_CHIPS, rows, qkv_width),
        (z_count, X_CHIPS, half, 2 * (columns - qkv_width)),
    ]
    at = jnp.stack([z, x]).astype(jnp.int32)
    placed = ()
    ahead = behind = shard
    fresh = [(0, shard)]
    late = None
    for step in range(1, z_count // 2 + 1):
        if step < z_count // 2:
            ahead = lax.ppermute(ahead, "dp", along_z(1))
            behind = lax.ppermute(behind, "dp", along_z(-1))
            fresh += [(-step, ahead), (step, behind)]
        else:
            upper = lax.ppermute(ahead[:half], "dp", along_z(1))
            lower = lax.ppermute(behind[half:], "dp", along_z(-1))
            fresh.append((step, jnp.concatenate([upper, lower], axis=0)))
        if step not in CUTS:
            continue
        chunk = jnp.stack([data for _, data in fresh])
        right = lax.ppermute(chunk, "dp", along_x(1))
        left = lax.ppermute(chunk, "dp", along_x(-1))
        far_upper = lax.ppermute(right[:, :half], "dp", along_x(1))
        far_lower = lax.ppermute(left[:, half:], "dp", along_x(-1))
        pieces = (chunk, right, left, far_upper, far_lower)
        placed = place([offset for offset, _ in fresh], at, pieces, placed, shapes)
        fresh = []
        if step == CUTS[1]:
            late = left
    return (
        placed[0].reshape(replicas * rows, qkv_width),
        placed[1].reshape(replicas * half, 2 * (columns - qkv_width)),
        late,
    )


def sum_over_replicas(parts, replica, replicas):
    count, rows, columns = parts.shape
    x = replica % X_CHIPS
    low_bit, high_bit = x % 2, x // 2

    def swap(t, mask):
        return lax.ppermute(t, "dp", [(i, i ^ mask) for i in range(replicas)])

    def add(t, other):
        return (t.astype(F32) + other.astype(F32)).astype(BF16)

    def pick(t, axis, at):
        return lax.dynamic_index_in_dim(t, at, axis, keepdims=False)

    def join(own, other, bit, axis):
        return jnp.where(
            bit == 0, jnp.stack([own, other], axis=axis), jnp.stack([other, own], axis=axis)
        )

    total = parts.reshape(2, 2, rows, columns)
    total = add(pick(total, 1, low_bit), swap(pick(total, 1, 1 - low_bit), 1))
    total = add(pick(total, 0, high_bit), swap(pick(total, 0, 1 - high_bit), 2))
    mask = X_CHIPS
    while mask < replicas:
        total = add(total, swap(total, mask))
        mask *= 2
    total = join(total, swap(total, 2), high_bit, 0)
    total = join(total, swap(total, 1), low_bit, 1)
    whole = total.reshape(count, rows, columns).astype(F32)
    return whole.transpose(1, 0, 2).reshape(rows, count * columns)


def exchange_tokens(source_tokens, send_counts, replica, replicas, stream_count, late):
    slot_count = source_tokens.shape[0] // replicas
    features = source_tokens.shape[1]
    sent_counts = lax.dynamic_index_in_dim(send_counts, replica, 0, keepdims=False)
    send_start = jnp.cumsum(sent_counts) - sent_counts
    slot_ids = jnp.arange(slot_count, dtype=jnp.int32)
    occupied = slot_ids[None, :] < sent_counts[:, None]
    pick_rows = jnp.where(occupied, send_start[:, None] + slot_ids[None, :], -1).reshape(-1)
    own_rows = jnp.arange(source_tokens.shape[0], dtype=jnp.int32)
    choose = (pick_rows[:, None] == own_rows[None, :]).astype(BF16)
    packed = dot(choose, source_tokens).astype(BF16).reshape(replicas, slot_count, features)
    packed, _ = lax.optimization_barrier((packed, late))
    arrived = lax.all_to_all(packed, "dp", split_axis=0, concat_axis=0, tiled=True)
    incoming = lax.dynamic_index_in_dim(send_counts, replica, 1, keepdims=False)
    end_rows = jnp.cumsum(incoming)
    starts = end_rows - incoming
    places = jnp.arange(stream_count, dtype=jnp.int32)
    slot_place = starts[:, None] + slot_ids[None, :]
    slot_place = jnp.where(slot_ids[None, :] < incoming[:, None], slot_place, -1).reshape(-1)
    choose = (places[:, None] == slot_place[None, :]).astype(BF16)
    stream = dot(choose, arrived.reshape(replicas * slot_count, features)).astype(BF16)
    return stream, places < end_rows[replicas - 1]


def layout(segments, filled):
    micro_count, token_count = segments.shape
    tokens = micro_count * token_count
    segment = segments.reshape(tokens)
    places = jnp.arange(tokens, dtype=jnp.int32)
    sequence = places // token_count
    same = (segment[:, None] == segment[None, :]) & (sequence[:, None] == sequence[None, :])
    before = places[None, :] < places[:, None]
    position = jnp.sum(jnp.where(same & before, 1.0, 0.0).astype(F32), axis=1)
    alone = places[None, :] == places[:, None]
    allowed = (before & same & filled[:, None] & filled[None, :]) | alone
    half = HEAD_SIZE // 2
    frequency = ROPE_BASE ** (-2.0 * jnp.arange(half, dtype=F32) / HEAD_SIZE)
    angles = position[:, None] * frequency[None, :]
    cosine, sine = jnp.cos(angles), jnp.sin(angles)
    heads = LANES // HEAD_SIZE
    return (
        jnp.concatenate([cosine, cosine] * heads, axis=1),
        jnp.concatenate([-sine, sine] * heads, axis=1),
        allowed.astype(F32),
    )


def local(
    source_tokens,
    send_counts,
    doc_segments,
    out_cotangent,
    norm_gain,
    query_weight,
    frozen_key_matrix,
    frozen_value_matrix,
    out_weight,
    adapter_down,
    adapter_up_maps,
):
    replicas = lax.axis_size("dp")
    sections = lax.axis_size("section")
    replica = lax.axis_index("dp")
    section = lax.axis_index("section")
    features = source_tokens.shape[1]
    tokens = doc_segments.shape[0] * doc_segments.shape[1]

    half = out_weight.shape[2] // 2
    out_rows = jnp.concatenate([out_weight[0, :, :half], out_weight[0, :, half:]], axis=0)
    shard = jnp.concatenate(
        [query_weight[0], frozen_key_matrix[0], frozen_value_matrix[0], out_rows], axis=1
    )
    wqkv, wout, late = gather_weights(shard, replica, replicas)
    stream, filled = exchange_tokens(source_tokens, send_counts, replica, replicas, tokens, late)
    cosine, sine, allowed = layout(doc_segments, filled)
    gain = norm_gain[0].reshape(1, features)
    spare = LANES - 2 * RANK
    down = jnp.concatenate(
        [adapter_down[0, 0], adapter_down[0, 1], jnp.zeros((features, spare), BF16)], axis=1
    )
    up = adapter_up_maps[0]
    up_q = jnp.concatenate([up[:, :QUERY_WIDTH], jnp.zeros((LANES - RANK, QUERY_WIDTH), BF16)])
    up_v = jnp.concatenate(
        [
            jnp.zeros((RANK, KEY_WIDTH), BF16),
            up[:, QUERY_WIDTH:],
            jnp.zeros((spare, KEY_WIDTH), BF16),
        ]
    )

    saved_shapes = [
        ((tokens, features), BF16),
        ((tokens, QUERY_WIDTH), BF16),
        ((tokens, KEY_WIDTH), BF16),
        ((tokens, KEY_WIDTH), BF16),
        ((tokens, QUERY_HEADS * tokens), BF16),
        ((tokens, LANES), BF16),
        ((tokens, features), BF16),
    ]
    weight_space = [pltpu.VMEM(wqkv.shape, BF16), pltpu.VMEM(wout.shape, BF16)]
    x = stream
    saved = tuple(jnp.zeros(shape, dtype) for shape, dtype in saved_shapes)
    for turn in range(sections):

        def run(x, saved):
            made = call(
                functools.partial(forward_kernel, turn + 1 == sections),
                [((tokens, features), BF16)] + saved_shapes,
                (x, gain, wqkv, wout, down, up_q, up_v, cosine, sine, allowed),
                (0, 2, 3),
                weight_space + [pltpu.SemaphoreType.DMA((3 + KEY_VALUE_HEADS,))],
            )
            return made[0], tuple(made[1:])

        y, saved = lax.cond(section == turn, run, lambda x, saved: (x, saved), x, saved)
        if turn + 1 < sections:
            x = lax.ppermute(y, "section", [(turn, turn + 1)])

    x, q, k, v, shares, low, normed = saved
    c = out_cotangent
    kept = (
        jnp.zeros((tokens, QUERY_WIDTH), BF16),
        jnp.zeros((tokens, KEY_WIDTH), BF16),
        jnp.zeros((tokens, LANES), BF16),
    )
    for turn in range(sections - 1, -1, -1):

        def run_back(c, kept):
            made = call(
                functools.partial(backward_kernel, turn == 0),
                [((tokens, features), BF16)] + [(t.shape, t.dtype) for t in kept],
                (c, x, gain, wqkv, wout, down, up_q, up_v, cosine, sine, q, k, v, shares),
                (0, 3, 4),
                [pltpu.VMEM((tokens, features), BF16)]
                + weight_space
                + [pltpu.SemaphoreType.DMA((2 + 2 * KEY_VALUE_HEADS,))],
            )
            return made[0], tuple(made[1:])

        back, kept = lax.cond(section == turn, run_back, lambda c, kept: (c, kept), c, kept)
        if turn > 0:
            c = lax.ppermute(back, "section", [(turn, turn - 1)])

    (grads,) = call(
        grads_kernel,
        [((X_CHIPS, 3 * RANK, features // X_CHIPS), BF16)],
        (normed, low, kept[0], kept[1], kept[2]),
    )
    grads = sum_over_replicas(grads, replica, replicas)
    down_grads = grads[: 2 * RANK].reshape(2, RANK, features).transpose(0, 2, 1)
    up_grads = grads[2 * RANK :, : QUERY_WIDTH + KEY_WIDTH]
    return (down_grads[None], up_grads[None])


def solution(mesh):
    placed = (
        P("dp", None),
        P(),
        P("dp", None),
        P("dp", None),
        P("section", None),
        P("section", "dp", None),
        P("section", "dp", None),
        P("section", "dp", None),
        P("section", "dp", None),
        P("section", None, None, None),
        P("section", None, None),
    )
    return jax.shard_map(
        local,
        mesh=mesh,
        in_specs=placed,
        out_specs=(P("section", None, None, None), P("section", None, None)),
        check_vma=False,
    )
```

```python
import functools

import jax
import jax.numpy as jnp
from jax import lax
from jax.experimental import pallas as pl
from jax.experimental.pallas import tpu as pltpu
from jax.sharding import PartitionSpec as P

QUERY_HEADS = 16
KEY_VALUE_HEADS = 4
GROUP = QUERY_HEADS // KEY_VALUE_HEADS
HEAD_SIZE = 64
QUERY_WIDTH = QUERY_HEADS * HEAD_SIZE
KEY_WIDTH = KEY_VALUE_HEADS * HEAD_SIZE
RANK = 16
LANES = 128

ROPE_BASE = 500000.0
ADAPTER_SCALE = 2.0
NORM_EPS = 1e-05
SCORE_SCALE = HEAD_SIZE ** (-0.5)

X_CHIPS = 4

F32 = jnp.float32
BF16 = jnp.bfloat16
VMEM_LIMIT = 32 * 1024 * 1024
CUTS = (2, 5, 8)


def dot(a, b):
    return jnp.dot(a, b, preferred_element_type=F32)


def dot_nt(a, b):
    return lax.dot_general(a, b, (((1,), (1,)), ((), ())), preferred_element_type=F32)


def dot_tn(a, b):
    return lax.dot_general(a, b, (((0,), (0,)), ((), ())), preferred_element_type=F32)


def lanes_of(rows, width):
    return lax.broadcasted_iota(jnp.int32, (rows, width), 1)


def rope(t, cosine, signed_sine):
    rows, width = t.shape
    copies = width // LANES
    wide_cos = jnp.concatenate([cosine] * copies, axis=1)
    wide_sin = jnp.concatenate([signed_sine] * copies, axis=1)
    half = HEAD_SIZE // 2
    leading = (lanes_of(rows, width) % HEAD_SIZE) < half
    partner = jnp.where(leading, pltpu.roll(t, width - half, 1), pltpu.roll(t, half, 1))
    return t * wide_cos + partner * wide_sin


def expand(turned, head):
    rows, width = turned[0].shape
    block = lanes_of(rows, width) // HEAD_SIZE
    zero = jnp.zeros((), turned[0].dtype)
    parts = [
        jnp.where(block == g, turned[(g - head) % KEY_VALUE_HEADS], zero) for g in range(GROUP)
    ]
    return jnp.concatenate(parts, axis=0)


def turns_of(t):
    width = t.shape[1]
    wide = t.astype(F32)
    return [t] + [
        pltpu.roll(wide, j * HEAD_SIZE, 1).astype(t.dtype) for j in range(1, KEY_VALUE_HEADS)
    ]


def fold(products):
    rows = products[0].shape[0] // GROUP
    width = products[0].shape[1]
    block = lanes_of(rows, width) // HEAD_SIZE
    total = None
    for h, product in enumerate(products):
        diagonal = None
        for g in range(GROUP):
            part = jnp.where(block == g, product[g * rows : (g + 1) * rows], 0.0)
            diagonal = part if diagonal is None else diagonal + part
        pair = diagonal + pltpu.roll(diagonal, HEAD_SIZE, 1)
        whole = pair + pltpu.roll(pair, 2 * HEAD_SIZE, 1)
        kept = jnp.where(block == h, whole, 0.0)
        total = kept if total is None else total + kept
    return total


def load(copies):
    for copy in copies:
        copy.start()


def forward_kernel(turn, last, turn_ref, x_ref, *refs):
    fixed, y_ref, kept = refs[:6], refs[13], refs[14:21]

    @pl.when(turn_ref[0] == turn)
    def _():
        forward_step(last, x_ref, *fixed, y_ref, *kept)


def forward_step(
    last,
    x_ref, tables, gain, down, up, wqkv, wout,
    y_ref, kept_x_ref, q_ref, k_ref, v_ref, p_ref, low_ref, n_ref,
):
    width = GROUP * HEAD_SIZE
    head_at = [slice(h * width, (h + 1) * width) for h in range(KEY_VALUE_HEADS)]
    cosine, sine = tables[0], tables[1]
    allowed = tables[2] > 0.0
    x = x_ref[...]
    kept_x_ref[...] = x
    hidden = x.astype(F32)
    energy = jnp.mean(hidden * hidden, axis=-1, keepdims=True)
    n = (hidden * lax.rsqrt(energy + NORM_EPS) * gain[...]).astype(BF16)
    n_ref[...] = n
    low = dot_nt(n, down[...]).astype(BF16)
    low_ref[...] = low
    kv = dot(n, wqkv[:, QUERY_WIDTH:])
    k = rope(kv[:, :KEY_WIDTH], cosine, sine).astype(BF16)
    k_ref[...] = k
    v = kv[:, KEY_WIDTH:] + ADAPTER_SCALE * dot(low, up[:, QUERY_WIDTH:])
    v = v.astype(BF16)
    v_ref[...] = v
    k_turns, v_turns = turns_of(k), turns_of(v)
    tokens = hidden.shape[0]
    blended = []
    for h, at in enumerate(head_at):
        q = dot(n, wqkv[:, at]) + ADAPTER_SCALE * dot(low, up[:, at])
        q = rope(q, cosine, sine).astype(BF16)
        q_ref[:, at] = q
        scores = dot_nt(q, expand(k_turns, h)) * SCORE_SCALE
        shares = []
        for g in range(GROUP):
            weights = jnp.where(allowed, jnp.exp(scores[:, g * tokens : (g + 1) * tokens]), 0.0)
            shares.append((weights / jnp.sum(weights, axis=-1, keepdims=True)).astype(BF16))
        shares = jnp.concatenate(shares, axis=1)
        p_ref[:, h * GROUP * tokens : (h + 1) * GROUP * tokens] = shares
        if not last:
            blended.append(dot(shares, expand(v_turns, h)).astype(BF16))
    if not last:
        y_ref[...] = (hidden + dot(jnp.concatenate(blended, axis=1), wout[...])).astype(BF16)


def backward_kernel(turn, first, turn_ref, c_ref, *refs):
    fixed, held, out_ref, kept = refs[:6], refs[6:11], refs[14], refs[15:18]

    @pl.when(turn_ref[0] == turn)
    def _():
        backward_step(first, c_ref, *fixed, *held, out_ref, *kept)


def backward_step(
    first,
    c_ref, tables, gain, down, up, wqkv, wout,
    x_ref, q_ref, k_ref, v_ref, p_ref,
    out_ref, dq_ref, dv_ref, dlow_ref,
):
    width = GROUP * HEAD_SIZE
    head_at = [slice(h * width, (h + 1) * width) for h in range(KEY_VALUE_HEADS)]
    cosine, sine = tables[0], tables[1]
    k_turns, v_turns = turns_of(k_ref[...]), turns_of(v_ref[...])
    c = c_ref[...]
    tokens = c.shape[0]
    dn = None
    dlow = None
    dk_products, dv_products = [], []
    for h, at in enumerate(head_at):
        dblended = dot_nt(c, wout[at, :]).astype(BF16)
        shares = p_ref[:, h * GROUP * tokens : (h + 1) * GROUP * tokens]
        dshares = dot_nt(dblended, expand(v_turns, h))
        dscores = []
        for g in range(GROUP):
            span = slice(g * tokens, (g + 1) * tokens)
            p = shares[:, span].astype(F32)
            dp = dshares[:, span]
            pdp = p * dp
            dscores.append(
                ((pdp - p * jnp.sum(pdp, axis=-1, keepdims=True)) * SCORE_SCALE).astype(BF16)
            )
        dscores = jnp.concatenate(dscores, axis=1)
        dq = dot(dscores, expand(k_turns, h))
        dq = rope(dq, cosine, -sine).astype(BF16)
        dq_ref[:, at] = dq
        part = dot_nt(dq, up[:, at])
        dlow = part if dlow is None else dlow + part
        dv_products.append(dot_tn(shares, dblended))
        if not first:
            dk_products.append(dot_tn(dscores, q_ref[:, at]))
            part = dot_nt(dq, wqkv[:, at])
            dn = part if dn is None else dn + part
    dv = fold(dv_products).astype(BF16)
    dv_ref[...] = dv
    dlow = (ADAPTER_SCALE * (dlow + dot_nt(dv, up[:, QUERY_WIDTH:]))).astype(BF16)
    dlow_ref[...] = dlow
    if first:
        return
    dk = rope(fold(dk_products), cosine, -sine).astype(BF16)
    dn = dn + dot_nt(jnp.concatenate([dk, dv], axis=1), wqkv[:, QUERY_WIDTH:])
    dn = dn + dot(dlow, down[...])
    hidden = x_ref[...].astype(F32)
    energy = jnp.mean(hidden * hidden, axis=-1, keepdims=True)
    scale = lax.rsqrt(energy + NORM_EPS)
    dy = dn * gain[...]
    along = jnp.mean(hidden * dy, axis=-1, keepdims=True)
    dh = scale * dy - hidden * (scale * scale * scale * along)
    out_ref[...] = (c.astype(F32) + dh).astype(BF16)


def grads_kernel(n_ref, low_ref, dq_ref, dv_ref, dlow_ref, g_ref):
    part = g_ref.shape[2]
    down = dot_tn(dlow_ref[...], n_ref[...]).astype(BF16)
    low = low_ref[...]
    up_q = ADAPTER_SCALE * dot_tn(low, dq_ref[...])[:RANK]
    up_v = ADAPTER_SCALE * dot_tn(low, dv_ref[...])[RANK : 2 * RANK]
    spare = jnp.zeros((RANK, g_ref.shape[0] * part - QUERY_WIDTH - KEY_WIDTH), F32)
    up = jnp.concatenate([up_q, up_v, spare], axis=1).astype(BF16)
    for i in range(g_ref.shape[0]):
        at = slice(i * part, (i + 1) * part)
        g_ref[i, 0 : 2 * RANK, :] = down[:, at]
        g_ref[i, 2 * RANK : 3 * RANK, :] = up[:, at]


def place_kernel(offsets, at_ref, *refs):
    own, right, left, far_upper, far_lower = refs[:5]
    qkv, out, qkv_held, out_held, sems = refs[-5:]
    z_count, x_count, rows, qkv_width = qkv.shape
    half, width = rows // 2, out.shape[3] // 2
    z, x = at_ref[0], at_ref[1]
    first, second = pl.ds(0, half), pl.ds(half, half)
    wide, rest = pl.ds(0, qkv_width), pl.ds(qkv_width, width)
    sides = pl.ds(0, width), pl.ds(width, width)
    ends = []
    for source, turn in ((own, 0), (right, x_count - 1), (left, 1)):
        x_at = lax.rem(x + turn, x_count)
        ends.append((source.at[:, :, wide], qkv_held.at[:, x_at]))
        ends.append((source.at[:, first, rest], out_held.at[:, x_at, :, sides[0]]))
        ends.append((source.at[:, second, rest], out_held.at[:, x_at, :, sides[1]]))
    x_at = lax.rem(x + 2, x_count)
    for source, rows_at, side in ((far_upper, first, sides[0]), (far_lower, second, sides[1])):
        ends.append((source.at[:, :, wide], qkv_held.at[:, x_at, rows_at]))
        ends.append((source.at[:, :, rest], out_held.at[:, x_at, :, side]))
    copies = [pltpu.make_async_copy(a, b, sems.at[i]) for i, (a, b) in enumerate(ends)]
    for copy in copies:
        copy.start()
    for copy in copies:
        copy.wait()
    ends = []
    for i, offset in enumerate(offsets):
        z_at = lax.rem(z + (offset + z_count), z_count)
        ends += [(qkv_held.at[i], qkv.at[z_at]), (out_held.at[i], out.at[z_at])]
    copies = [pltpu.make_async_copy(a, b, sems.at[i]) for i, (a, b) in enumerate(ends)]
    for copy in copies:
        copy.start()
    for copy in copies:
        copy.wait()


def place(offsets, at, pieces, kept, shapes):
    anywhere = pl.BlockSpec(memory_space=pl.ANY)
    first_kept = 1 + len(pieces)
    held = [pltpu.VMEM((len(offsets), *shape[1:]), BF16) for shape in shapes]
    return pl.pallas_call(
        functools.partial(place_kernel, offsets),
        out_shape=[jax.ShapeDtypeStruct(shape, BF16) for shape in shapes],
        in_specs=[pl.BlockSpec(memory_space=pltpu.SMEM)] + [anywhere] * (len(pieces) + len(kept)),
        out_specs=[pl.BlockSpec(memory_space=pltpu.HBM)] * len(shapes),
        scratch_shapes=held + [pltpu.SemaphoreType.DMA((13 + 2 * len(offsets),))],
        input_output_aliases={first_kept + i: i for i in range(len(kept))},
        compiler_params=pltpu.CompilerParams(vmem_limit_bytes=VMEM_LIMIT),
    )(at, *pieces, *kept)


def call(kernel, outs, args):
    return pl.pallas_call(
        kernel,
        out_shape=[jax.ShapeDtypeStruct(shape, dtype) for shape, dtype in outs],
        in_specs=[pl.BlockSpec(memory_space=pltpu.VMEM)] * len(args),
        out_specs=[pl.BlockSpec(memory_space=pltpu.VMEM)] * len(outs),
        compiler_params=pltpu.CompilerParams(vmem_limit_bytes=VMEM_LIMIT),
    )(*args)


def step(kernel, section, arrived, fixed, read, kept):
    args = (section, arrived, *fixed, *read, *kept)
    outs = [arrived, *kept]
    first_kept = len(args) - len(kept)
    made = pl.pallas_call(
        kernel,
        out_shape=[jax.ShapeDtypeStruct(t.shape, t.dtype) for t in outs],
        in_specs=[pl.BlockSpec(memory_space=pltpu.SMEM)]
        + [pl.BlockSpec(memory_space=pltpu.VMEM)] * (len(args) - 1),
        out_specs=[pl.BlockSpec(memory_space=pltpu.VMEM)] * len(outs),
        input_output_aliases={first_kept + i: 1 + i for i in range(len(kept))},
        compiler_params=pltpu.CompilerParams(vmem_limit_bytes=VMEM_LIMIT),
    )(*args)
    return made[0], tuple(made[1:])


def z_route(replicas, distance):
    return [(i, (i + distance * X_CHIPS) % replicas) for i in range(replicas)]


def x_route(replicas, distance):
    return [
        (i, i // X_CHIPS * X_CHIPS + (i % X_CHIPS + distance) % X_CHIPS) for i in range(replicas)
    ]


def gather_weights(shard, replica, replicas):
    rows, columns = shard.shape
    z_count = replicas // X_CHIPS
    z, x = replica // X_CHIPS, replica % X_CHIPS
    along_z = functools.partial(z_route, replicas)
    along_x = functools.partial(x_route, replicas)
    qkv_width = QUERY_WIDTH + 2 * KEY_WIDTH
    half = rows // 2
    shapes = [
        (z_count, X_CHIPS, rows, qkv_width),
        (z_count, X_CHIPS, half, 2 * (columns - qkv_width)),
    ]
    at = jnp.stack([z, x]).astype(jnp.int32)
    placed = ()
    ahead = behind = shard
    fresh = [(0, shard)]
    sets = []

    def along(fresh):
        chunk = jnp.stack([data for _, data in fresh])
        right = lax.ppermute(chunk, "dp", along_x(1))
        left = lax.ppermute(chunk, "dp", along_x(-1))
        return tuple(offset for offset, _ in fresh), chunk, right, left

    def along_far(offsets, chunk, right, left):
        far_upper = lax.ppermute(right[:, :half], "dp", along_x(1))
        far_lower = lax.ppermute(left[:, half:], "dp", along_x(-1))
        sets.append((offsets, (chunk, right, left, far_upper, far_lower)))

    sent = None
    for step in range(1, z_count // 2 + 1):
        if step - 1 == CUTS[0] + 2:
            ahead, behind, *came = lax.optimization_barrier((ahead, behind, *sent[2:]))
            along_far(*sent[:2], *came)
        if step - 1 == CUTS[1] + 2:
            ahead, behind, *came = lax.optimization_barrier(
                (ahead, behind, *sent[2:], *sets[0][1][3:])
            )
            sets[0] = (sets[0][0], (*sets[0][1][:3], *came[2:]))
            along_far(*sent[:2], *came[:2])
        if step < z_count // 2:
            ahead = lax.ppermute(ahead, "dp", along_z(1))
            behind = lax.ppermute(behind, "dp", along_z(-1))
            fresh += [(-step, ahead), (step, behind)]
        else:
            upper = lax.ppermute(ahead[:half], "dp", along_z(1))
            lower = lax.ppermute(behind[half:], "dp", along_z(-1))
            upper, lower, *came = lax.optimization_barrier((upper, lower, *sets[1][1][3:]))
            sets[1] = (sets[1][0], (*sets[1][1][:3], *came))
            fresh.append((step, jnp.concatenate([upper, lower], axis=0)))
        if step in CUTS:
            sent = along(fresh)
            fresh = []
    along_far(*sent)
    late = sets[1][1][3]
    for offsets, pieces in sets:
        placed = place(offsets, at, pieces, placed, shapes)
    return (
        placed[0].reshape(replicas * rows, qkv_width),
        placed[1].reshape(replicas * half, 2 * (columns - qkv_width)),
        late,
    )


def sum_over_replicas(parts, replica, replicas):
    count, rows, columns = parts.shape
    x = replica % X_CHIPS
    low_bit, high_bit = x % 2, x // 2

    def swap(t, mask):
        return lax.ppermute(t, "dp", [(i, i ^ mask) for i in range(replicas)])

    def add(t, other):
        return (t.astype(F32) + other.astype(F32)).astype(BF16)

    def pick(t, axis, at):
        return lax.dynamic_index_in_dim(t, at, axis, keepdims=False)

    def join(own, other, bit, axis):
        return jnp.where(
            bit == 0, jnp.stack([own, other], axis=axis), jnp.stack([other, own], axis=axis)
        )

    total = parts.reshape(2, 2, rows, columns)
    total = add(pick(total, 1, low_bit), swap(pick(total, 1, 1 - low_bit), 1))
    total = add(pick(total, 0, high_bit), swap(pick(total, 0, 1 - high_bit), 2))
    mask = X_CHIPS
    while mask < replicas:
        total = add(total, swap(total, mask))
        mask *= 2
    total = join(total, swap(total, 2), high_bit, 0)
    total = join(total, swap(total, 1), low_bit, 1)
    whole = total.reshape(count, rows, columns).astype(F32)
    return whole.transpose(1, 0, 2).reshape(rows, count * columns)


def exchange_tokens(source_tokens, send_counts, replica, replicas, stream_count, late):
    slot_count = source_tokens.shape[0] // replicas
    features = source_tokens.shape[1]
    sent_counts = lax.dynamic_index_in_dim(send_counts, replica, 0, keepdims=False)
    send_start = jnp.cumsum(sent_counts) - sent_counts
    slot_ids = jnp.arange(slot_count, dtype=jnp.int32)
    occupied = slot_ids[None, :] < sent_counts[:, None]
    pick_rows = jnp.where(occupied, send_start[:, None] + slot_ids[None, :], -1).reshape(-1)
    own_rows = jnp.arange(source_tokens.shape[0], dtype=jnp.int32)
    choose = (pick_rows[:, None] == own_rows[None, :]).astype(BF16)
    packed = dot(choose, source_tokens).astype(BF16).reshape(replicas, slot_count, features)
    packed, _ = lax.optimization_barrier((packed, late))
    arrived = lax.all_to_all(packed, "dp", split_axis=0, concat_axis=0, tiled=True)
    incoming = lax.dynamic_index_in_dim(send_counts, replica, 1, keepdims=False)
    end_rows = jnp.cumsum(incoming)
    starts = end_rows - incoming
    places = jnp.arange(stream_count, dtype=jnp.int32)
    slot_place = starts[:, None] + slot_ids[None, :]
    slot_place = jnp.where(slot_ids[None, :] < incoming[:, None], slot_place, -1).reshape(-1)
    choose = (places[:, None] == slot_place[None, :]).astype(BF16)
    stream = dot(choose, arrived.reshape(replicas * slot_count, features)).astype(BF16)
    return stream, places < end_rows[replicas - 1]


def layout(segments, filled):
    micro_count, token_count = segments.shape
    tokens = micro_count * token_count
    segment = segments.reshape(tokens)
    places = jnp.arange(tokens, dtype=jnp.int32)
    sequence = places // token_count
    same = (segment[:, None] == segment[None, :]) & (sequence[:, None] == sequence[None, :])
    before = places[None, :] < places[:, None]
    position = jnp.sum(jnp.where(same & before, 1.0, 0.0).astype(F32), axis=1)
    alone = places[None, :] == places[:, None]
    allowed = (before & same & filled[:, None] & filled[None, :]) | alone
    half = HEAD_SIZE // 2
    frequency = ROPE_BASE ** (-2.0 * jnp.arange(half, dtype=F32) / HEAD_SIZE)
    angles = position[:, None] * frequency[None, :]
    cosine, sine = jnp.cos(angles), jnp.sin(angles)
    heads = LANES // HEAD_SIZE
    return (
        jnp.concatenate([cosine, cosine] * heads, axis=1),
        jnp.concatenate([-sine, sine] * heads, axis=1),
        allowed.astype(F32),
    )


def local(
    source_tokens,
    send_counts,
    doc_segments,
    out_cotangent,
    norm_gain,
    query_weight,
    frozen_key_matrix,
    frozen_value_matrix,
    out_weight,
    adapter_down,
    adapter_up_maps,
):
    replicas = lax.axis_size("dp")
    sections = lax.axis_size("section")
    replica = lax.axis_index("dp")
    section = lax.axis_index("section")
    features = source_tokens.shape[1]
    tokens = doc_segments.shape[0] * doc_segments.shape[1]

    half = out_weight.shape[2] // 2
    out_rows = jnp.concatenate([out_weight[0, :, :half], out_weight[0, :, half:]], axis=0)
    shard = jnp.concatenate(
        [query_weight[0], frozen_key_matrix[0], frozen_value_matrix[0], out_rows], axis=1
    )
    wqkv, wout, late = gather_weights(shard, replica, replicas)
    stream, filled = exchange_tokens(source_tokens, send_counts, replica, replicas, tokens, late)
    cosine, sine, allowed = layout(doc_segments, filled)
    gain = norm_gain[0].reshape(1, features)
    tables = jnp.stack([cosine, sine, allowed])
    down = adapter_down[0].transpose(0, 2, 1).reshape(2 * RANK, features)
    up = adapter_up_maps[0]
    up = jnp.concatenate(
        [
            jnp.pad(up[:, :QUERY_WIDTH], ((0, RANK), (0, 0))),
            jnp.pad(up[:, QUERY_WIDTH:], ((RANK, 0), (0, 0))),
        ],
        axis=1,
    )

    saved_shapes = [
        ((tokens, features), BF16),
        ((tokens, QUERY_WIDTH), BF16),
        ((tokens, KEY_WIDTH), BF16),
        ((tokens, KEY_WIDTH), BF16),
        ((tokens, QUERY_HEADS * tokens), BF16),
        ((tokens, 2 * RANK), BF16),
        ((tokens, features), BF16),
    ]
    fixed = (tables, gain, down, up, wqkv, wout)
    has_turn = section.astype(jnp.int32).reshape(1)
    x = stream
    saved = tuple(jnp.zeros(shape, dtype) for shape, dtype in saved_shapes)
    for turn in range(sections):
        last = turn + 1 == sections
        kernel = functools.partial(forward_kernel, turn, last)
        y, saved = step(kernel, has_turn, x, fixed, (), saved)
        if not last:
            x = lax.ppermute(y, "section", [(turn, turn + 1)])

    held, (low, normed) = saved[:5], saved[5:]
    c = out_cotangent
    kept = (
        jnp.zeros((tokens, QUERY_WIDTH), BF16),
        jnp.zeros((tokens, KEY_WIDTH), BF16),
        jnp.zeros((tokens, 2 * RANK), BF16),
    )
    for turn in range(sections - 1, -1, -1):
        kernel = functools.partial(backward_kernel, turn, turn == 0)
        back, kept = step(kernel, has_turn, c, fixed, held, kept)
        if turn > 0:
            c = lax.ppermute(back, "section", [(turn, turn - 1)])

    (grads,) = call(
        grads_kernel,
        [((X_CHIPS, 3 * RANK, features // X_CHIPS), BF16)],
        (normed, low, kept[0], kept[1], kept[2]),
    )
    grads = sum_over_replicas(grads, replica, replicas)
    down_grads = grads[: 2 * RANK].reshape(2, RANK, features).transpose(0, 2, 1)
    up_grads = grads[2 * RANK :, : QUERY_WIDTH + KEY_WIDTH]
    return (down_grads[None], up_grads[None])


def solution(mesh):
    placed = (
        P("dp", None),
        P(),
        P("dp", None),
        P("dp", None),
        P("section", None),
        P("section", "dp", None),
        P("section", "dp", None),
        P("section", "dp", None),
        P("section", "dp", None),
        P("section", None, None, None),
        P("section", None, None),
    )
    return jax.shard_map(
        local,
        mesh=mesh,
        in_specs=placed,
        out_specs=(P("section", None, None, None), P("section", None, None)),
        check_vma=False,
    )
```

```python
import functools

import jax
import jax.numpy as jnp
from jax import lax
from jax.experimental import pallas as pl
from jax.experimental.pallas import tpu as pltpu
from jax.sharding import PartitionSpec as P

QUERY_HEADS = 16
KEY_VALUE_HEADS = 4
GROUP = QUERY_HEADS // KEY_VALUE_HEADS
HEAD_SIZE = 64
QUERY_WIDTH = QUERY_HEADS * HEAD_SIZE
KEY_WIDTH = KEY_VALUE_HEADS * HEAD_SIZE
RANK = 16
LANES = 128

ROPE_BASE = 500000.0
ADAPTER_SCALE = 2.0
NORM_EPS = 1e-05
SCORE_SCALE = HEAD_SIZE ** (-0.5)

X_CHIPS = 4

F32 = jnp.float32
BF16 = jnp.bfloat16
VMEM_LIMIT = 32 * 1024 * 1024
LATE_ROUND = 3


def dot(a, b):
    return jnp.dot(a, b, preferred_element_type=F32)


def dot_nt(a, b):
    return lax.dot_general(a, b, (((1,), (1,)), ((), ())), preferred_element_type=F32)


def dot_tn(a, b):
    return lax.dot_general(a, b, (((0,), (0,)), ((), ())), preferred_element_type=F32)


def lanes_of(rows, width):
    return lax.broadcasted_iota(jnp.int32, (rows, width), 1)


def rope(t, cosine, signed_sine):
    rows, width = t.shape
    copies = width // LANES
    wide_cos = jnp.concatenate([cosine] * copies, axis=1)
    wide_sin = jnp.concatenate([signed_sine] * copies, axis=1)
    half = HEAD_SIZE // 2
    leading = (lanes_of(rows, width) % HEAD_SIZE) < half
    partner = jnp.where(leading, pltpu.roll(t, width - half, 1), pltpu.roll(t, half, 1))
    return t * wide_cos + partner * wide_sin


def expand(turned, head):
    rows, width = turned[0].shape
    block = lanes_of(rows, width) // HEAD_SIZE
    zero = jnp.zeros((), turned[0].dtype)
    parts = [
        jnp.where(block == g, turned[(g - head) % KEY_VALUE_HEADS], zero) for g in range(GROUP)
    ]
    return jnp.concatenate(parts, axis=0)


def turns_of(t):
    width = t.shape[1]
    wide = t.astype(F32)
    return [t] + [
        pltpu.roll(wide, j * HEAD_SIZE, 1).astype(t.dtype) for j in range(1, KEY_VALUE_HEADS)
    ]


def fold(products):
    rows = products[0].shape[0] // GROUP
    width = products[0].shape[1]
    block = lanes_of(rows, width) // HEAD_SIZE
    total = None
    for h, product in enumerate(products):
        diagonal = None
        for g in range(GROUP):
            part = jnp.where(block == g, product[g * rows : (g + 1) * rows], 0.0)
            diagonal = part if diagonal is None else diagonal + part
        pair = diagonal + pltpu.roll(diagonal, HEAD_SIZE, 1)
        whole = pair + pltpu.roll(pair, 2 * HEAD_SIZE, 1)
        kept = jnp.where(block == h, whole, 0.0)
        total = kept if total is None else total + kept
    return total


def load(copies):
    for copy in copies:
        copy.start()


def forward_kernel(turn, last, turn_ref, x_ref, *refs):
    fixed, y_ref, kept = refs[:6], refs[13], refs[14:21]

    @pl.when(turn_ref[0] == turn)
    def _():
        forward_step(last, x_ref, *fixed, y_ref, *kept)


def forward_step(
    last,
    x_ref, tables, gain, down, up, wqkv, wout,
    y_ref, kept_x_ref, q_ref, k_ref, v_ref, p_ref, low_ref, n_ref,
):
    width = GROUP * HEAD_SIZE
    head_at = [slice(h * width, (h + 1) * width) for h in range(KEY_VALUE_HEADS)]
    cosine, sine = tables[0], tables[1]
    allowed = tables[2] > 0.0
    x = x_ref[...]
    kept_x_ref[...] = x
    hidden = x.astype(F32)
    energy = jnp.mean(hidden * hidden, axis=-1, keepdims=True)
    n = (hidden * lax.rsqrt(energy + NORM_EPS) * gain[...]).astype(BF16)
    n_ref[...] = n
    low = dot_nt(n, down[...]).astype(BF16)
    low_ref[...] = low
    kv = dot(n, wqkv[:, QUERY_WIDTH:])
    k = rope(kv[:, :KEY_WIDTH], cosine, sine).astype(BF16)
    k_ref[...] = k
    v = kv[:, KEY_WIDTH:] + ADAPTER_SCALE * dot(low, up[:, QUERY_WIDTH:])
    v = v.astype(BF16)
    v_ref[...] = v
    k_turns, v_turns = turns_of(k), turns_of(v)
    tokens = hidden.shape[0]
    blended = []
    for h, at in enumerate(head_at):
        q = dot(n, wqkv[:, at]) + ADAPTER_SCALE * dot(low, up[:, at])
        q = rope(q, cosine, sine).astype(BF16)
        q_ref[:, at] = q
        scores = dot_nt(q, expand(k_turns, h)) * SCORE_SCALE
        shares = []
        for g in range(GROUP):
            weights = jnp.where(allowed, jnp.exp(scores[:, g * tokens : (g + 1) * tokens]), 0.0)
            shares.append((weights / jnp.sum(weights, axis=-1, keepdims=True)).astype(BF16))
        shares = jnp.concatenate(shares, axis=1)
        p_ref[:, h * GROUP * tokens : (h + 1) * GROUP * tokens] = shares
        if not last:
            blended.append(dot(shares, expand(v_turns, h)).astype(BF16))
    if not last:
        y_ref[...] = (hidden + dot(jnp.concatenate(blended, axis=1), wout[...])).astype(BF16)


def backward_kernel(turn, first, turn_ref, c_ref, *refs):
    out_ref, kept = refs[-4], refs[-3:]

    @pl.when(turn_ref[0] == turn)
    def _():
        if first:
            tables, up, wout, k_ref, v_ref, p_ref = refs[:6]
            fixed, held = (tables, None, None, up, None, wout), (None, None, k_ref, v_ref, p_ref)
        else:
            fixed, held = refs[:6], refs[6:11]
        backward_step(first, c_ref, *fixed, *held, out_ref, *kept)


def backward_step(
    first,
    c_ref, tables, gain, down, up, wqkv, wout,
    x_ref, q_ref, k_ref, v_ref, p_ref,
    out_ref, dq_ref, dv_ref, dlow_ref,
):
    width = GROUP * HEAD_SIZE
    head_at = [slice(h * width, (h + 1) * width) for h in range(KEY_VALUE_HEADS)]
    cosine, sine = tables[0], tables[1]
    k_turns, v_turns = turns_of(k_ref[...]), turns_of(v_ref[...])
    c = c_ref[...]
    tokens = c.shape[0]
    dn = None
    dlow = None
    dk_products, dv_products = [], []
    for h, at in enumerate(head_at):
        dblended = dot_nt(c, wout[at, :]).astype(BF16)
        shares = p_ref[:, h * GROUP * tokens : (h + 1) * GROUP * tokens]
        dshares = dot_nt(dblended, expand(v_turns, h))
        dscores = []
        for g in range(GROUP):
            span = slice(g * tokens, (g + 1) * tokens)
            p = shares[:, span].astype(F32)
            dp = dshares[:, span]
            pdp = p * dp
            dscores.append(
                ((pdp - p * jnp.sum(pdp, axis=-1, keepdims=True)) * SCORE_SCALE).astype(BF16)
            )
        dscores = jnp.concatenate(dscores, axis=1)
        dq = dot(dscores, expand(k_turns, h))
        dq = rope(dq, cosine, -sine).astype(BF16)
        dq_ref[:, at] = dq
        part = dot_nt(dq, up[:, at])
        dlow = part if dlow is None else dlow + part
        dv_products.append(dot_tn(shares, dblended))
        if not first:
            dk_products.append(dot_tn(dscores, q_ref[:, at]))
            part = dot_nt(dq, wqkv[:, at])
            dn = part if dn is None else dn + part
    dv = fold(dv_products).astype(BF16)
    dv_ref[...] = dv
    dlow = (ADAPTER_SCALE * (dlow + dot_nt(dv, up[:, QUERY_WIDTH:]))).astype(BF16)
    dlow_ref[...] = dlow
    if first:
        return
    dk = rope(fold(dk_products), cosine, -sine).astype(BF16)
    dn = dn + dot_nt(jnp.concatenate([dk, dv], axis=1), wqkv[:, QUERY_WIDTH:])
    dn = dn + dot(dlow, down[...])
    hidden = x_ref[...].astype(F32)
    energy = jnp.mean(hidden * hidden, axis=-1, keepdims=True)
    scale = lax.rsqrt(energy + NORM_EPS)
    dy = dn * gain[...]
    along = jnp.mean(hidden * dy, axis=-1, keepdims=True)
    dh = scale * dy - hidden * (scale * scale * scale * along)
    out_ref[...] = (c.astype(F32) + dh).astype(BF16)


def grads_kernel(n_ref, low_ref, dq_ref, dv_ref, dlow_ref, g_ref):
    part = g_ref.shape[2]
    down = dot_tn(dlow_ref[...], n_ref[...]).astype(BF16)
    low = low_ref[...]
    up_q = ADAPTER_SCALE * dot_tn(low, dq_ref[...])[:RANK]
    up_v = ADAPTER_SCALE * dot_tn(low, dv_ref[...])[RANK : 2 * RANK]
    spare = jnp.zeros((RANK, g_ref.shape[0] * part - QUERY_WIDTH - KEY_WIDTH), F32)
    up = jnp.concatenate([up_q, up_v, spare], axis=1).astype(BF16)
    for i in range(g_ref.shape[0]):
        at = slice(i * part, (i + 1) * part)
        g_ref[i, 0 : 2 * RANK, :] = down[:, at]
        g_ref[i, 2 * RANK : 3 * RANK, :] = up[:, at]


def place_kernel(offsets, at_ref, *refs):
    qkv, out, sems = refs[-3:]
    z_count, _, rows, qkv_width = qkv.shape
    half, width = rows // 2, out.shape[3] // 2
    rest = pl.ds(qkv_width, width)
    ends = []
    for piece, offset in zip(refs, offsets):
        z_at = lax.rem(at_ref[0] + (offset + z_count), z_count)
        ends += [
            (piece.at[:, :, pl.ds(0, qkv_width)], qkv.at[z_at]),
            (piece.at[:, pl.ds(0, half), rest], out.at[z_at, :, :, pl.ds(0, width)]),
            (piece.at[:, pl.ds(half, half), rest], out.at[z_at, :, :, pl.ds(width, width)]),
        ]
    copies = [pltpu.make_async_copy(a, b, sems.at[i]) for i, (a, b) in enumerate(ends)]
    for copy in copies:
        copy.start()
    for copy in copies:
        copy.wait()


def place(offsets, z, pieces):
    x_count, rows, columns = pieces[0].shape
    qkv_width = QUERY_WIDTH + 2 * KEY_WIDTH
    z_count, out_width = len(pieces), 2 * (columns - qkv_width)
    shapes = [(z_count, x_count, rows, qkv_width), (z_count, x_count, rows // 2, out_width)]
    wqkv, wout = pl.pallas_call(
        functools.partial(place_kernel, offsets),
        out_shape=[jax.ShapeDtypeStruct(shape, BF16) for shape in shapes],
        in_specs=[pl.BlockSpec(memory_space=pltpu.SMEM)]
        + [pl.BlockSpec(memory_space=pl.ANY)] * len(pieces),
        out_specs=[pl.BlockSpec(memory_space=pltpu.VMEM)] * len(shapes),
        scratch_shapes=[pltpu.SemaphoreType.DMA((3 * len(offsets),))],
        compiler_params=pltpu.CompilerParams(vmem_limit_bytes=VMEM_LIMIT),
    )(z.astype(jnp.int32).reshape(1), *pieces)
    all_rows = z_count * x_count * rows
    return wqkv.reshape(all_rows, qkv_width), wout.reshape(all_rows // 2, out_width)


def call(kernel, outs, args):
    return pl.pallas_call(
        kernel,
        out_shape=[jax.ShapeDtypeStruct(shape, dtype) for shape, dtype in outs],
        in_specs=[pl.BlockSpec(memory_space=pltpu.VMEM)] * len(args),
        out_specs=[pl.BlockSpec(memory_space=pltpu.VMEM)] * len(outs),
        compiler_params=pltpu.CompilerParams(vmem_limit_bytes=VMEM_LIMIT),
    )(*args)


def step(kernel, section, arrived, fixed, read, kept):
    args = (section, arrived, *fixed, *read, *kept)
    outs = [arrived, *kept]
    first_kept = len(args) - len(kept)
    made = pl.pallas_call(
        kernel,
        out_shape=[jax.ShapeDtypeStruct(t.shape, t.dtype) for t in outs],
        in_specs=[pl.BlockSpec(memory_space=pltpu.SMEM)]
        + [pl.BlockSpec(memory_space=pltpu.VMEM)] * (len(args) - 1),
        out_specs=[pl.BlockSpec(memory_space=pltpu.VMEM)] * len(outs),
        input_output_aliases={first_kept + i: 1 + i for i in range(len(kept))},
        compiler_params=pltpu.CompilerParams(vmem_limit_bytes=VMEM_LIMIT),
    )(*args)
    return made[0], tuple(made[1:])


def z_route(replicas, distance):
    return [(i, (i + distance * X_CHIPS) % replicas) for i in range(replicas)]


def x_route(replicas, distance):
    return [
        (i, i // X_CHIPS * X_CHIPS + (i % X_CHIPS + distance) % X_CHIPS) for i in range(replicas)
    ]


def gather_shards(shard, replica, replicas):
    rows, columns = shard.shape
    z_count = replicas // X_CHIPS
    x = replica % X_CHIPS
    along_z = functools.partial(z_route, replicas)
    along_x = functools.partial(x_route, replicas)
    half = rows // 2
    right = lax.ppermute(shard, "dp", along_x(1))
    left = lax.ppermute(shard, "dp", along_x(-1))
    far_upper = lax.ppermute(right[:half], "dp", along_x(1))
    far_lower = lax.ppermute(left[half:], "dp", along_x(-1))
    far = jnp.concatenate([far_upper, far_lower], axis=0)
    line = jnp.zeros((X_CHIPS, rows, columns), shard.dtype)
    for turn, data in ((0, shard), (-1, right), (1, left), (2, far)):
        line = lax.dynamic_update_slice(line, data[None], ((x + turn) % X_CHIPS, 0, 0))
    ahead = behind = line
    pieces = [(0, line)]
    late = None
    middle = X_CHIPS // 2
    for step in range(1, z_count // 2):
        ahead = lax.ppermute(ahead, "dp", along_z(1))
        behind = lax.ppermute(behind, "dp", along_z(-1))
        pieces += [(-step, ahead), (step, behind)]
        if step == LATE_ROUND:
            late = ahead
    upper = lax.ppermute(ahead[:middle], "dp", along_z(1))
    lower = lax.ppermute(behind[middle:], "dp", along_z(-1))
    pieces.append((z_count // 2, jnp.concatenate([upper, lower], axis=0)))
    return pieces, late


def sum_over_replicas(parts, replica, replicas):
    count, rows, columns = parts.shape
    x = replica % X_CHIPS
    low_bit, high_bit = x % 2, x // 2

    def swap(t, mask):
        return lax.ppermute(t, "dp", [(i, i ^ mask) for i in range(replicas)])

    def add(t, other):
        return (t.astype(F32) + other.astype(F32)).astype(BF16)

    def pick(t, axis, at):
        return lax.dynamic_index_in_dim(t, at, axis, keepdims=False)

    def join(own, other, bit, axis):
        return jnp.where(
            bit == 0, jnp.stack([own, other], axis=axis), jnp.stack([other, own], axis=axis)
        )

    total = parts.reshape(2, 2, rows, columns)
    total = add(pick(total, 1, low_bit), swap(pick(total, 1, 1 - low_bit), 1))
    total = add(pick(total, 0, high_bit), swap(pick(total, 0, 1 - high_bit), 2))
    mask = X_CHIPS
    while mask < replicas:
        total = add(total, swap(total, mask))
        mask *= 2
    total = join(total, swap(total, 2), high_bit, 0)
    total = join(total, swap(total, 1), low_bit, 1)
    whole = total.reshape(count, rows, columns).astype(F32)
    return whole.transpose(1, 0, 2).reshape(rows, count * columns)


def exchange_tokens(source_tokens, send_counts, replica, replicas, stream_count, late):
    slot_count = source_tokens.shape[0] // replicas
    features = source_tokens.shape[1]
    sent_counts = lax.dynamic_index_in_dim(send_counts, replica, 0, keepdims=False)
    send_start = jnp.cumsum(sent_counts) - sent_counts
    slot_ids = jnp.arange(slot_count, dtype=jnp.int32)
    occupied = slot_ids[None, :] < sent_counts[:, None]
    pick_rows = jnp.where(occupied, send_start[:, None] + slot_ids[None, :], -1).reshape(-1)
    own_rows = jnp.arange(source_tokens.shape[0], dtype=jnp.int32)
    choose = (pick_rows[:, None] == own_rows[None, :]).astype(BF16)
    packed = dot(choose, source_tokens).astype(BF16).reshape(replicas, slot_count, features)
    packed, _ = lax.optimization_barrier((packed, late))
    arrived = lax.all_to_all(packed, "dp", split_axis=0, concat_axis=0, tiled=True)
    incoming = lax.dynamic_index_in_dim(send_counts, replica, 1, keepdims=False)
    end_rows = jnp.cumsum(incoming)
    starts = end_rows - incoming
    places = jnp.arange(stream_count, dtype=jnp.int32)
    slot_place = starts[:, None] + slot_ids[None, :]
    slot_place = jnp.where(slot_ids[None, :] < incoming[:, None], slot_place, -1).reshape(-1)
    choose = (places[:, None] == slot_place[None, :]).astype(BF16)
    stream = dot(choose, arrived.reshape(replicas * slot_count, features)).astype(BF16)
    return stream, places < end_rows[replicas - 1]


def layout(segments, filled):
    micro_count, token_count = segments.shape
    tokens = micro_count * token_count
    segment = segments.reshape(tokens)
    places = jnp.arange(tokens, dtype=jnp.int32)
    sequence = places // token_count
    same = (segment[:, None] == segment[None, :]) & (sequence[:, None] == sequence[None, :])
    before = places[None, :] < places[:, None]
    position = jnp.sum(jnp.where(same & before, 1.0, 0.0).astype(F32), axis=1)
    alone = places[None, :] == places[:, None]
    allowed = (before & same & filled[:, None] & filled[None, :]) | alone
    half = HEAD_SIZE // 2
    frequency = ROPE_BASE ** (-2.0 * jnp.arange(half, dtype=F32) / HEAD_SIZE)
    angles = position[:, None] * frequency[None, :]
    cosine, sine = jnp.cos(angles), jnp.sin(angles)
    heads = LANES // HEAD_SIZE
    return (
        jnp.concatenate([cosine, cosine] * heads, axis=1),
        jnp.concatenate([-sine, sine] * heads, axis=1),
        allowed.astype(F32),
    )


def local(
    source_tokens,
    send_counts,
    doc_segments,
    out_cotangent,
    norm_gain,
    query_weight,
    frozen_key_matrix,
    frozen_value_matrix,
    out_weight,
    adapter_down,
    adapter_up_maps,
):
    replicas = lax.axis_size("dp")
    sections = lax.axis_size("section")
    replica = lax.axis_index("dp")
    section = lax.axis_index("section")
    features = source_tokens.shape[1]
    tokens = doc_segments.shape[0] * doc_segments.shape[1]

    half = out_weight.shape[2] // 2
    out_rows = jnp.concatenate([out_weight[0, :, :half], out_weight[0, :, half:]], axis=0)
    shard = jnp.concatenate(
        [query_weight[0], frozen_key_matrix[0], frozen_value_matrix[0], out_rows], axis=1
    )
    shards, late = gather_shards(shard, replica, replicas)
    stream, filled = exchange_tokens(source_tokens, send_counts, replica, replicas, tokens, late)
    cosine, sine, allowed = layout(doc_segments, filled)
    gain = norm_gain[0].reshape(1, features)
    tables = jnp.stack([cosine, sine, allowed])
    down = adapter_down[0].transpose(0, 2, 1).reshape(2 * RANK, features)
    up = adapter_up_maps[0]
    up = jnp.concatenate(
        [
            jnp.pad(up[:, :QUERY_WIDTH], ((0, RANK), (0, 0))),
            jnp.pad(up[:, QUERY_WIDTH:], ((RANK, 0), (0, 0))),
        ],
        axis=1,
    )

    saved_shapes = [
        ((tokens, features), BF16),
        ((tokens, QUERY_WIDTH), BF16),
        ((tokens, KEY_WIDTH), BF16),
        ((tokens, KEY_WIDTH), BF16),
        ((tokens, QUERY_HEADS * tokens), BF16),
        ((tokens, 2 * RANK), BF16),
        ((tokens, features), BF16),
    ]
    stream, tables, gain, down, up, *pieces = lax.optimization_barrier(
        (stream, tables, gain, down, up, *[data for _, data in shards])
    )
    wqkv, wout = place([offset for offset, _ in shards], replica // X_CHIPS, pieces)
    fixed = (tables, gain, down, up, wqkv, wout)
    has_turn = section.astype(jnp.int32).reshape(1)
    x = stream
    saved = tuple(jnp.zeros(shape, dtype) for shape, dtype in saved_shapes)
    for turn in range(sections):
        last = turn + 1 == sections
        kernel = functools.partial(forward_kernel, turn, last)
        y, saved = step(kernel, has_turn, x, fixed, (), saved)
        if not last:
            x = lax.ppermute(y, "section", [(turn, turn + 1)])

    held, (low, normed) = saved[:5], saved[5:]
    c = out_cotangent
    kept = (
        jnp.zeros((tokens, QUERY_WIDTH), BF16),
        jnp.zeros((tokens, KEY_WIDTH), BF16),
        jnp.zeros((tokens, 2 * RANK), BF16),
    )
    for turn in range(sections - 1, -1, -1):
        kernel = functools.partial(backward_kernel, turn, turn == 0)
        if turn > 0:
            back, kept = step(kernel, has_turn, c, fixed, held, kept)
        else:
            back, kept = step(kernel, has_turn, c, (tables, up, wout), held[2:], kept)
        if turn > 0:
            c = lax.ppermute(back, "section", [(turn, turn - 1)])

    (grads,) = call(
        grads_kernel,
        [((X_CHIPS, 3 * RANK, features // X_CHIPS), BF16)],
        (normed, low, kept[0], kept[1], kept[2]),
    )
    grads = sum_over_replicas(grads, replica, replicas)
    down_grads = grads[: 2 * RANK].reshape(2, RANK, features).transpose(0, 2, 1)
    up_grads = grads[2 * RANK :, : QUERY_WIDTH + KEY_WIDTH]
    return (down_grads[None], up_grads[None])


def solution(mesh):
    placed = (
        P("dp", None),
        P(),
        P("dp", None),
        P("dp", None),
        P("section", None),
        P("section", "dp", None),
        P("section", "dp", None),
        P("section", "dp", None),
        P("section", "dp", None),
        P("section", None, None, None),
        P("section", None, None),
    )
    return jax.shard_map(
        local,
        mesh=mesh,
        in_specs=placed,
        out_specs=(P("section", None, None, None), P("section", None, None)),
        check_vma=False,
    )
```

```python
import functools

import jax
import jax.numpy as jnp
from jax import lax
from jax.experimental import pallas as pl
from jax.experimental.pallas import tpu as pltpu
from jax.sharding import PartitionSpec as P

QUERY_HEADS = 16
KEY_VALUE_HEADS = 4
GROUP = QUERY_HEADS // KEY_VALUE_HEADS
HEAD_SIZE = 64
QUERY_WIDTH = QUERY_HEADS * HEAD_SIZE
KEY_WIDTH = KEY_VALUE_HEADS * HEAD_SIZE
RANK = 16
LANES = 128

ROPE_BASE = 500000.0
ADAPTER_SCALE = 2.0
NORM_EPS = 1e-05
SCORE_SCALE = HEAD_SIZE ** (-0.5)

X_CHIPS = 4

F32 = jnp.float32
BF16 = jnp.bfloat16
VMEM_LIMIT = 32 * 1024 * 1024
LATE_ROUND = 2


def dot(a, b):
    return jnp.dot(a, b, preferred_element_type=F32)


def dot_nt(a, b):
    return lax.dot_general(a, b, (((1,), (1,)), ((), ())), preferred_element_type=F32)


def dot_tn(a, b):
    return lax.dot_general(a, b, (((0,), (0,)), ((), ())), preferred_element_type=F32)


def lanes_of(rows, width):
    return lax.broadcasted_iota(jnp.int32, (rows, width), 1)


def rope(t, cosine, signed_sine):
    rows, width = t.shape
    copies = width // LANES
    wide_cos = jnp.concatenate([cosine] * copies, axis=1)
    wide_sin = jnp.concatenate([signed_sine] * copies, axis=1)
    half = HEAD_SIZE // 2
    leading = (lanes_of(rows, width) % HEAD_SIZE) < half
    partner = jnp.where(leading, pltpu.roll(t, width - half, 1), pltpu.roll(t, half, 1))
    return t * wide_cos + partner * wide_sin


def expand(turned, head):
    rows, width = turned[0].shape
    block = lanes_of(rows, width) // HEAD_SIZE
    zero = jnp.zeros((), turned[0].dtype)
    parts = [
        jnp.where(block == g, turned[(g - head) % KEY_VALUE_HEADS], zero) for g in range(GROUP)
    ]
    return jnp.concatenate(parts, axis=0)


def turns_of(t):
    width = t.shape[1]
    wide = t.astype(F32)
    return [t] + [
        pltpu.roll(wide, j * HEAD_SIZE, 1).astype(t.dtype) for j in range(1, KEY_VALUE_HEADS)
    ]


def fold(products):
    rows = products[0].shape[0] // GROUP
    width = products[0].shape[1]
    block = lanes_of(rows, width) // HEAD_SIZE
    total = None
    for h, product in enumerate(products):
        diagonal = None
        for g in range(GROUP):
            part = jnp.where(block == g, product[g * rows : (g + 1) * rows], 0.0)
            diagonal = part if diagonal is None else diagonal + part
        pair = diagonal + pltpu.roll(diagonal, HEAD_SIZE, 1)
        whole = pair + pltpu.roll(pair, 2 * HEAD_SIZE, 1)
        kept = jnp.where(block == h, whole, 0.0)
        total = kept if total is None else total + kept
    return total


def load(copies):
    for copy in copies:
        copy.start()


def forward_kernel(turn, last, turn_ref, x_ref, *refs):
    fixed, y_ref, kept = refs[:6], refs[13], refs[14:21]

    @pl.when(turn_ref[0] == turn)
    def _():
        forward_step(last, x_ref, *fixed, y_ref, *kept)


def forward_step(
    last,
    x_ref, tables, gain, down, up, wqkv, wout,
    y_ref, kept_x_ref, q_ref, k_ref, v_ref, p_ref, low_ref, n_ref,
):
    width = GROUP * HEAD_SIZE
    head_at = [slice(h * width, (h + 1) * width) for h in range(KEY_VALUE_HEADS)]
    cosine, sine = tables[0], tables[1]
    allowed = tables[2] > 0.0
    x = x_ref[...]
    kept_x_ref[...] = x
    hidden = x.astype(F32)
    energy = jnp.mean(hidden * hidden, axis=-1, keepdims=True)
    n = (hidden * lax.rsqrt(energy + NORM_EPS) * gain[...]).astype(BF16)
    n_ref[...] = n
    low = dot_nt(n, down[...]).astype(BF16)
    low_ref[...] = low
    kv = dot(n, wqkv[:, QUERY_WIDTH:])
    k = rope(kv[:, :KEY_WIDTH], cosine, sine).astype(BF16)
    k_ref[...] = k
    v = kv[:, KEY_WIDTH:] + ADAPTER_SCALE * dot(low, up[:, QUERY_WIDTH:])
    v = v.astype(BF16)
    v_ref[...] = v
    k_turns, v_turns = turns_of(k), turns_of(v)
    tokens = hidden.shape[0]
    blended = []
    for h, at in enumerate(head_at):
        q = dot(n, wqkv[:, at]) + ADAPTER_SCALE * dot(low, up[:, at])
        q = rope(q, cosine, sine).astype(BF16)
        q_ref[:, at] = q
        scores = dot_nt(q, expand(k_turns, h)) * SCORE_SCALE
        shares = []
        for g in range(GROUP):
            weights = jnp.where(allowed, jnp.exp(scores[:, g * tokens : (g + 1) * tokens]), 0.0)
            shares.append((weights / jnp.sum(weights, axis=-1, keepdims=True)).astype(BF16))
        shares = jnp.concatenate(shares, axis=1)
        p_ref[:, h * GROUP * tokens : (h + 1) * GROUP * tokens] = shares
        if not last:
            blended.append(dot(shares, expand(v_turns, h)).astype(BF16))
    if not last:
        y_ref[...] = (hidden + dot(jnp.concatenate(blended, axis=1), wout[...])).astype(BF16)


def backward_kernel(turn, first, turn_ref, c_ref, *refs):
    out_ref, kept = refs[-4], refs[-3:]

    @pl.when(turn_ref[0] == turn)
    def _():
        if first:
            tables, up, wout, k_ref, v_ref, p_ref = refs[:6]
            fixed, held = (tables, None, None, up, None, wout), (None, None, k_ref, v_ref, p_ref)
        else:
            fixed, held = refs[:6], refs[6:11]
        backward_step(first, c_ref, *fixed, *held, out_ref, *kept)


def backward_step(
    first,
    c_ref, tables, gain, down, up, wqkv, wout,
    x_ref, q_ref, k_ref, v_ref, p_ref,
    out_ref, dq_ref, dv_ref, dlow_ref,
):
    width = GROUP * HEAD_SIZE
    head_at = [slice(h * width, (h + 1) * width) for h in range(KEY_VALUE_HEADS)]
    cosine, sine = tables[0], tables[1]
    k_turns, v_turns = turns_of(k_ref[...]), turns_of(v_ref[...])
    c = c_ref[...]
    tokens = c.shape[0]
    dn = None
    dlow = None
    dk_products, dv_products = [], []
    for h, at in enumerate(head_at):
        dblended = dot_nt(c, wout[at, :]).astype(BF16)
        shares = p_ref[:, h * GROUP * tokens : (h + 1) * GROUP * tokens]
        dshares = dot_nt(dblended, expand(v_turns, h))
        dscores = []
        for g in range(GROUP):
            span = slice(g * tokens, (g + 1) * tokens)
            p = shares[:, span].astype(F32)
            dp = dshares[:, span]
            pdp = p * dp
            dscores.append(
                ((pdp - p * jnp.sum(pdp, axis=-1, keepdims=True)) * SCORE_SCALE).astype(BF16)
            )
        dscores = jnp.concatenate(dscores, axis=1)
        dq = dot(dscores, expand(k_turns, h))
        dq = rope(dq, cosine, -sine).astype(BF16)
        dq_ref[:, at] = dq
        part = dot_nt(dq, up[:, at])
        dlow = part if dlow is None else dlow + part
        dv_products.append(dot_tn(shares, dblended))
        if not first:
            dk_products.append(dot_tn(dscores, q_ref[:, at]))
            part = dot_nt(dq, wqkv[:, at])
            dn = part if dn is None else dn + part
    dv = fold(dv_products).astype(BF16)
    dv_ref[...] = dv
    dlow = (ADAPTER_SCALE * (dlow + dot_nt(dv, up[:, QUERY_WIDTH:]))).astype(BF16)
    dlow_ref[...] = dlow
    if first:
        return
    dk = rope(fold(dk_products), cosine, -sine).astype(BF16)
    dn = dn + dot_nt(jnp.concatenate([dk, dv], axis=1), wqkv[:, QUERY_WIDTH:])
    dn = dn + dot(dlow, down[...])
    hidden = x_ref[...].astype(F32)
    energy = jnp.mean(hidden * hidden, axis=-1, keepdims=True)
    scale = lax.rsqrt(energy + NORM_EPS)
    dy = dn * gain[...]
    along = jnp.mean(hidden * dy, axis=-1, keepdims=True)
    dh = scale * dy - hidden * (scale * scale * scale * along)
    out_ref[...] = (c.astype(F32) + dh).astype(BF16)


def grads_kernel(n_ref, low_ref, dq_ref, dv_ref, dlow_ref, g_ref):
    part = g_ref.shape[2]
    down = dot_tn(dlow_ref[...], n_ref[...]).astype(BF16)
    low = low_ref[...]
    up_q = ADAPTER_SCALE * dot_tn(low, dq_ref[...])[:RANK]
    up_v = ADAPTER_SCALE * dot_tn(low, dv_ref[...])[RANK : 2 * RANK]
    spare = jnp.zeros((RANK, g_ref.shape[0] * part - QUERY_WIDTH - KEY_WIDTH), F32)
    up = jnp.concatenate([up_q, up_v, spare], axis=1).astype(BF16)
    for i in range(g_ref.shape[0]):
        at = slice(i * part, (i + 1) * part)
        g_ref[i, 0 : 2 * RANK, :] = down[:, at]
        g_ref[i, 2 * RANK : 3 * RANK, :] = up[:, at]


def place_kernel(offsets, at_ref, *refs):
    qkv, out, sems = refs[-3:]
    z_count, _, rows, qkv_width = qkv.shape
    half, width = rows // 2, out.shape[3] // 2
    rest = pl.ds(qkv_width, width)
    ends = []
    for piece, offset in zip(refs, offsets):
        z_at = lax.rem(at_ref[0] + (offset + z_count), z_count)
        ends += [
            (piece.at[:, :, pl.ds(0, qkv_width)], qkv.at[z_at]),
            (piece.at[:, pl.ds(0, half), rest], out.at[z_at, :, :, pl.ds(0, width)]),
            (piece.at[:, pl.ds(half, half), rest], out.at[z_at, :, :, pl.ds(width, width)]),
        ]
    copies = [pltpu.make_async_copy(a, b, sems.at[i]) for i, (a, b) in enumerate(ends)]
    for copy in copies:
        copy.start()
    for copy in copies:
        copy.wait()


def place(offsets, z, pieces):
    x_count, rows, columns = pieces[0].shape
    qkv_width = QUERY_WIDTH + 2 * KEY_WIDTH
    z_count, out_width = len(pieces), 2 * (columns - qkv_width)
    shapes = [(z_count, x_count, rows, qkv_width), (z_count, x_count, rows // 2, out_width)]
    wqkv, wout = pl.pallas_call(
        functools.partial(place_kernel, offsets),
        out_shape=[jax.ShapeDtypeStruct(shape, BF16) for shape in shapes],
        in_specs=[pl.BlockSpec(memory_space=pltpu.SMEM)]
        + [pl.BlockSpec(memory_space=pl.ANY)] * len(pieces),
        out_specs=[pl.BlockSpec(memory_space=pltpu.VMEM)] * len(shapes),
        scratch_shapes=[pltpu.SemaphoreType.DMA((3 * len(offsets),))],
        compiler_params=pltpu.CompilerParams(vmem_limit_bytes=VMEM_LIMIT),
    )(z.astype(jnp.int32).reshape(1), *pieces)
    all_rows = z_count * x_count * rows
    return wqkv.reshape(all_rows, qkv_width), wout.reshape(all_rows // 2, out_width)


def call(kernel, outs, args):
    return pl.pallas_call(
        kernel,
        out_shape=[jax.ShapeDtypeStruct(shape, dtype) for shape, dtype in outs],
        in_specs=[pl.BlockSpec(memory_space=pltpu.VMEM)] * len(args),
        out_specs=[pl.BlockSpec(memory_space=pltpu.VMEM)] * len(outs),
        compiler_params=pltpu.CompilerParams(vmem_limit_bytes=VMEM_LIMIT),
    )(*args)


def step(kernel, section, arrived, fixed, read, kept):
    args = (section, arrived, *fixed, *read, *kept)
    outs = [arrived, *kept]
    first_kept = len(args) - len(kept)
    made = pl.pallas_call(
        kernel,
        out_shape=[jax.ShapeDtypeStruct(t.shape, t.dtype) for t in outs],
        in_specs=[pl.BlockSpec(memory_space=pltpu.SMEM)]
        + [pl.BlockSpec(memory_space=pltpu.VMEM)] * (len(args) - 1),
        out_specs=[pl.BlockSpec(memory_space=pltpu.VMEM)] * len(outs),
        input_output_aliases={first_kept + i: 1 + i for i in range(len(kept))},
        compiler_params=pltpu.CompilerParams(vmem_limit_bytes=VMEM_LIMIT),
    )(*args)
    return made[0], tuple(made[1:])


def z_route(replicas, distance):
    return [(i, (i + distance * X_CHIPS) % replicas) for i in range(replicas)]


def x_route(replicas, distance):
    return [
        (i, i // X_CHIPS * X_CHIPS + (i % X_CHIPS + distance) % X_CHIPS) for i in range(replicas)
    ]


def gather_shards(shard, replica, replicas):
    rows, columns = shard.shape
    z_count = replicas // X_CHIPS
    x = replica % X_CHIPS
    along_z = functools.partial(z_route, replicas)
    along_x = functools.partial(x_route, replicas)
    half = rows // 2
    right = lax.ppermute(shard, "dp", along_x(1))
    left = lax.ppermute(shard, "dp", along_x(-1))
    far_upper = lax.ppermute(right[:half], "dp", along_x(1))
    far_lower = lax.ppermute(left[half:], "dp", along_x(-1))
    far = jnp.concatenate([far_upper, far_lower], axis=0)
    line = jnp.zeros((X_CHIPS, rows, columns), shard.dtype)
    for turn, data in ((0, shard), (-1, right), (1, left), (2, far)):
        line = lax.dynamic_update_slice(line, data[None], ((x + turn) % X_CHIPS, 0, 0))
    ahead = behind = line
    pieces = [(0, line)]
    late = None
    middle = X_CHIPS // 2
    for step in range(1, z_count // 2):
        ahead = lax.ppermute(ahead, "dp", along_z(1))
        behind = lax.ppermute(behind, "dp", along_z(-1))
        pieces += [(-step, ahead), (step, behind)]
        if step == LATE_ROUND:
            late = ahead
    upper = lax.ppermute(ahead[:middle], "dp", along_z(1))
    lower = lax.ppermute(behind[middle:], "dp", along_z(-1))
    pieces.append((z_count // 2, jnp.concatenate([upper, lower], axis=0)))
    return pieces, late


def sum_over_replicas(parts, replica, replicas):
    count, rows, columns = parts.shape
    x = replica % X_CHIPS
    low_bit, high_bit = x % 2, x // 2

    def swap(t, mask):
        return lax.ppermute(t, "dp", [(i, i ^ mask) for i in range(replicas)])

    def add(t, other):
        return (t.astype(F32) + other.astype(F32)).astype(BF16)

    def pick(t, axis, at):
        return lax.dynamic_index_in_dim(t, at, axis, keepdims=False)

    def join(own, other, bit, axis):
        return jnp.where(
            bit == 0, jnp.stack([own, other], axis=axis), jnp.stack([other, own], axis=axis)
        )

    total = parts.reshape(2, 2, rows, columns)
    total = add(pick(total, 1, low_bit), swap(pick(total, 1, 1 - low_bit), 1))
    total = add(pick(total, 0, high_bit), swap(pick(total, 0, 1 - high_bit), 2))
    mask = X_CHIPS
    while mask < replicas:
        total = add(total, swap(total, mask))
        mask *= 2
    total = join(total, swap(total, 2), high_bit, 0)
    total = join(total, swap(total, 1), low_bit, 1)
    whole = total.reshape(count, rows, columns).astype(F32)
    return whole.transpose(1, 0, 2).reshape(rows, count * columns)


def exchange_tokens(source_tokens, send_counts, replica, replicas, section, sections, stream_count, late):
    slot_count = source_tokens.shape[0] // replicas
    width = source_tokens.shape[1] // sections
    share = lax.dynamic_slice_in_dim(source_tokens, section * width, width, 1)
    share, _ = lax.optimization_barrier((share, late))
    sent_counts = lax.dynamic_index_in_dim(send_counts, replica, 0, keepdims=False)
    send_start = jnp.cumsum(sent_counts) - sent_counts
    slot_ids = jnp.arange(slot_count, dtype=jnp.int32)
    occupied = slot_ids[None, :] < sent_counts[:, None]
    pick_rows = jnp.where(occupied, send_start[:, None] + slot_ids[None, :], -1).reshape(-1)
    own_rows = jnp.arange(source_tokens.shape[0], dtype=jnp.int32)
    choose = (pick_rows[:, None] == own_rows[None, :]).astype(BF16)
    packed = dot(choose, share).astype(BF16).reshape(replicas, slot_count, width)
    arrived = lax.all_to_all(packed, "dp", split_axis=0, concat_axis=0, tiled=True)
    incoming = lax.dynamic_index_in_dim(send_counts, replica, 1, keepdims=False)
    end_rows = jnp.cumsum(incoming)
    starts = end_rows - incoming
    places = jnp.arange(stream_count, dtype=jnp.int32)
    slot_place = starts[:, None] + slot_ids[None, :]
    slot_place = jnp.where(slot_ids[None, :] < incoming[:, None], slot_place, -1).reshape(-1)
    choose = (places[:, None] == slot_place[None, :]).astype(BF16)
    stream = dot(choose, arrived.reshape(replicas * slot_count, width)).astype(BF16)
    reach = 1
    while reach < sections:
        route = [(i + reach, i) for i in range(0, sections, 2 * reach)]
        stream = jnp.concatenate([stream, lax.ppermute(stream, "section", route)], axis=1)
        reach *= 2
    return stream, places < end_rows[replicas - 1]


def layout(segments, filled):
    micro_count, token_count = segments.shape
    tokens = micro_count * token_count
    segment = segments.reshape(tokens)
    places = jnp.arange(tokens, dtype=jnp.int32)
    sequence = places // token_count
    same = (segment[:, None] == segment[None, :]) & (sequence[:, None] == sequence[None, :])
    before = places[None, :] < places[:, None]
    position = jnp.sum(jnp.where(same & before, 1.0, 0.0).astype(F32), axis=1)
    alone = places[None, :] == places[:, None]
    allowed = (before & same & filled[:, None] & filled[None, :]) | alone
    half = HEAD_SIZE // 2
    frequency = ROPE_BASE ** (-2.0 * jnp.arange(half, dtype=F32) / HEAD_SIZE)
    angles = position[:, None] * frequency[None, :]
    cosine, sine = jnp.cos(angles), jnp.sin(angles)
    heads = LANES // HEAD_SIZE
    return (
        jnp.concatenate([cosine, cosine] * heads, axis=1),
        jnp.concatenate([-sine, sine] * heads, axis=1),
        allowed.astype(F32),
    )


def local(
    source_tokens,
    send_counts,
    doc_segments,
    out_cotangent,
    norm_gain,
    query_weight,
    frozen_key_matrix,
    frozen_value_matrix,
    out_weight,
    adapter_down,
    adapter_up_maps,
):
    replicas = lax.axis_size("dp")
    sections = lax.axis_size("section")
    replica = lax.axis_index("dp")
    section = lax.axis_index("section")
    features = source_tokens.shape[1]
    tokens = doc_segments.shape[0] * doc_segments.shape[1]

    half = out_weight.shape[2] // 2
    out_rows = jnp.concatenate([out_weight[0, :, :half], out_weight[0, :, half:]], axis=0)
    shard = jnp.concatenate(
        [query_weight[0], frozen_key_matrix[0], frozen_value_matrix[0], out_rows], axis=1
    )
    shards, late = gather_shards(shard, replica, replicas)
    stream, filled = exchange_tokens(
        source_tokens, send_counts, replica, replicas, section, sections, tokens, late
    )
    cosine, sine, allowed = layout(doc_segments, filled)
    gain = norm_gain[0].reshape(1, features)
    tables = jnp.stack([cosine, sine, allowed])
    down = adapter_down[0].transpose(0, 2, 1).reshape(2 * RANK, features)
    up = adapter_up_maps[0]
    up = jnp.concatenate(
        [
            jnp.pad(up[:, :QUERY_WIDTH], ((0, RANK), (0, 0))),
            jnp.pad(up[:, QUERY_WIDTH:], ((RANK, 0), (0, 0))),
        ],
        axis=1,
    )

    saved_shapes = [
        ((tokens, features), BF16),
        ((tokens, QUERY_WIDTH), BF16),
        ((tokens, KEY_WIDTH), BF16),
        ((tokens, KEY_WIDTH), BF16),
        ((tokens, QUERY_HEADS * tokens), BF16),
        ((tokens, 2 * RANK), BF16),
        ((tokens, features), BF16),
    ]
    stream, tables, gain, down, up, *pieces = lax.optimization_barrier(
        (stream, tables, gain, down, up, *[data for _, data in shards])
    )
    wqkv, wout = place([offset for offset, _ in shards], replica // X_CHIPS, pieces)
    fixed = (tables, gain, down, up, wqkv, wout)
    has_turn = section.astype(jnp.int32).reshape(1)
    x = stream
    saved = tuple(jnp.zeros(shape, dtype) for shape, dtype in saved_shapes)
    for turn in range(sections):
        last = turn + 1 == sections
        kernel = functools.partial(forward_kernel, turn, last)
        y, saved = step(kernel, has_turn, x, fixed, (), saved)
        if not last:
            x = lax.ppermute(y, "section", [(turn, turn + 1)])

    held, (low, normed) = saved[:5], saved[5:]
    c = out_cotangent
    kept = (
        jnp.zeros((tokens, QUERY_WIDTH), BF16),
        jnp.zeros((tokens, KEY_WIDTH), BF16),
        jnp.zeros((tokens, 2 * RANK), BF16),
    )
    for turn in range(sections - 1, -1, -1):
        kernel = functools.partial(backward_kernel, turn, turn == 0)
        if turn > 0:
            back, kept = step(kernel, has_turn, c, fixed, held, kept)
        else:
            back, kept = step(kernel, has_turn, c, (tables, up, wout), held[2:], kept)
        if turn > 0:
            c = lax.ppermute(back, "section", [(turn, turn - 1)])

    (grads,) = call(
        grads_kernel,
        [((X_CHIPS, 3 * RANK, features // X_CHIPS), BF16)],
        (normed, low, kept[0], kept[1], kept[2]),
    )
    grads = sum_over_replicas(grads, replica, replicas)
    down_grads = grads[: 2 * RANK].reshape(2, RANK, features).transpose(0, 2, 1)
    up_grads = grads[2 * RANK :, : QUERY_WIDTH + KEY_WIDTH]
    return (down_grads[None], up_grads[None])


def solution(mesh):
    placed = (
        P("dp", None),
        P(),
        P("dp", None),
        P("dp", None),
        P("section", None),
        P("section", "dp", None),
        P("section", "dp", None),
        P("section", "dp", None),
        P("section", "dp", None),
        P("section", None, None, None),
        P("section", None, None),
    )
    return jax.shard_map(
        local,
        mesh=mesh,
        in_specs=placed,
        out_specs=(P("section", None, None, None), P("section", None, None)),
        check_vma=False,
    )
```

```python
import functools

import jax
import jax.numpy as jnp
from jax import lax
from jax.experimental import pallas as pl
from jax.experimental.pallas import tpu as pltpu
from jax.sharding import PartitionSpec as P

QUERY_HEADS = 16
KEY_VALUE_HEADS = 4
GROUP = QUERY_HEADS // KEY_VALUE_HEADS
HEAD_SIZE = 64
QUERY_WIDTH = QUERY_HEADS * HEAD_SIZE
KEY_WIDTH = KEY_VALUE_HEADS * HEAD_SIZE
RANK = 16
LANES = 128

ROPE_BASE = 500000.0
ADAPTER_SCALE = 2.0
NORM_EPS = 1e-05
SCORE_SCALE = HEAD_SIZE ** (-0.5)

X_CHIPS = 4

F32 = jnp.float32
BF16 = jnp.bfloat16
VMEM_LIMIT = 32 * 1024 * 1024
LATE_ROUND = 2


def dot(a, b):
    return jnp.dot(a, b, preferred_element_type=F32)


def dot_nt(a, b):
    return lax.dot_general(a, b, (((1,), (1,)), ((), ())), preferred_element_type=F32)


def dot_tn(a, b):
    return lax.dot_general(a, b, (((0,), (0,)), ((), ())), preferred_element_type=F32)


def lanes_of(rows, width):
    return lax.broadcasted_iota(jnp.int32, (rows, width), 1)


def rope(t, cosine, signed_sine):
    rows, width = t.shape
    copies = width // LANES
    wide_cos = jnp.concatenate([cosine] * copies, axis=1)
    wide_sin = jnp.concatenate([signed_sine] * copies, axis=1)
    half = HEAD_SIZE // 2
    leading = (lanes_of(rows, width) % HEAD_SIZE) < half
    partner = jnp.where(leading, pltpu.roll(t, width - half, 1), pltpu.roll(t, half, 1))
    return t * wide_cos + partner * wide_sin


def expand(turned, head):
    rows, width = turned[0].shape
    block = lanes_of(rows, width) // HEAD_SIZE
    zero = jnp.zeros((), turned[0].dtype)
    parts = [
        jnp.where(block == g, turned[(g - head) % KEY_VALUE_HEADS], zero) for g in range(GROUP)
    ]
    return jnp.concatenate(parts, axis=0)


def turns_of(t):
    width = t.shape[1]
    wide = t.astype(F32)
    return [t] + [
        pltpu.roll(wide, j * HEAD_SIZE, 1).astype(t.dtype) for j in range(1, KEY_VALUE_HEADS)
    ]


def fold(products):
    rows = products[0].shape[0] // GROUP
    width = products[0].shape[1]
    block = lanes_of(rows, width) // HEAD_SIZE
    total = None
    for h, product in enumerate(products):
        diagonal = None
        for g in range(GROUP):
            part = jnp.where(block == g, product[g * rows : (g + 1) * rows], 0.0)
            diagonal = part if diagonal is None else diagonal + part
        pair = diagonal + pltpu.roll(diagonal, HEAD_SIZE, 1)
        whole = pair + pltpu.roll(pair, 2 * HEAD_SIZE, 1)
        kept = jnp.where(block == h, whole, 0.0)
        total = kept if total is None else total + kept
    return total


def load(copies):
    for copy in copies:
        copy.start()


def forward_kernel(turn, last, turn_ref, x_ref, *refs):
    fixed, y_ref, kept = refs[:6], refs[13], refs[14:21]

    @pl.when(turn_ref[0] == turn)
    def _():
        forward_step(last, x_ref, *fixed, y_ref, *kept)


def forward_step(
    last,
    x_ref, tables, gain, down, up, wqkv, wout,
    y_ref, kept_x_ref, q_ref, k_ref, v_ref, p_ref, low_ref, n_ref,
):
    width = GROUP * HEAD_SIZE
    head_at = [slice(h * width, (h + 1) * width) for h in range(KEY_VALUE_HEADS)]
    cosine, sine = tables[0], tables[1]
    allowed = tables[2] > 0.0
    x = x_ref[...]
    kept_x_ref[...] = x
    hidden = x.astype(F32)
    energy = jnp.mean(hidden * hidden, axis=-1, keepdims=True)
    n = (hidden * lax.rsqrt(energy + NORM_EPS) * gain[...]).astype(BF16)
    n_ref[...] = n
    low = dot_nt(n, down[...]).astype(BF16)
    low_ref[...] = low
    kv = dot(n, wqkv[:, QUERY_WIDTH:])
    k = rope(kv[:, :KEY_WIDTH], cosine, sine).astype(BF16)
    k_ref[...] = k
    v = kv[:, KEY_WIDTH:] + ADAPTER_SCALE * dot(low, up[:, QUERY_WIDTH:])
    v = v.astype(BF16)
    v_ref[...] = v
    k_turns, v_turns = turns_of(k), turns_of(v)
    tokens = hidden.shape[0]
    blended = []
    for h, at in enumerate(head_at):
        q = dot(n, wqkv[:, at]) + ADAPTER_SCALE * dot(low, up[:, at])
        q = rope(q, cosine, sine).astype(BF16)
        q_ref[:, at] = q
        scores = dot_nt(q, expand(k_turns, h)) * SCORE_SCALE
        shares = []
        for g in range(GROUP):
            weights = jnp.where(allowed, jnp.exp(scores[:, g * tokens : (g + 1) * tokens]), 0.0)
            shares.append((weights / jnp.sum(weights, axis=-1, keepdims=True)).astype(BF16))
        shares = jnp.concatenate(shares, axis=1)
        p_ref[:, h * GROUP * tokens : (h + 1) * GROUP * tokens] = shares
        if not last:
            blended.append(dot(shares, expand(v_turns, h)).astype(BF16))
    if not last:
        y_ref[...] = (hidden + dot(jnp.concatenate(blended, axis=1), wout[...])).astype(BF16)


def backward_kernel(turn, first, turn_ref, c_ref, *refs):
    out_ref, kept = refs[-4], refs[-3:]

    @pl.when(turn_ref[0] == turn)
    def _():
        if first:
            tables, up, wout, k_ref, v_ref, p_ref = refs[:6]
            fixed, held = (tables, None, None, up, None, wout), (None, None, k_ref, v_ref, p_ref)
        else:
            fixed, held = refs[:6], refs[6:11]
        backward_step(first, c_ref, *fixed, *held, out_ref, *kept)


def backward_step(
    first,
    c_ref, tables, gain, down, up, wqkv, wout,
    x_ref, q_ref, k_ref, v_ref, p_ref,
    out_ref, dq_ref, dv_ref, dlow_ref,
):
    width = GROUP * HEAD_SIZE
    head_at = [slice(h * width, (h + 1) * width) for h in range(KEY_VALUE_HEADS)]
    cosine, sine = tables[0], tables[1]
    k_turns, v_turns = turns_of(k_ref[...]), turns_of(v_ref[...])
    c = c_ref[...]
    tokens = c.shape[0]
    dn = None
    dlow = None
    dk_products, dv_products = [], []
    for h, at in enumerate(head_at):
        dblended = dot(c, wout[:, at]).astype(BF16)
        shares = p_ref[:, h * GROUP * tokens : (h + 1) * GROUP * tokens]
        dshares = dot_nt(dblended, expand(v_turns, h))
        dscores = []
        for g in range(GROUP):
            span = slice(g * tokens, (g + 1) * tokens)
            p = shares[:, span].astype(F32)
            dp = dshares[:, span]
            pdp = p * dp
            dscores.append(
                ((pdp - p * jnp.sum(pdp, axis=-1, keepdims=True)) * SCORE_SCALE).astype(BF16)
            )
        dscores = jnp.concatenate(dscores, axis=1)
        dq = dot(dscores, expand(k_turns, h))
        dq = rope(dq, cosine, -sine).astype(BF16)
        dq_ref[:, at] = dq
        part = dot_nt(dq, up[:, at])
        dlow = part if dlow is None else dlow + part
        dv_products.append(dot_tn(shares, dblended))
        if not first:
            dk_products.append(dot_tn(dscores, q_ref[:, at]))
            part = dot(dq, wqkv[at, :])
            dn = part if dn is None else dn + part
    dv = fold(dv_products).astype(BF16)
    dv_ref[...] = dv
    dlow = (ADAPTER_SCALE * (dlow + dot_nt(dv, up[:, QUERY_WIDTH:]))).astype(BF16)
    dlow_ref[...] = dlow
    if first:
        return
    dk = rope(fold(dk_products), cosine, -sine).astype(BF16)
    dn = dn + dot(jnp.concatenate([dk, dv], axis=1), wqkv[QUERY_WIDTH:, :])
    dn = dn + dot(dlow, down[...])
    hidden = x_ref[...].astype(F32)
    energy = jnp.mean(hidden * hidden, axis=-1, keepdims=True)
    scale = lax.rsqrt(energy + NORM_EPS)
    dy = dn * gain[...]
    along = jnp.mean(hidden * dy, axis=-1, keepdims=True)
    dh = scale * dy - hidden * (scale * scale * scale * along)
    out_ref[...] = (c.astype(F32) + dh).astype(BF16)


def turn_kernel(act, turn_ref, wqkv, wout, *refs):
    wqkv_turned, wout_turned = refs[-2:]

    @pl.when(act(turn_ref[0]))
    def _():
        wqkv_turned[...] = wqkv[...].T
        wout_turned[...] = wout[...].T


def turn_weights(act, section, weights, kept=()):
    return pl.pallas_call(
        functools.partial(turn_kernel, act),
        out_shape=[jax.ShapeDtypeStruct(t.shape[::-1], t.dtype) for t in weights],
        in_specs=[pl.BlockSpec(memory_space=pltpu.SMEM)]
        + [pl.BlockSpec(memory_space=pltpu.VMEM)] * (len(weights) + len(kept)),
        out_specs=[pl.BlockSpec(memory_space=pltpu.VMEM)] * len(weights),
        input_output_aliases={1 + len(weights) + i: i for i in range(len(kept))},
        compiler_params=pltpu.CompilerParams(vmem_limit_bytes=VMEM_LIMIT),
    )(section, *weights, *kept)


def grads_kernel(n_ref, low_ref, dq_ref, dv_ref, dlow_ref, g_ref):
    part = g_ref.shape[2]
    down = dot_tn(dlow_ref[...], n_ref[...]).astype(BF16)
    low = low_ref[...]
    up_q = ADAPTER_SCALE * dot_tn(low, dq_ref[...])[:RANK]
    up_v = ADAPTER_SCALE * dot_tn(low, dv_ref[...])[RANK : 2 * RANK]
    spare = jnp.zeros((RANK, g_ref.shape[0] * part - QUERY_WIDTH - KEY_WIDTH), F32)
    up = jnp.concatenate([up_q, up_v, spare], axis=1).astype(BF16)
    for i in range(g_ref.shape[0]):
        at = slice(i * part, (i + 1) * part)
        g_ref[i, 0 : 2 * RANK, :] = down[:, at]
        g_ref[i, 2 * RANK : 3 * RANK, :] = up[:, at]


def place_kernel(offsets, at_ref, *refs):
    qkv, out, sems = refs[-3:]
    z_count, _, rows, qkv_width = qkv.shape
    half, width = rows // 2, out.shape[3] // 2
    rest = pl.ds(qkv_width, width)
    ends = []
    for piece, offset in zip(refs, offsets):
        z_at = lax.rem(at_ref[0] + (offset + z_count), z_count)
        ends += [
            (piece.at[:, :, pl.ds(0, qkv_width)], qkv.at[z_at]),
            (piece.at[:, pl.ds(0, half), rest], out.at[z_at, :, :, pl.ds(0, width)]),
            (piece.at[:, pl.ds(half, half), rest], out.at[z_at, :, :, pl.ds(width, width)]),
        ]
    copies = [pltpu.make_async_copy(a, b, sems.at[i]) for i, (a, b) in enumerate(ends)]
    for copy in copies:
        copy.start()
    for copy in copies:
        copy.wait()


def place(offsets, z, pieces):
    x_count, rows, columns = pieces[0].shape
    qkv_width = QUERY_WIDTH + 2 * KEY_WIDTH
    z_count, out_width = len(pieces), 2 * (columns - qkv_width)
    shapes = [(z_count, x_count, rows, qkv_width), (z_count, x_count, rows // 2, out_width)]
    wqkv, wout = pl.pallas_call(
        functools.partial(place_kernel, offsets),
        out_shape=[jax.ShapeDtypeStruct(shape, BF16) for shape in shapes],
        in_specs=[pl.BlockSpec(memory_space=pltpu.SMEM)]
        + [pl.BlockSpec(memory_space=pl.ANY)] * len(pieces),
        out_specs=[pl.BlockSpec(memory_space=pltpu.VMEM)] * len(shapes),
        scratch_shapes=[pltpu.SemaphoreType.DMA((3 * len(offsets),))],
        compiler_params=pltpu.CompilerParams(vmem_limit_bytes=VMEM_LIMIT),
    )(z.astype(jnp.int32).reshape(1), *pieces)
    all_rows = z_count * x_count * rows
    return wqkv.reshape(all_rows, qkv_width), wout.reshape(all_rows // 2, out_width)


def call(kernel, outs, args):
    return pl.pallas_call(
        kernel,
        out_shape=[jax.ShapeDtypeStruct(shape, dtype) for shape, dtype in outs],
        in_specs=[pl.BlockSpec(memory_space=pltpu.VMEM)] * len(args),
        out_specs=[pl.BlockSpec(memory_space=pltpu.VMEM)] * len(outs),
        compiler_params=pltpu.CompilerParams(vmem_limit_bytes=VMEM_LIMIT),
    )(*args)


def step(kernel, section, arrived, fixed, read, kept):
    args = (section, arrived, *fixed, *read, *kept)
    outs = [arrived, *kept]
    first_kept = len(args) - len(kept)
    made = pl.pallas_call(
        kernel,
        out_shape=[jax.ShapeDtypeStruct(t.shape, t.dtype) for t in outs],
        in_specs=[pl.BlockSpec(memory_space=pltpu.SMEM)]
        + [pl.BlockSpec(memory_space=pltpu.VMEM)] * (len(args) - 1),
        out_specs=[pl.BlockSpec(memory_space=pltpu.VMEM)] * len(outs),
        input_output_aliases={first_kept + i: 1 + i for i in range(len(kept))},
        compiler_params=pltpu.CompilerParams(vmem_limit_bytes=VMEM_LIMIT),
    )(*args)
    return made[0], tuple(made[1:])


def z_route(replicas, distance):
    return [(i, (i + distance * X_CHIPS) % replicas) for i in range(replicas)]


def x_route(replicas, distance):
    return [
        (i, i // X_CHIPS * X_CHIPS + (i % X_CHIPS + distance) % X_CHIPS) for i in range(replicas)
    ]


def gather_shards(shard, replica, replicas):
    rows, columns = shard.shape
    z_count = replicas // X_CHIPS
    x = replica % X_CHIPS
    along_z = functools.partial(z_route, replicas)
    along_x = functools.partial(x_route, replicas)
    far = lax.ppermute(shard, "dp", along_x(2))
    right = lax.ppermute(shard, "dp", along_x(1))
    left = lax.ppermute(shard, "dp", along_x(-1))
    line = jnp.zeros((X_CHIPS, rows, columns), shard.dtype)
    for turn, data in ((0, shard), (-1, right), (1, left), (2, far)):
        line = lax.dynamic_update_slice(line, data[None], ((x + turn) % X_CHIPS, 0, 0))
    ahead = behind = line
    pieces = [(0, line)]
    late = None
    middle = X_CHIPS // 2
    for step in range(1, z_count // 2):
        ahead = lax.ppermute(ahead, "dp", along_z(1))
        behind = lax.ppermute(behind, "dp", along_z(-1))
        pieces += [(-step, ahead), (step, behind)]
        if step == LATE_ROUND:
            late = ahead
    upper = lax.ppermute(ahead[:middle], "dp", along_z(1))
    lower = lax.ppermute(behind[middle:], "dp", along_z(-1))
    pieces.append((z_count // 2, jnp.concatenate([upper, lower], axis=0)))
    return pieces, late


def sum_over_replicas(parts, replica, replicas):
    count, rows, columns = parts.shape
    x = replica % X_CHIPS
    low_bit, high_bit = x % 2, x // 2

    def swap(t, mask):
        return lax.ppermute(t, "dp", [(i, i ^ mask) for i in range(replicas)])

    def add(t, other):
        return (t.astype(F32) + other.astype(F32)).astype(BF16)

    def pick(t, axis, at):
        return lax.dynamic_index_in_dim(t, at, axis, keepdims=False)

    def join(own, other, bit, axis):
        return jnp.where(
            bit == 0, jnp.stack([own, other], axis=axis), jnp.stack([other, own], axis=axis)
        )

    total = parts.reshape(2, 2, rows, columns)
    total = add(pick(total, 1, low_bit), swap(pick(total, 1, 1 - low_bit), 1))
    total = add(pick(total, 0, high_bit), swap(pick(total, 0, 1 - high_bit), 2))
    mask = X_CHIPS
    while 2 * mask < replicas:
        total = add(total, swap(total, mask))
        mask *= 2
    route = [(i, replicas - X_CHIPS - i // X_CHIPS * X_CHIPS + i % X_CHIPS) for i in range(replicas)]
    total = add(total, lax.ppermute(total, "dp", route))
    total = join(total, swap(total, 2), high_bit, 0)
    total = join(total, swap(total, 1), low_bit, 1)
    whole = total.reshape(count, rows, columns).astype(F32)
    return whole.transpose(1, 0, 2).reshape(rows, count * columns)


def exchange_tokens(source_tokens, send_counts, replica, replicas, section, sections, stream_count, late):
    slot_count = source_tokens.shape[0] // replicas
    width = source_tokens.shape[1] // sections
    share = lax.dynamic_slice_in_dim(source_tokens, section * width, width, 1)
    share, _ = lax.optimization_barrier((share, late))
    sent_counts = lax.dynamic_index_in_dim(send_counts, replica, 0, keepdims=False)
    send_start = jnp.cumsum(sent_counts) - sent_counts
    slot_ids = jnp.arange(slot_count, dtype=jnp.int32)
    occupied = slot_ids[None, :] < sent_counts[:, None]
    pick_rows = jnp.where(occupied, send_start[:, None] + slot_ids[None, :], -1).reshape(-1)
    own_rows = jnp.arange(source_tokens.shape[0], dtype=jnp.int32)
    choose = (pick_rows[:, None] == own_rows[None, :]).astype(BF16)
    packed = dot(choose, share).astype(BF16).reshape(replicas, slot_count, width)
    arrived = lax.all_to_all(packed, "dp", split_axis=0, concat_axis=0, tiled=True)
    incoming = lax.dynamic_index_in_dim(send_counts, replica, 1, keepdims=False)
    end_rows = jnp.cumsum(incoming)
    starts = end_rows - incoming
    places = jnp.arange(stream_count, dtype=jnp.int32)
    slot_place = starts[:, None] + slot_ids[None, :]
    slot_place = jnp.where(slot_ids[None, :] < incoming[:, None], slot_place, -1).reshape(-1)
    choose = (places[:, None] == slot_place[None, :]).astype(BF16)
    stream = dot(choose, arrived.reshape(replicas * slot_count, width)).astype(BF16)
    reach = 1
    while reach < sections:
        route = [(i + reach, i) for i in range(0, sections, 2 * reach)]
        stream = jnp.concatenate([stream, lax.ppermute(stream, "section", route)], axis=1)
        reach *= 2
    return stream, places < end_rows[replicas - 1]


def layout(segments, filled):
    micro_count, token_count = segments.shape
    tokens = micro_count * token_count
    segment = segments.reshape(tokens)
    places = jnp.arange(tokens, dtype=jnp.int32)
    sequence = places // token_count
    same = (segment[:, None] == segment[None, :]) & (sequence[:, None] == sequence[None, :])
    before = places[None, :] < places[:, None]
    position = jnp.sum(jnp.where(same & before, 1.0, 0.0).astype(F32), axis=1)
    alone = places[None, :] == places[:, None]
    allowed = (before & same & filled[:, None] & filled[None, :]) | alone
    half = HEAD_SIZE // 2
    frequency = ROPE_BASE ** (-2.0 * jnp.arange(half, dtype=F32) / HEAD_SIZE)
    angles = position[:, None] * frequency[None, :]
    cosine, sine = jnp.cos(angles), jnp.sin(angles)
    heads = LANES // HEAD_SIZE
    return (
        jnp.concatenate([cosine, cosine] * heads, axis=1),
        jnp.concatenate([-sine, sine] * heads, axis=1),
        allowed.astype(F32),
    )


def local(
    source_tokens,
    send_counts,
    doc_segments,
    out_cotangent,
    norm_gain,
    query_weight,
    frozen_key_matrix,
    frozen_value_matrix,
    out_weight,
    adapter_down,
    adapter_up_maps,
):
    replicas = lax.axis_size("dp")
    sections = lax.axis_size("section")
    replica = lax.axis_index("dp")
    section = lax.axis_index("section")
    features = source_tokens.shape[1]
    tokens = doc_segments.shape[0] * doc_segments.shape[1]

    half = out_weight.shape[2] // 2
    out_rows = jnp.concatenate([out_weight[0, :, :half], out_weight[0, :, half:]], axis=0)
    shard = jnp.concatenate(
        [query_weight[0], frozen_key_matrix[0], frozen_value_matrix[0], out_rows], axis=1
    )
    shards, late = gather_shards(shard, replica, replicas)
    stream, filled = exchange_tokens(
        source_tokens, send_counts, replica, replicas, section, sections, tokens, late
    )
    cosine, sine, allowed = layout(doc_segments, filled)
    gain = norm_gain[0].reshape(1, features)
    tables = jnp.stack([cosine, sine, allowed])
    down = adapter_down[0].transpose(0, 2, 1).reshape(2 * RANK, features)
    up = adapter_up_maps[0]
    up = jnp.concatenate(
        [
            jnp.pad(up[:, :QUERY_WIDTH], ((0, RANK), (0, 0))),
            jnp.pad(up[:, QUERY_WIDTH:], ((RANK, 0), (0, 0))),
        ],
        axis=1,
    )

    saved_shapes = [
        ((tokens, features), BF16),
        ((tokens, QUERY_WIDTH), BF16),
        ((tokens, KEY_WIDTH), BF16),
        ((tokens, KEY_WIDTH), BF16),
        ((tokens, QUERY_HEADS * tokens), BF16),
        ((tokens, 2 * RANK), BF16),
        ((tokens, features), BF16),
    ]
    stream, tables, gain, down, up, *pieces = lax.optimization_barrier(
        (stream, tables, gain, down, up, *[data for _, data in shards])
    )
    wqkv, wout = place([offset for offset, _ in shards], replica // X_CHIPS, pieces)
    fixed = (tables, gain, down, up, wqkv, wout)
    has_turn = section.astype(jnp.int32).reshape(1)
    x = stream
    saved = tuple(jnp.zeros(shape, dtype) for shape, dtype in saved_shapes)
    turned = turn_weights(lambda at: at != 0, has_turn, fixed[4:])
    for turn in range(sections):
        if turn == 2:
            turned = turn_weights(lambda at: at == 0, has_turn, fixed[4:], turned)
        last = turn + 1 == sections
        kernel = functools.partial(forward_kernel, turn, last)
        y, saved = step(kernel, has_turn, x, fixed, (), saved)
        if not last:
            x = lax.ppermute(y, "section", [(turn, turn + 1)])

    held, (low, normed) = saved[:5], saved[5:]
    c = out_cotangent
    kept = (
        jnp.zeros((tokens, QUERY_WIDTH), BF16),
        jnp.zeros((tokens, KEY_WIDTH), BF16),
        jnp.zeros((tokens, 2 * RANK), BF16),
    )
    for turn in range(sections - 1, -1, -1):
        kernel = functools.partial(backward_kernel, turn, turn == 0)
        if turn > 0:
            back, kept = step(kernel, has_turn, c, (*fixed[:4], *turned), held, kept)
        else:
            back, kept = step(kernel, has_turn, c, (tables, up, turned[1]), held[2:], kept)
        if turn > 0:
            c = lax.ppermute(back, "section", [(turn, turn - 1)])

    (grads,) = call(
        grads_kernel,
        [((X_CHIPS, 3 * RANK, features // X_CHIPS), BF16)],
        (normed, low, kept[0], kept[1], kept[2]),
    )
    grads = sum_over_replicas(grads, replica, replicas)
    down_grads = grads[: 2 * RANK].reshape(2, RANK, features).transpose(0, 2, 1)
    up_grads = grads[2 * RANK :, : QUERY_WIDTH + KEY_WIDTH]
    return (down_grads[None], up_grads[None])


def solution(mesh):
    placed = (
        P("dp", None),
        P(),
        P("dp", None),
        P("dp", None),
        P("section", None),
        P("section", "dp", None),
        P("section", "dp", None),
        P("section", "dp", None),
        P("section", "dp", None),
        P("section", None, None, None),
        P("section", None, None),
    )
    return jax.shard_map(
        local,
        mesh=mesh,
        in_specs=placed,
        out_specs=(P("section", None, None, None), P("section", None, None)),
        check_vma=False,
    )
```

```python
import functools

import jax
import jax.numpy as jnp
from jax import lax
from jax.experimental import pallas as pl
from jax.experimental.pallas import tpu as pltpu
from jax.sharding import PartitionSpec as P

QUERY_HEADS = 16
KEY_VALUE_HEADS = 4
GROUP = QUERY_HEADS // KEY_VALUE_HEADS
HEAD_SIZE = 64
QUERY_WIDTH = QUERY_HEADS * HEAD_SIZE
KEY_WIDTH = KEY_VALUE_HEADS * HEAD_SIZE
RANK = 16
LANES = 128

ROPE_BASE = 500000.0
ADAPTER_SCALE = 2.0
NORM_EPS = 1e-05
SCORE_SCALE = HEAD_SIZE ** (-0.5)

X_CHIPS = 4

F32 = jnp.float32
BF16 = jnp.bfloat16
VMEM_LIMIT = 24 * 1024 * 1024
LATE_ROUND = 2


def dot(a, b):
    return jnp.dot(a, b, preferred_element_type=F32)


def dot_nt(a, b):
    return lax.dot_general(a, b, (((1,), (1,)), ((), ())), preferred_element_type=F32)


def dot_tn(a, b):
    return lax.dot_general(a, b, (((0,), (0,)), ((), ())), preferred_element_type=F32)


def lanes_of(rows, width):
    return lax.broadcasted_iota(jnp.int32, (rows, width), 1)


def rope(t, cosine, signed_sine):
    rows, width = t.shape
    copies = width // LANES
    wide_cos = jnp.concatenate([cosine] * copies, axis=1)
    wide_sin = jnp.concatenate([signed_sine] * copies, axis=1)
    half = HEAD_SIZE // 2
    leading = (lanes_of(rows, width) % HEAD_SIZE) < half
    partner = jnp.where(leading, pltpu.roll(t, width - half, 1), pltpu.roll(t, half, 1))
    return t * wide_cos + partner * wide_sin


def expand(turned, head):
    rows, width = turned[0].shape
    block = lanes_of(rows, width) // HEAD_SIZE
    zero = jnp.zeros((), turned[0].dtype)
    parts = [
        jnp.where(block == g, turned[(g - head) % KEY_VALUE_HEADS], zero) for g in range(GROUP)
    ]
    return jnp.concatenate(parts, axis=0)


def turns_of(t):
    width = t.shape[1]
    wide = t.astype(F32)
    return [t] + [
        pltpu.roll(wide, j * HEAD_SIZE, 1).astype(t.dtype) for j in range(1, KEY_VALUE_HEADS)
    ]


def fold(products):
    rows = products[0].shape[0] // GROUP
    width = products[0].shape[1]
    block = lanes_of(rows, width) // HEAD_SIZE
    total = None
    for h, product in enumerate(products):
        diagonal = None
        for g in range(GROUP):
            part = jnp.where(block == g, product[g * rows : (g + 1) * rows], 0.0)
            diagonal = part if diagonal is None else diagonal + part
        pair = diagonal + pltpu.roll(diagonal, HEAD_SIZE, 1)
        whole = pair + pltpu.roll(pair, 2 * HEAD_SIZE, 1)
        kept = jnp.where(block == h, whole, 0.0)
        total = kept if total is None else total + kept
    return total


def load(copies):
    for copy in copies:
        copy.start()


def forward_kernel(turn, last, turn_ref, x_ref, *refs):
    fixed, y_ref, kept = refs[:6], refs[13], refs[14:21]

    @pl.when(turn_ref[0] == turn)
    def _():
        forward_step(last, x_ref, *fixed, y_ref, *kept)


def forward_step(
    last,
    x_ref, tables, gain, down, up, wqkv, wout,
    y_ref, kept_x_ref, q_ref, k_ref, v_ref, p_ref, low_ref, n_ref,
):
    width = GROUP * HEAD_SIZE
    head_at = [slice(h * width, (h + 1) * width) for h in range(KEY_VALUE_HEADS)]
    cosine, sine = tables[0], tables[1]
    allowed = tables[2] > 0.0
    x = x_ref[...]
    kept_x_ref[...] = x
    hidden = x.astype(F32)
    energy = jnp.mean(hidden * hidden, axis=-1, keepdims=True)
    n = (hidden * lax.rsqrt(energy + NORM_EPS) * gain[...]).astype(BF16)
    n_ref[...] = n
    low = dot_nt(n, down[...]).astype(BF16)
    low_ref[...] = low
    kv = dot(n, wqkv[:, QUERY_WIDTH:])
    k = rope(kv[:, :KEY_WIDTH], cosine, sine).astype(BF16)
    k_ref[...] = k
    v = kv[:, KEY_WIDTH:] + ADAPTER_SCALE * dot(low, up[:, QUERY_WIDTH:])
    v = v.astype(BF16)
    v_ref[...] = v
    k_turns, v_turns = turns_of(k), turns_of(v)
    tokens = hidden.shape[0]
    blended = []
    for h, at in enumerate(head_at):
        q = dot(n, wqkv[:, at]) + ADAPTER_SCALE * dot(low, up[:, at])
        q = rope(q, cosine, sine).astype(BF16)
        q_ref[:, at] = q
        scores = dot_nt(q, expand(k_turns, h)) * SCORE_SCALE
        shares = []
        for g in range(GROUP):
            weights = jnp.where(allowed, jnp.exp(scores[:, g * tokens : (g + 1) * tokens]), 0.0)
            shares.append((weights / jnp.sum(weights, axis=-1, keepdims=True)).astype(BF16))
        shares = jnp.concatenate(shares, axis=1)
        p_ref[:, h * GROUP * tokens : (h + 1) * GROUP * tokens] = shares
        if not last:
            blended.append(dot(shares, expand(v_turns, h)).astype(BF16))
    if not last:
        y_ref[...] = (hidden + dot(jnp.concatenate(blended, axis=1), wout[...])).astype(BF16)


def backward_kernel(turn, first, turn_ref, c_ref, *refs):
    out_ref, kept = refs[-4], refs[-3:]

    @pl.when(turn_ref[0] == turn)
    def _():
        if first:
            tables, up, wout, k_ref, v_ref, p_ref = refs[:6]
            fixed, held = (tables, None, None, up, None, wout), (None, None, k_ref, v_ref, p_ref)
        else:
            fixed, held = refs[:6], refs[6:11]
        backward_step(first, c_ref, *fixed, *held, out_ref, *kept)


def backward_step(
    first,
    c_ref, tables, gain, down, up, wqkv, wout,
    x_ref, q_ref, k_ref, v_ref, p_ref,
    out_ref, dq_ref, dv_ref, dlow_ref,
):
    width = GROUP * HEAD_SIZE
    head_at = [slice(h * width, (h + 1) * width) for h in range(KEY_VALUE_HEADS)]
    cosine, sine = tables[0], tables[1]
    k_turns, v_turns = turns_of(k_ref[...]), turns_of(v_ref[...])
    c = c_ref[...]
    tokens = c.shape[0]
    dn = None
    dlow = None
    dk_products, dv_products = [], []
    for h, at in enumerate(head_at):
        dblended = dot(c, wout[:, at]).astype(BF16)
        shares = p_ref[:, h * GROUP * tokens : (h + 1) * GROUP * tokens]
        dshares = dot_nt(dblended, expand(v_turns, h))
        dscores = []
        for g in range(GROUP):
            span = slice(g * tokens, (g + 1) * tokens)
            p = shares[:, span].astype(F32)
            dp = dshares[:, span]
            pdp = p * dp
            dscores.append(
                ((pdp - p * jnp.sum(pdp, axis=-1, keepdims=True)) * SCORE_SCALE).astype(BF16)
            )
        dscores = jnp.concatenate(dscores, axis=1)
        dq = dot(dscores, expand(k_turns, h))
        dq = rope(dq, cosine, -sine).astype(BF16)
        dq_ref[:, at] = dq
        part = dot_nt(dq, up[:, at])
        dlow = part if dlow is None else dlow + part
        dv_products.append(dot_tn(shares, dblended))
        if not first:
            dk_products.append(dot_tn(dscores, q_ref[:, at]))
            part = dot(dq, wqkv[at, :])
            dn = part if dn is None else dn + part
    dv = fold(dv_products).astype(BF16)
    dv_ref[...] = dv
    dlow = (ADAPTER_SCALE * (dlow + dot_nt(dv, up[:, QUERY_WIDTH:]))).astype(BF16)
    dlow_ref[...] = dlow
    if first:
        return
    dk = rope(fold(dk_products), cosine, -sine).astype(BF16)
    dn = dn + dot(jnp.concatenate([dk, dv], axis=1), wqkv[QUERY_WIDTH:, :])
    dn = dn + dot(dlow, down[...])
    hidden = x_ref[...].astype(F32)
    energy = jnp.mean(hidden * hidden, axis=-1, keepdims=True)
    scale = lax.rsqrt(energy + NORM_EPS)
    dy = dn * gain[...]
    along = jnp.mean(hidden * dy, axis=-1, keepdims=True)
    dh = scale * dy - hidden * (scale * scale * scale * along)
    out_ref[...] = (c.astype(F32) + dh).astype(BF16)


def turn_kernel(act, turn_ref, wqkv, wout, *refs):
    wqkv_turned, wout_turned = refs[-2:]

    @pl.when(act(turn_ref[0]))
    def _():
        wqkv_turned[...] = wqkv[...].T
        wout_turned[...] = wout[...].T


def turn_weights(act, section, weights, kept=()):
    return pl.pallas_call(
        functools.partial(turn_kernel, act),
        out_shape=[jax.ShapeDtypeStruct(t.shape[::-1], t.dtype) for t in weights],
        in_specs=[pl.BlockSpec(memory_space=pltpu.SMEM)]
        + [pl.BlockSpec(memory_space=pltpu.VMEM)] * (len(weights) + len(kept)),
        out_specs=[pl.BlockSpec(memory_space=pltpu.VMEM)] * len(weights),
        input_output_aliases={1 + len(weights) + i: i for i in range(len(kept))},
        compiler_params=pltpu.CompilerParams(vmem_limit_bytes=VMEM_LIMIT),
    )(section, *weights, *kept)


def grads_kernel(n_ref, low_ref, dq_ref, dv_ref, dlow_ref, g_ref):
    part = g_ref.shape[2]
    down = dot_tn(dlow_ref[...], n_ref[...]).astype(BF16)
    low = low_ref[...]
    up_q = ADAPTER_SCALE * dot_tn(low, dq_ref[...])[:RANK]
    up_v = ADAPTER_SCALE * dot_tn(low, dv_ref[...])[RANK : 2 * RANK]
    spare = jnp.zeros((RANK, g_ref.shape[0] * part - QUERY_WIDTH - KEY_WIDTH), F32)
    up = jnp.concatenate([up_q, up_v, spare], axis=1).astype(BF16)
    for i in range(g_ref.shape[0]):
        at = slice(i * part, (i + 1) * part)
        g_ref[i, 0 : 2 * RANK, :] = down[:, at]
        g_ref[i, 2 * RANK : 3 * RANK, :] = up[:, at]


def place_kernel(offsets, at_ref, *refs):
    qkv, out, sems = refs[-3:]
    z_count, _, rows, qkv_width = qkv.shape
    half, width = rows // 2, out.shape[3] // 2
    rest = pl.ds(qkv_width, width)
    ends = []
    for piece, offset in zip(refs, offsets):
        z_at = lax.rem(at_ref[0] + (offset + z_count), z_count)
        ends += [
            (piece.at[:, :, pl.ds(0, qkv_width)], qkv.at[z_at]),
            (piece.at[:, pl.ds(0, half), rest], out.at[z_at, :, :, pl.ds(0, width)]),
            (piece.at[:, pl.ds(half, half), rest], out.at[z_at, :, :, pl.ds(width, width)]),
        ]
    copies = [pltpu.make_async_copy(a, b, sems.at[i]) for i, (a, b) in enumerate(ends)]
    for copy in copies:
        copy.start()
    for copy in copies:
        copy.wait()


def place(offsets, z, pieces):
    x_count, rows, columns = pieces[0].shape
    qkv_width = QUERY_WIDTH + 2 * KEY_WIDTH
    z_count, out_width = len(pieces), 2 * (columns - qkv_width)
    shapes = [(z_count, x_count, rows, qkv_width), (z_count, x_count, rows // 2, out_width)]
    wqkv, wout = pl.pallas_call(
        functools.partial(place_kernel, offsets),
        out_shape=[jax.ShapeDtypeStruct(shape, BF16) for shape in shapes],
        in_specs=[pl.BlockSpec(memory_space=pltpu.SMEM)]
        + [pl.BlockSpec(memory_space=pl.ANY)] * len(pieces),
        out_specs=[pl.BlockSpec(memory_space=pltpu.VMEM)] * len(shapes),
        scratch_shapes=[pltpu.SemaphoreType.DMA((3 * len(offsets),))],
        compiler_params=pltpu.CompilerParams(vmem_limit_bytes=VMEM_LIMIT),
    )(z.astype(jnp.int32).reshape(1), *pieces)
    all_rows = z_count * x_count * rows
    return wqkv.reshape(all_rows, qkv_width), wout.reshape(all_rows // 2, out_width)


def call(kernel, outs, args):
    return pl.pallas_call(
        kernel,
        out_shape=[jax.ShapeDtypeStruct(shape, dtype) for shape, dtype in outs],
        in_specs=[pl.BlockSpec(memory_space=pltpu.VMEM)] * len(args),
        out_specs=[pl.BlockSpec(memory_space=pltpu.VMEM)] * len(outs),
        compiler_params=pltpu.CompilerParams(vmem_limit_bytes=VMEM_LIMIT),
    )(*args)


def step(kernel, section, arrived, fixed, read, kept):
    args = (section, arrived, *fixed, *read, *kept)
    outs = [arrived, *kept]
    first_kept = len(args) - len(kept)
    made = pl.pallas_call(
        kernel,
        out_shape=[jax.ShapeDtypeStruct(t.shape, t.dtype) for t in outs],
        in_specs=[pl.BlockSpec(memory_space=pltpu.SMEM)]
        + [pl.BlockSpec(memory_space=pltpu.VMEM)] * (len(args) - 1),
        out_specs=[pl.BlockSpec(memory_space=pltpu.VMEM)] * len(outs),
        input_output_aliases={first_kept + i: 1 + i for i in range(len(kept))},
        compiler_params=pltpu.CompilerParams(vmem_limit_bytes=VMEM_LIMIT),
    )(*args)
    return made[0], tuple(made[1:])


def z_route(replicas, distance):
    return [(i, (i + distance * X_CHIPS) % replicas) for i in range(replicas)]


def x_route(replicas, distance):
    return [
        (i, i // X_CHIPS * X_CHIPS + (i % X_CHIPS + distance) % X_CHIPS) for i in range(replicas)
    ]


def gather_shards(shard, replica, replicas):
    rows, columns = shard.shape
    z_count = replicas // X_CHIPS
    x = replica % X_CHIPS
    along_z = functools.partial(z_route, replicas)
    along_x = functools.partial(x_route, replicas)
    far = lax.ppermute(shard, "dp", along_x(2))
    right = lax.ppermute(shard, "dp", along_x(1))
    left = lax.ppermute(shard, "dp", along_x(-1))
    line = jnp.zeros((X_CHIPS, rows, columns), shard.dtype)
    for turn, data in ((0, shard), (-1, right), (1, left), (2, far)):
        line = lax.dynamic_update_slice(line, data[None], ((x + turn) % X_CHIPS, 0, 0))
    ahead = behind = line
    pieces = [(0, line)]
    late = None
    middle = X_CHIPS // 2
    for step in range(1, z_count // 2):
        ahead = lax.ppermute(ahead, "dp", along_z(1))
        behind = lax.ppermute(behind, "dp", along_z(-1))
        pieces += [(-step, ahead), (step, behind)]
        if step == LATE_ROUND:
            late = ahead
    upper = lax.ppermute(ahead[:middle], "dp", along_z(1))
    lower = lax.ppermute(behind[middle:], "dp", along_z(-1))
    pieces.append((z_count // 2, jnp.concatenate([upper, lower], axis=0)))
    return pieces, late


def sum_over_replicas(parts, replicas):
    count, rows, columns = parts.shape

    def swap(t, mask):
        return lax.ppermute(t, "dp", [(i, i ^ mask) for i in range(replicas)])

    def add(t, other):
        return (t.astype(F32) + other.astype(F32)).astype(BF16)

    lines = [list(range(i, i + X_CHIPS)) for i in range(0, replicas, X_CHIPS)]

    def trade(t):
        return lax.all_to_all(t, "dp", 0, 0, axis_index_groups=lines, tiled=True)

    total = jnp.sum(trade(parts).astype(F32), axis=0).astype(BF16)
    mask = X_CHIPS
    while 2 * mask < replicas:
        total = add(total, swap(total, mask))
        mask *= 2
    route = [(i, replicas - X_CHIPS - i // X_CHIPS * X_CHIPS + i % X_CHIPS) for i in range(replicas)]
    total = add(total, lax.ppermute(total, "dp", route))
    whole = trade(jnp.broadcast_to(total[None], parts.shape)).astype(F32)
    return whole.transpose(1, 0, 2).reshape(rows, count * columns)


def exchange_tokens(source_tokens, send_counts, replica, replicas, section, sections, stream_count, late):
    slot_count = source_tokens.shape[0] // replicas
    width = source_tokens.shape[1] // sections
    share = lax.dynamic_slice_in_dim(source_tokens, section * width, width, 1)
    share, _ = lax.optimization_barrier((share, late))
    sent_counts = lax.dynamic_index_in_dim(send_counts, replica, 0, keepdims=False)
    send_start = jnp.cumsum(sent_counts) - sent_counts
    slot_ids = jnp.arange(slot_count, dtype=jnp.int32)
    occupied = slot_ids[None, :] < sent_counts[:, None]
    pick_rows = jnp.where(occupied, send_start[:, None] + slot_ids[None, :], -1).reshape(-1)
    own_rows = jnp.arange(source_tokens.shape[0], dtype=jnp.int32)
    choose = (pick_rows[:, None] == own_rows[None, :]).astype(BF16)
    packed = dot(choose, share).astype(BF16).reshape(replicas, slot_count, width)
    arrived = lax.all_to_all(packed, "dp", split_axis=0, concat_axis=0, tiled=True)
    incoming = lax.dynamic_index_in_dim(send_counts, replica, 1, keepdims=False)
    end_rows = jnp.cumsum(incoming)
    starts = end_rows - incoming
    places = jnp.arange(stream_count, dtype=jnp.int32)
    slot_place = starts[:, None] + slot_ids[None, :]
    slot_place = jnp.where(slot_ids[None, :] < incoming[:, None], slot_place, -1).reshape(-1)
    choose = (places[:, None] == slot_place[None, :]).astype(BF16)
    stream = dot(choose, arrived.reshape(replicas * slot_count, width)).astype(BF16)
    reach = 1
    while reach < sections:
        route = [(i + reach, i) for i in range(0, sections, 2 * reach)]
        stream = jnp.concatenate([stream, lax.ppermute(stream, "section", route)], axis=1)
        reach *= 2
    return stream, places < end_rows[replicas - 1]


def layout(segments, filled):
    micro_count, token_count = segments.shape
    tokens = micro_count * token_count
    segment = segments.reshape(tokens)
    places = jnp.arange(tokens, dtype=jnp.int32)
    sequence = places // token_count
    same = (segment[:, None] == segment[None, :]) & (sequence[:, None] == sequence[None, :])
    before = places[None, :] < places[:, None]
    position = jnp.sum(jnp.where(same & before, 1.0, 0.0).astype(F32), axis=1)
    alone = places[None, :] == places[:, None]
    allowed = (before & same & filled[:, None] & filled[None, :]) | alone
    half = HEAD_SIZE // 2
    frequency = ROPE_BASE ** (-2.0 * jnp.arange(half, dtype=F32) / HEAD_SIZE)
    angles = position[:, None] * frequency[None, :]
    cosine, sine = jnp.cos(angles), jnp.sin(angles)
    heads = LANES // HEAD_SIZE
    return (
        jnp.concatenate([cosine, cosine] * heads, axis=1),
        jnp.concatenate([-sine, sine] * heads, axis=1),
        allowed.astype(F32),
    )


def local(
    source_tokens,
    send_counts,
    doc_segments,
    out_cotangent,
    norm_gain,
    query_weight,
    frozen_key_matrix,
    frozen_value_matrix,
    out_weight,
    adapter_down,
    adapter_up_maps,
):
    replicas = lax.axis_size("dp")
    sections = lax.axis_size("section")
    replica = lax.axis_index("dp")
    section = lax.axis_index("section")
    features = source_tokens.shape[1]
    tokens = doc_segments.shape[0] * doc_segments.shape[1]

    half = out_weight.shape[2] // 2
    out_rows = jnp.concatenate([out_weight[0, :, :half], out_weight[0, :, half:]], axis=0)
    shard = jnp.concatenate(
        [query_weight[0], frozen_key_matrix[0], frozen_value_matrix[0], out_rows], axis=1
    )
    shards, late = gather_shards(shard, replica, replicas)
    stream, filled = exchange_tokens(
        source_tokens, send_counts, replica, replicas, section, sections, tokens, late
    )
    cosine, sine, allowed = layout(doc_segments, filled)
    gain = norm_gain[0].reshape(1, features)
    tables = jnp.stack([cosine, sine, allowed])
    down = adapter_down[0].transpose(0, 2, 1).reshape(2 * RANK, features)
    up = adapter_up_maps[0]
    up = jnp.concatenate(
        [
            jnp.pad(up[:, :QUERY_WIDTH], ((0, RANK), (0, 0))),
            jnp.pad(up[:, QUERY_WIDTH:], ((RANK, 0), (0, 0))),
        ],
        axis=1,
    )

    saved_shapes = [
        ((tokens, features), BF16),
        ((tokens, QUERY_WIDTH), BF16),
        ((tokens, KEY_WIDTH), BF16),
        ((tokens, KEY_WIDTH), BF16),
        ((tokens, QUERY_HEADS * tokens), BF16),
        ((tokens, 2 * RANK), BF16),
        ((tokens, features), BF16),
    ]
    stream, tables, gain, down, up, *pieces = lax.optimization_barrier(
        (stream, tables, gain, down, up, *[data for _, data in shards])
    )
    wqkv, wout = place([offset for offset, _ in shards], replica // X_CHIPS, pieces)
    fixed = (tables, gain, down, up, wqkv, wout)
    has_turn = section.astype(jnp.int32).reshape(1)
    x = stream
    saved = tuple(jnp.zeros(shape, dtype) for shape, dtype in saved_shapes)
    turned = turn_weights(lambda at: at != 0, has_turn, fixed[4:])
    for turn in range(sections):
        if turn == 2:
            turned = turn_weights(lambda at: at == 0, has_turn, fixed[4:], turned)
        last = turn + 1 == sections
        kernel = functools.partial(forward_kernel, turn, last)
        y, saved = step(kernel, has_turn, x, fixed, (), saved)
        if not last:
            x = lax.ppermute(y, "section", [(turn, turn + 1)])

    held, (low, normed) = saved[:5], saved[5:]
    c = out_cotangent
    kept = (
        jnp.zeros((tokens, QUERY_WIDTH), BF16),
        jnp.zeros((tokens, KEY_WIDTH), BF16),
        jnp.zeros((tokens, 2 * RANK), BF16),
    )
    for turn in range(sections - 1, -1, -1):
        kernel = functools.partial(backward_kernel, turn, turn == 0)
        if turn > 0:
            back, kept = step(kernel, has_turn, c, (*fixed[:4], *turned), held, kept)
        else:
            back, kept = step(kernel, has_turn, c, (tables, up, turned[1]), held[2:], kept)
        if turn > 0:
            c = lax.ppermute(back, "section", [(turn, turn - 1)])

    (grads,) = call(
        grads_kernel,
        [((X_CHIPS, 3 * RANK, features // X_CHIPS), BF16)],
        (normed, low, kept[0], kept[1], kept[2]),
    )
    grads = sum_over_replicas(grads, replicas)
    down_grads = grads[: 2 * RANK].reshape(2, RANK, features).transpose(0, 2, 1)
    up_grads = grads[2 * RANK :, : QUERY_WIDTH + KEY_WIDTH]
    return (down_grads[None], up_grads[None])


def solution(mesh):
    placed = (
        P("dp", None),
        P(),
        P("dp", None),
        P("dp", None),
        P("section", None),
        P("section", "dp", None),
        P("section", "dp", None),
        P("section", "dp", None),
        P("section", "dp", None),
        P("section", None, None, None),
        P("section", None, None),
    )
    return jax.shard_map(
        local,
        mesh=mesh,
        in_specs=placed,
        out_specs=(P("section", None, None, None), P("section", None, None)),
        check_vma=False,
    )
```

```python
import functools

import jax
import jax.numpy as jnp
from jax import lax
from jax.experimental import pallas as pl
from jax.experimental.pallas import tpu as pltpu
from jax.sharding import PartitionSpec as P

QUERY_HEADS = 16
KEY_VALUE_HEADS = 4
GROUP = QUERY_HEADS // KEY_VALUE_HEADS
HEAD_SIZE = 64
QUERY_WIDTH = QUERY_HEADS * HEAD_SIZE
KEY_WIDTH = KEY_VALUE_HEADS * HEAD_SIZE
RANK = 16
LANES = 128

ROPE_BASE = 500000.0
ADAPTER_SCALE = 2.0
NORM_EPS = 1e-05
SCORE_SCALE = HEAD_SIZE ** (-0.5)

X_CHIPS = 4
SUM_GROUP = 16

F32 = jnp.float32
BF16 = jnp.bfloat16
VMEM_LIMIT = 24 * 1024 * 1024
LATE_ROUND = 2
PLACE_ROUND = 5


def dot(a, b):
    return jnp.dot(a, b, preferred_element_type=F32)


def dot_nt(a, b):
    return lax.dot_general(a, b, (((1,), (1,)), ((), ())), preferred_element_type=F32)


def dot_tn(a, b):
    return lax.dot_general(a, b, (((0,), (0,)), ((), ())), preferred_element_type=F32)


def lanes_of(rows, width):
    return lax.broadcasted_iota(jnp.int32, (rows, width), 1)


def rope(t, cosine, signed_sine):
    rows, width = t.shape
    copies = width // LANES
    wide_cos = jnp.concatenate([cosine] * copies, axis=1)
    wide_sin = jnp.concatenate([signed_sine] * copies, axis=1)
    half = HEAD_SIZE // 2
    leading = (lanes_of(rows, width) % HEAD_SIZE) < half
    partner = jnp.where(leading, pltpu.roll(t, width - half, 1), pltpu.roll(t, half, 1))
    return t * wide_cos + partner * wide_sin


def expand(turned, head):
    rows, width = turned[0].shape
    block = lanes_of(rows, width) // HEAD_SIZE
    zero = jnp.zeros((), turned[0].dtype)
    parts = [
        jnp.where(block == g, turned[(g - head) % KEY_VALUE_HEADS], zero) for g in range(GROUP)
    ]
    return jnp.concatenate(parts, axis=0)


def turns_of(t):
    width = t.shape[1]
    wide = t.astype(F32)
    return [t] + [
        pltpu.roll(wide, j * HEAD_SIZE, 1).astype(t.dtype) for j in range(1, KEY_VALUE_HEADS)
    ]


def fold(products):
    rows = products[0].shape[0] // GROUP
    width = products[0].shape[1]
    block = lanes_of(rows, width) // HEAD_SIZE
    total = None
    for h, product in enumerate(products):
        diagonal = None
        for g in range(GROUP):
            part = jnp.where(block == g, product[g * rows : (g + 1) * rows], 0.0)
            diagonal = part if diagonal is None else diagonal + part
        pair = diagonal + pltpu.roll(diagonal, HEAD_SIZE, 1)
        whole = pair + pltpu.roll(pair, 2 * HEAD_SIZE, 1)
        kept = jnp.where(block == h, whole, 0.0)
        total = kept if total is None else total + kept
    return total


def load(copies):
    for copy in copies:
        copy.start()


def forward_kernel(turn, last, turn_ref, x_ref, *refs):
    fixed, y_ref, kept = refs[:6], refs[13], refs[14:21]

    @pl.when(turn_ref[0] == turn)
    def _():
        forward_step(last, x_ref, *fixed, y_ref, *kept)


def forward_step(
    last,
    x_ref, tables, gain, down, up, wqkv, wout,
    y_ref, kept_x_ref, q_ref, k_ref, v_ref, p_ref, low_ref, n_ref,
):
    width = GROUP * HEAD_SIZE
    head_at = [slice(h * width, (h + 1) * width) for h in range(KEY_VALUE_HEADS)]
    cosine, sine = tables[0], tables[1]
    allowed = tables[2] > 0.0
    x = x_ref[...]
    kept_x_ref[...] = x
    hidden = x.astype(F32)
    energy = jnp.mean(hidden * hidden, axis=-1, keepdims=True)
    n = (hidden * lax.rsqrt(energy + NORM_EPS) * gain[...]).astype(BF16)
    n_ref[...] = n
    low = dot_nt(n, down[...]).astype(BF16)
    low_ref[...] = low
    kv = dot(n, wqkv[:, QUERY_WIDTH:])
    k = rope(kv[:, :KEY_WIDTH], cosine, sine).astype(BF16)
    k_ref[...] = k
    v = kv[:, KEY_WIDTH:] + ADAPTER_SCALE * dot(low, up[:, QUERY_WIDTH:])
    v = v.astype(BF16)
    v_ref[...] = v
    k_turns, v_turns = turns_of(k), turns_of(v)
    tokens = hidden.shape[0]
    blended = []
    for h, at in enumerate(head_at):
        q = dot(n, wqkv[:, at]) + ADAPTER_SCALE * dot(low, up[:, at])
        q = rope(q, cosine, sine).astype(BF16)
        q_ref[:, at] = q
        scores = dot_nt(q, expand(k_turns, h)) * SCORE_SCALE
        shares = []
        for g in range(GROUP):
            weights = jnp.where(allowed, jnp.exp(scores[:, g * tokens : (g + 1) * tokens]), 0.0)
            shares.append((weights / jnp.sum(weights, axis=-1, keepdims=True)).astype(BF16))
        shares = jnp.concatenate(shares, axis=1)
        p_ref[:, h * GROUP * tokens : (h + 1) * GROUP * tokens] = shares
        if not last:
            blended.append(dot(shares, expand(v_turns, h)).astype(BF16))
    if not last:
        y_ref[...] = (hidden + dot(jnp.concatenate(blended, axis=1), wout[...])).astype(BF16)


def backward_kernel(turn, first, turn_ref, c_ref, *refs):
    out_ref, kept = refs[-4], refs[-3:]

    @pl.when(turn_ref[0] == turn)
    def _():
        if first:
            tables, up, wout, k_ref, v_ref, p_ref = refs[:6]
            fixed, held = (tables, None, None, up, None, wout), (None, None, k_ref, v_ref, p_ref)
        else:
            fixed, held = refs[:6], refs[6:11]
        backward_step(first, c_ref, *fixed, *held, out_ref, *kept)


def backward_step(
    first,
    c_ref, tables, gain, down, up, wqkv, wout,
    x_ref, q_ref, k_ref, v_ref, p_ref,
    out_ref, dq_ref, dv_ref, dlow_ref,
):
    width = GROUP * HEAD_SIZE
    head_at = [slice(h * width, (h + 1) * width) for h in range(KEY_VALUE_HEADS)]
    cosine, sine = tables[0], tables[1]
    k_turns, v_turns = turns_of(k_ref[...]), turns_of(v_ref[...])
    c = c_ref[...]
    tokens = c.shape[0]
    dn = None
    dlow = None
    dk_products, dv_products = [], []
    for h, at in enumerate(head_at):
        dblended = dot(c, wout[:, at]).astype(BF16)
        shares = p_ref[:, h * GROUP * tokens : (h + 1) * GROUP * tokens]
        dshares = dot_nt(dblended, expand(v_turns, h))
        dscores = []
        for g in range(GROUP):
            span = slice(g * tokens, (g + 1) * tokens)
            p = shares[:, span].astype(F32)
            dp = dshares[:, span]
            pdp = p * dp
            dscores.append(
                ((pdp - p * jnp.sum(pdp, axis=-1, keepdims=True)) * SCORE_SCALE).astype(BF16)
            )
        dscores = jnp.concatenate(dscores, axis=1)
        dq = dot(dscores, expand(k_turns, h))
        dq = rope(dq, cosine, -sine).astype(BF16)
        dq_ref[:, at] = dq
        part = dot_nt(dq, up[:, at])
        dlow = part if dlow is None else dlow + part
        dv_products.append(dot_tn(shares, dblended))
        if not first:
            dk_products.append(dot_tn(dscores, q_ref[:, at]))
            part = dot(dq, wqkv[at, :])
            dn = part if dn is None else dn + part
    dv = fold(dv_products).astype(BF16)
    dv_ref[...] = dv
    dlow = (ADAPTER_SCALE * (dlow + dot_nt(dv, up[:, QUERY_WIDTH:]))).astype(BF16)
    dlow_ref[...] = dlow
    if first:
        return
    dk = rope(fold(dk_products), cosine, -sine).astype(BF16)
    dn = dn + dot(jnp.concatenate([dk, dv], axis=1), wqkv[QUERY_WIDTH:, :])
    dn = dn + dot(dlow, down[...])
    hidden = x_ref[...].astype(F32)
    energy = jnp.mean(hidden * hidden, axis=-1, keepdims=True)
    scale = lax.rsqrt(energy + NORM_EPS)
    dy = dn * gain[...]
    along = jnp.mean(hidden * dy, axis=-1, keepdims=True)
    dh = scale * dy - hidden * (scale * scale * scale * along)
    out_ref[...] = (c.astype(F32) + dh).astype(BF16)


def turn_kernel(act, turn_ref, wqkv, wout, *refs):
    wqkv_turned, wout_turned = refs[-2:]

    @pl.when(act(turn_ref[0]))
    def _():
        wqkv_turned[...] = wqkv[...].T
        wout_turned[...] = wout[...].T


def turn_weights(act, section, weights, kept=()):
    return pl.pallas_call(
        functools.partial(turn_kernel, act),
        out_shape=[jax.ShapeDtypeStruct(t.shape[::-1], t.dtype) for t in weights],
        in_specs=[pl.BlockSpec(memory_space=pltpu.SMEM)]
        + [pl.BlockSpec(memory_space=pltpu.VMEM)] * (len(weights) + len(kept)),
        out_specs=[pl.BlockSpec(memory_space=pltpu.VMEM)] * len(weights),
        input_output_aliases={1 + len(weights) + i: i for i in range(len(kept))},
        compiler_params=pltpu.CompilerParams(vmem_limit_bytes=VMEM_LIMIT),
    )(section, *weights, *kept)


def grads_kernel(n_ref, low_ref, dq_ref, dv_ref, dlow_ref, g_ref):
    part = g_ref.shape[2]
    down = dot_tn(dlow_ref[...], n_ref[...]).astype(BF16)
    low = low_ref[...]
    up_q = ADAPTER_SCALE * dot_tn(low, dq_ref[...])[:RANK]
    up_v = ADAPTER_SCALE * dot_tn(low, dv_ref[...])[RANK : 2 * RANK]
    spare = jnp.zeros((RANK, g_ref.shape[0] * part - QUERY_WIDTH - KEY_WIDTH), F32)
    up = jnp.concatenate([up_q, up_v, spare], axis=1).astype(BF16)
    for i in range(g_ref.shape[0]):
        at = slice(i * part, (i + 1) * part)
        g_ref[i, 0 : 2 * RANK, :] = down[:, at]
        g_ref[i, 2 * RANK : 3 * RANK, :] = up[:, at]


def place_kernel(offsets, at_ref, *refs):
    qkv, out, sems = refs[-3:]
    z_count, _, rows, qkv_width = qkv.shape
    half, width = rows // 2, out.shape[3] // 2
    rest = pl.ds(qkv_width, width)
    ends = []
    for piece, offset in zip(refs, offsets):
        z_at = lax.rem(at_ref[0] + (offset + z_count), z_count)
        ends += [
            (piece.at[:, :, pl.ds(0, qkv_width)], qkv.at[z_at]),
            (piece.at[:, pl.ds(0, half), rest], out.at[z_at, :, :, pl.ds(0, width)]),
            (piece.at[:, pl.ds(half, half), rest], out.at[z_at, :, :, pl.ds(width, width)]),
        ]
    copies = [pltpu.make_async_copy(a, b, sems.at[i]) for i, (a, b) in enumerate(ends)]
    for copy in copies:
        copy.start()
    for copy in copies:
        copy.wait()


def place(offsets, z, pieces, z_count, kept=()):
    x_count, rows, columns = pieces[0].shape
    qkv_width = QUERY_WIDTH + 2 * KEY_WIDTH
    shapes = [
        (z_count, x_count, rows, qkv_width),
        (z_count, x_count, rows // 2, 2 * (columns - qkv_width)),
    ]
    first_kept = 1 + len(pieces)
    return pl.pallas_call(
        functools.partial(place_kernel, offsets),
        out_shape=[jax.ShapeDtypeStruct(shape, BF16) for shape in shapes],
        in_specs=[pl.BlockSpec(memory_space=pltpu.SMEM)]
        + [pl.BlockSpec(memory_space=pl.ANY)] * len(pieces)
        + [pl.BlockSpec(memory_space=pltpu.VMEM)] * len(kept),
        out_specs=[pl.BlockSpec(memory_space=pltpu.VMEM)] * len(shapes),
        scratch_shapes=[pltpu.SemaphoreType.DMA((3 * len(offsets),))],
        input_output_aliases={first_kept + i: i for i in range(len(kept))},
        compiler_params=pltpu.CompilerParams(vmem_limit_bytes=VMEM_LIMIT),
    )(z.astype(jnp.int32).reshape(1), *pieces, *kept)


def call(kernel, outs, args):
    return pl.pallas_call(
        kernel,
        out_shape=[jax.ShapeDtypeStruct(shape, dtype) for shape, dtype in outs],
        in_specs=[pl.BlockSpec(memory_space=pltpu.VMEM)] * len(args),
        out_specs=[pl.BlockSpec(memory_space=pltpu.VMEM)] * len(outs),
        compiler_params=pltpu.CompilerParams(vmem_limit_bytes=VMEM_LIMIT),
    )(*args)


def step(kernel, section, arrived, fixed, read, kept):
    args = (section, arrived, *fixed, *read, *kept)
    outs = [arrived, *kept]
    first_kept = len(args) - len(kept)
    made = pl.pallas_call(
        kernel,
        out_shape=[jax.ShapeDtypeStruct(t.shape, t.dtype) for t in outs],
        in_specs=[pl.BlockSpec(memory_space=pltpu.SMEM)]
        + [pl.BlockSpec(memory_space=pltpu.VMEM)] * (len(args) - 1),
        out_specs=[pl.BlockSpec(memory_space=pltpu.VMEM)] * len(outs),
        input_output_aliases={first_kept + i: 1 + i for i in range(len(kept))},
        compiler_params=pltpu.CompilerParams(vmem_limit_bytes=VMEM_LIMIT),
    )(*args)
    return made[0], tuple(made[1:])


def z_route(replicas, distance):
    return [(i, (i + distance * X_CHIPS) % replicas) for i in range(replicas)]


def x_route(replicas, distance):
    return [
        (i, i // X_CHIPS * X_CHIPS + (i % X_CHIPS + distance) % X_CHIPS) for i in range(replicas)
    ]


def gather_shards(shard, replica, replicas):
    rows, columns = shard.shape
    z_count = replicas // X_CHIPS
    x = replica % X_CHIPS
    along_z = functools.partial(z_route, replicas)
    along_x = functools.partial(x_route, replicas)
    far = lax.ppermute(shard, "dp", along_x(2))
    right = lax.ppermute(shard, "dp", along_x(1))
    left = lax.ppermute(shard, "dp", along_x(-1))
    line = jnp.zeros((X_CHIPS, rows, columns), shard.dtype)
    for turn, data in ((0, shard), (-1, right), (1, left), (2, far)):
        line = lax.dynamic_update_slice(line, data[None], ((x + turn) % X_CHIPS, 0, 0))
    ahead = behind = line
    pieces = [(0, line)]
    late = None
    middle = X_CHIPS // 2
    for step in range(1, z_count // 2):
        ahead = lax.ppermute(ahead, "dp", along_z(1))
        behind = lax.ppermute(behind, "dp", along_z(-1))
        pieces += [(-step, ahead), (step, behind)]
        if step == LATE_ROUND:
            late = ahead
        if step == PLACE_ROUND:
            early = [data for _, data in pieces]
            placed = place([offset for offset, _ in pieces], replica // X_CHIPS, early, z_count)
            pieces = []
        if step == PLACE_ROUND + 1:
            ahead, behind, *placed = lax.optimization_barrier((ahead, behind, *placed))
    upper = lax.ppermute(ahead[:middle], "dp", along_z(1))
    lower = lax.ppermute(behind[middle:], "dp", along_z(-1))
    pieces.append((z_count // 2, jnp.concatenate([upper, lower], axis=0)))
    return pieces, placed, late


def sum_over_replicas(parts, replicas):
    count, rows, columns = parts.shape
    blocks = replicas // count
    groups = [list(range(i, i + count)) for i in range(0, replicas, count)]

    def trade(t):
        return lax.all_to_all(t, "dp", 0, 0, axis_index_groups=groups, tiled=True)

    total = jnp.sum(trade(parts).astype(F32), axis=0).astype(BF16)
    for pair in (lambda block: block ^ 1, lambda block: blocks - 1 - block):
        route = [(i, pair(i // count) * count + i % count) for i in range(replicas)]
        other = lax.ppermute(total, "dp", route)
        total = (total.astype(F32) + other.astype(F32)).astype(BF16)
    whole = trade(jnp.broadcast_to(total[None], parts.shape)).astype(F32)
    return whole.transpose(1, 0, 2).reshape(rows, count * columns)


def exchange_tokens(source_tokens, send_counts, replica, replicas, section, sections, stream_count, late):
    slot_count = source_tokens.shape[0] // replicas
    width = source_tokens.shape[1] // sections
    share = lax.dynamic_slice_in_dim(source_tokens, section * width, width, 1)
    share, _ = lax.optimization_barrier((share, late))
    sent_counts = lax.dynamic_index_in_dim(send_counts, replica, 0, keepdims=False)
    send_start = jnp.cumsum(sent_counts) - sent_counts
    slot_ids = jnp.arange(slot_count, dtype=jnp.int32)
    occupied = slot_ids[None, :] < sent_counts[:, None]
    pick_rows = jnp.where(occupied, send_start[:, None] + slot_ids[None, :], -1).reshape(-1)
    own_rows = jnp.arange(source_tokens.shape[0], dtype=jnp.int32)
    choose = (pick_rows[:, None] == own_rows[None, :]).astype(BF16)
    packed = dot(choose, share).astype(BF16).reshape(replicas, slot_count, width)
    arrived = lax.all_to_all(packed, "dp", split_axis=0, concat_axis=0, tiled=True)
    incoming = lax.dynamic_index_in_dim(send_counts, replica, 1, keepdims=False)
    end_rows = jnp.cumsum(incoming)
    starts = end_rows - incoming
    places = jnp.arange(stream_count, dtype=jnp.int32)
    slot_place = starts[:, None] + slot_ids[None, :]
    slot_place = jnp.where(slot_ids[None, :] < incoming[:, None], slot_place, -1).reshape(-1)
    choose = (places[:, None] == slot_place[None, :]).astype(BF16)
    stream = dot(choose, arrived.reshape(replicas * slot_count, width)).astype(BF16)
    reach = 1
    while reach < sections:
        route = [(i + reach, i) for i in range(0, sections, 2 * reach)]
        stream = jnp.concatenate([stream, lax.ppermute(stream, "section", route)], axis=1)
        reach *= 2
    return stream, places < end_rows[replicas - 1]


def layout(segments, filled):
    micro_count, token_count = segments.shape
    tokens = micro_count * token_count
    segment = segments.reshape(tokens)
    places = jnp.arange(tokens, dtype=jnp.int32)
    sequence = places // token_count
    same = (segment[:, None] == segment[None, :]) & (sequence[:, None] == sequence[None, :])
    before = places[None, :] < places[:, None]
    position = jnp.sum(jnp.where(same & before, 1.0, 0.0).astype(F32), axis=1)
    alone = places[None, :] == places[:, None]
    allowed = (before & same & filled[:, None] & filled[None, :]) | alone
    half = HEAD_SIZE // 2
    frequency = ROPE_BASE ** (-2.0 * jnp.arange(half, dtype=F32) / HEAD_SIZE)
    angles = position[:, None] * frequency[None, :]
    cosine, sine = jnp.cos(angles), jnp.sin(angles)
    heads = LANES // HEAD_SIZE
    return (
        jnp.concatenate([cosine, cosine] * heads, axis=1),
        jnp.concatenate([-sine, sine] * heads, axis=1),
        allowed.astype(F32),
    )


def local(
    source_tokens,
    send_counts,
    doc_segments,
    out_cotangent,
    norm_gain,
    query_weight,
    frozen_key_matrix,
    frozen_value_matrix,
    out_weight,
    adapter_down,
    adapter_up_maps,
):
    replicas = lax.axis_size("dp")
    sections = lax.axis_size("section")
    replica = lax.axis_index("dp")
    section = lax.axis_index("section")
    features = source_tokens.shape[1]
    tokens = doc_segments.shape[0] * doc_segments.shape[1]

    half = out_weight.shape[2] // 2
    out_rows = jnp.concatenate([out_weight[0, :, :half], out_weight[0, :, half:]], axis=0)
    shard = jnp.concatenate(
        [query_weight[0], frozen_key_matrix[0], frozen_value_matrix[0], out_rows], axis=1
    )
    shards, placed, late = gather_shards(shard, replica, replicas)
    stream, filled = exchange_tokens(
        source_tokens, send_counts, replica, replicas, section, sections, tokens, late
    )
    cosine, sine, allowed = layout(doc_segments, filled)
    gain = norm_gain[0].reshape(1, features)
    tables = jnp.stack([cosine, sine, allowed])
    down = adapter_down[0].transpose(0, 2, 1).reshape(2 * RANK, features)
    up = adapter_up_maps[0]
    up = jnp.concatenate(
        [
            jnp.pad(up[:, :QUERY_WIDTH], ((0, RANK), (0, 0))),
            jnp.pad(up[:, QUERY_WIDTH:], ((RANK, 0), (0, 0))),
        ],
        axis=1,
    )

    saved_shapes = [
        ((tokens, features), BF16),
        ((tokens, QUERY_WIDTH), BF16),
        ((tokens, KEY_WIDTH), BF16),
        ((tokens, KEY_WIDTH), BF16),
        ((tokens, QUERY_HEADS * tokens), BF16),
        ((tokens, 2 * RANK), BF16),
        ((tokens, features), BF16),
    ]
    stream, tables, gain, down, up, *pieces = lax.optimization_barrier(
        (stream, tables, gain, down, up, *[data for _, data in shards])
    )
    z_count = replicas // X_CHIPS
    offsets = [offset for offset, _ in shards]
    wqkv, wout = place(offsets, replica // X_CHIPS, pieces, z_count, placed)
    wqkv = wqkv.reshape(-1, wqkv.shape[-1])
    wout = wout.reshape(-1, wout.shape[-1])
    fixed = (tables, gain, down, up, wqkv, wout)
    has_turn = section.astype(jnp.int32).reshape(1)
    x = stream
    saved = tuple(jnp.zeros(shape, dtype) for shape, dtype in saved_shapes)
    turned = turn_weights(lambda at: at != 0, has_turn, fixed[4:])
    for turn in range(sections):
        if turn == 2:
            turned = turn_weights(lambda at: at == 0, has_turn, fixed[4:], turned)
        last = turn + 1 == sections
        kernel = functools.partial(forward_kernel, turn, last)
        y, saved = step(kernel, has_turn, x, fixed, (), saved)
        if not last:
            x = lax.ppermute(y, "section", [(turn, turn + 1)])

    held, (low, normed) = saved[:5], saved[5:]
    c = out_cotangent
    kept = (
        jnp.zeros((tokens, QUERY_WIDTH), BF16),
        jnp.zeros((tokens, KEY_WIDTH), BF16),
        jnp.zeros((tokens, 2 * RANK), BF16),
    )
    for turn in range(sections - 1, -1, -1):
        kernel = functools.partial(backward_kernel, turn, turn == 0)
        if turn > 0:
            back, kept = step(kernel, has_turn, c, (*fixed[:4], *turned), held, kept)
        else:
            back, kept = step(kernel, has_turn, c, (tables, up, turned[1]), held[2:], kept)
        if turn > 0:
            c = lax.ppermute(back, "section", [(turn, turn - 1)])

    (grads,) = call(
        grads_kernel,
        [((SUM_GROUP, 3 * RANK, features // SUM_GROUP), BF16)],
        (normed, low, kept[0], kept[1], kept[2]),
    )
    grads = sum_over_replicas(grads, replicas)
    down_grads = grads[: 2 * RANK].reshape(2, RANK, features).transpose(0, 2, 1)
    up_grads = grads[2 * RANK :, : QUERY_WIDTH + KEY_WIDTH]
    return (down_grads[None], up_grads[None])


def solution(mesh):
    placed = (
        P("dp", None),
        P(),
        P("dp", None),
        P("dp", None),
        P("section", None),
        P("section", "dp", None),
        P("section", "dp", None),
        P("section", "dp", None),
        P("section", "dp", None),
        P("section", None, None, None),
        P("section", None, None),
    )
    return jax.shard_map(
        local,
        mesh=mesh,
        in_specs=placed,
        out_specs=(P("section", None, None, None), P("section", None, None)),
        check_vma=False,
    )
```

```python
import functools

import jax
import jax.numpy as jnp
from jax import lax
from jax.experimental import pallas as pl
from jax.experimental.pallas import tpu as pltpu
from jax.sharding import PartitionSpec as P

QUERY_HEADS = 16
KEY_VALUE_HEADS = 4
GROUP = QUERY_HEADS // KEY_VALUE_HEADS
HEAD_SIZE = 64
QUERY_WIDTH = QUERY_HEADS * HEAD_SIZE
KEY_WIDTH = KEY_VALUE_HEADS * HEAD_SIZE
RANK = 16
LANES = 128

ROPE_BASE = 500000.0
ADAPTER_SCALE = 2.0
NORM_EPS = 1e-05
SCORE_SCALE = HEAD_SIZE ** (-0.5)

X_CHIPS = 4
SUM_GROUP = 16

F32 = jnp.float32
BF16 = jnp.bfloat16
VMEM_LIMIT = 24 * 1024 * 1024
LATE_ROUND = 2
PLACE_ROUND = 5


def dot(a, b):
    return jnp.dot(a, b, preferred_element_type=F32)


def dot_nt(a, b):
    return lax.dot_general(a, b, (((1,), (1,)), ((), ())), preferred_element_type=F32)


def dot_tn(a, b):
    return lax.dot_general(a, b, (((0,), (0,)), ((), ())), preferred_element_type=F32)


def lanes_of(rows, width):
    return lax.broadcasted_iota(jnp.int32, (rows, width), 1)


def rope(t, cosine, signed_sine):
    rows, width = t.shape
    copies = width // LANES
    wide_cos = jnp.concatenate([cosine] * copies, axis=1)
    wide_sin = jnp.concatenate([signed_sine] * copies, axis=1)
    half = HEAD_SIZE // 2
    leading = (lanes_of(rows, width) % HEAD_SIZE) < half
    partner = jnp.where(leading, pltpu.roll(t, width - half, 1), pltpu.roll(t, half, 1))
    return t * wide_cos + partner * wide_sin


def expand(turned, head):
    rows, width = turned[0].shape
    block = lanes_of(rows, width) // HEAD_SIZE
    zero = jnp.zeros((), turned[0].dtype)
    parts = [
        jnp.where(block == g, turned[(g - head) % KEY_VALUE_HEADS], zero) for g in range(GROUP)
    ]
    return jnp.concatenate(parts, axis=0)


def turns_of(t):
    width = t.shape[1]
    wide = t.astype(F32)
    return [t] + [
        pltpu.roll(wide, j * HEAD_SIZE, 1).astype(t.dtype) for j in range(1, KEY_VALUE_HEADS)
    ]


def fold(products):
    rows = products[0].shape[0] // GROUP
    width = products[0].shape[1]
    block = lanes_of(rows, width) // HEAD_SIZE
    total = None
    for h, product in enumerate(products):
        diagonal = None
        for g in range(GROUP):
            part = jnp.where(block == g, product[g * rows : (g + 1) * rows], 0.0)
            diagonal = part if diagonal is None else diagonal + part
        pair = diagonal + pltpu.roll(diagonal, HEAD_SIZE, 1)
        whole = pair + pltpu.roll(pair, 2 * HEAD_SIZE, 1)
        kept = jnp.where(block == h, whole, 0.0)
        total = kept if total is None else total + kept
    return total


def load(copies):
    for copy in copies:
        copy.start()


def forward_kernel(turn, last, turn_ref, x_ref, *refs):
    fixed, y_ref, kept = refs[:6], refs[13], refs[14:21]

    @pl.when(turn_ref[0] == turn)
    def _():
        forward_step(last, x_ref, *fixed, y_ref, *kept)


def forward_step(
    last,
    x_ref, tables, gain, down, up, wqkv, wout,
    y_ref, kept_x_ref, q_ref, k_ref, v_ref, p_ref, low_ref, n_ref,
):
    width = GROUP * HEAD_SIZE
    head_at = [slice(h * width, (h + 1) * width) for h in range(KEY_VALUE_HEADS)]
    cosine, sine = tables[0], tables[1]
    allowed = tables[2] > 0.0
    x = x_ref[...]
    kept_x_ref[...] = x
    hidden = x.astype(F32)
    energy = jnp.mean(hidden * hidden, axis=-1, keepdims=True)
    n = (hidden * lax.rsqrt(energy + NORM_EPS) * gain[...]).astype(BF16)
    n_ref[...] = n
    low = dot_nt(n, down[...]).astype(BF16)
    low_ref[...] = low
    kv = dot(n, wqkv[:, QUERY_WIDTH:])
    k = rope(kv[:, :KEY_WIDTH], cosine, sine).astype(BF16)
    k_ref[...] = k
    v = kv[:, KEY_WIDTH:] + ADAPTER_SCALE * dot(low, up[:, QUERY_WIDTH:])
    v = v.astype(BF16)
    v_ref[...] = v
    k_turns, v_turns = turns_of(k), turns_of(v)
    tokens = hidden.shape[0]
    blended = []
    for h, at in enumerate(head_at):
        q = dot(n, wqkv[:, at]) + ADAPTER_SCALE * dot(low, up[:, at])
        q = rope(q, cosine, sine).astype(BF16)
        q_ref[:, at] = q
        scores = dot_nt(q, expand(k_turns, h)) * SCORE_SCALE
        shares = []
        for g in range(GROUP):
            weights = jnp.where(allowed, jnp.exp(scores[:, g * tokens : (g + 1) * tokens]), 0.0)
            shares.append((weights / jnp.sum(weights, axis=-1, keepdims=True)).astype(BF16))
        shares = jnp.concatenate(shares, axis=1)
        p_ref[:, h * GROUP * tokens : (h + 1) * GROUP * tokens] = shares
        if not last:
            blended.append(dot(shares, expand(v_turns, h)).astype(BF16))
    if not last:
        y_ref[...] = (hidden + dot(jnp.concatenate(blended, axis=1), wout[...])).astype(BF16)


def backward_kernel(turn, first, turn_ref, c_ref, *refs):
    out_ref, kept = refs[-4], refs[-3:]

    @pl.when(turn_ref[0] == turn)
    def _():
        if first:
            tables, up, wout, k_ref, v_ref, p_ref = refs[:6]
            fixed, held = (tables, None, None, up, None, wout), (None, None, k_ref, v_ref, p_ref)
        else:
            fixed, held = refs[:6], refs[6:11]
        backward_step(first, c_ref, *fixed, *held, out_ref, *kept)


def backward_step(
    first,
    c_ref, tables, gain, down, up, wqkv, wout,
    x_ref, q_ref, k_ref, v_ref, p_ref,
    out_ref, dq_ref, dv_ref, dlow_ref,
):
    width = GROUP * HEAD_SIZE
    head_at = [slice(h * width, (h + 1) * width) for h in range(KEY_VALUE_HEADS)]
    cosine, sine = tables[0], tables[1]
    k_turns, v_turns = turns_of(k_ref[...]), turns_of(v_ref[...])
    c = c_ref[...]
    tokens = c.shape[0]
    dn = None
    dlow = None
    dk_products, dv_products = [], []
    for h, at in enumerate(head_at):
        dblended = dot(c, wout[:, at]).astype(BF16)
        shares = p_ref[:, h * GROUP * tokens : (h + 1) * GROUP * tokens]
        dshares = dot_nt(dblended, expand(v_turns, h))
        dscores = []
        for g in range(GROUP):
            span = slice(g * tokens, (g + 1) * tokens)
            p = shares[:, span].astype(F32)
            dp = dshares[:, span]
            pdp = p * dp
            dscores.append(
                ((pdp - p * jnp.sum(pdp, axis=-1, keepdims=True)) * SCORE_SCALE).astype(BF16)
            )
        dscores = jnp.concatenate(dscores, axis=1)
        dq = dot(dscores, expand(k_turns, h))
        dq = rope(dq, cosine, -sine).astype(BF16)
        dq_ref[:, at] = dq
        part = dot_nt(dq, up[:, at])
        dlow = part if dlow is None else dlow + part
        dv_products.append(dot_tn(shares, dblended))
        if not first:
            dk_products.append(dot_tn(dscores, q_ref[:, at]))
            part = dot(dq, wqkv[at, :])
            dn = part if dn is None else dn + part
    dv = fold(dv_products).astype(BF16)
    dv_ref[...] = dv
    dlow = (ADAPTER_SCALE * (dlow + dot_nt(dv, up[:, QUERY_WIDTH:]))).astype(BF16)
    dlow_ref[...] = dlow
    if first:
        return
    dk = rope(fold(dk_products), cosine, -sine).astype(BF16)
    dn = dn + dot(jnp.concatenate([dk, dv], axis=1), wqkv[QUERY_WIDTH:, :])
    dn = dn + dot(dlow, down[...])
    hidden = x_ref[...].astype(F32)
    energy = jnp.mean(hidden * hidden, axis=-1, keepdims=True)
    scale = lax.rsqrt(energy + NORM_EPS)
    dy = dn * gain[...]
    along = jnp.mean(hidden * dy, axis=-1, keepdims=True)
    dh = scale * dy - hidden * (scale * scale * scale * along)
    out_ref[...] = (c.astype(F32) + dh).astype(BF16)


def turn_kernel(act, turn_ref, wqkv, wout, *refs):
    wqkv_turned, wout_turned = refs[-2:]

    @pl.when(act(turn_ref[0]))
    def _():
        wqkv_turned[...] = wqkv[...].T
        wout_turned[...] = wout[...].T


def turn_weights(act, section, weights, kept=()):
    return pl.pallas_call(
        functools.partial(turn_kernel, act),
        out_shape=[jax.ShapeDtypeStruct(t.shape[::-1], t.dtype) for t in weights],
        in_specs=[pl.BlockSpec(memory_space=pltpu.SMEM)]
        + [pl.BlockSpec(memory_space=pltpu.VMEM)] * (len(weights) + len(kept)),
        out_specs=[pl.BlockSpec(memory_space=pltpu.VMEM)] * len(weights),
        input_output_aliases={1 + len(weights) + i: i for i in range(len(kept))},
        compiler_params=pltpu.CompilerParams(vmem_limit_bytes=VMEM_LIMIT),
    )(section, *weights, *kept)


def grads_kernel(n_ref, low_ref, dq_ref, dv_ref, dlow_ref, g_ref):
    part = g_ref.shape[2]
    down = dot_tn(dlow_ref[...], n_ref[...]).astype(BF16)
    low = low_ref[...]
    up_q = ADAPTER_SCALE * dot_tn(low, dq_ref[...])[:RANK]
    up_v = ADAPTER_SCALE * dot_tn(low, dv_ref[...])[RANK : 2 * RANK]
    spare = jnp.zeros((RANK, g_ref.shape[0] * part - QUERY_WIDTH - KEY_WIDTH), F32)
    up = jnp.concatenate([up_q, up_v, spare], axis=1).astype(BF16)
    for i in range(g_ref.shape[0]):
        at = slice(i * part, (i + 1) * part)
        g_ref[i, 0 : 2 * RANK, :] = down[:, at]
        g_ref[i, 2 * RANK : 3 * RANK, :] = up[:, at]


def place_kernel(offsets, at_ref, *refs):
    qkv, out, sems = refs[-3:]
    z_count, _, rows, qkv_width = qkv.shape
    half, width = rows // 2, out.shape[3] // 2
    rest = pl.ds(qkv_width, width)
    ends = []
    for piece, offset in zip(refs, offsets):
        z_at = lax.rem(at_ref[0] + (offset + z_count), z_count)
        ends += [
            (piece.at[:, :, pl.ds(0, qkv_width)], qkv.at[z_at]),
            (piece.at[:, pl.ds(0, half), rest], out.at[z_at, :, :, pl.ds(0, width)]),
            (piece.at[:, pl.ds(half, half), rest], out.at[z_at, :, :, pl.ds(width, width)]),
        ]
    copies = [pltpu.make_async_copy(a, b, sems.at[i]) for i, (a, b) in enumerate(ends)]
    for copy in copies:
        copy.start()
    for copy in copies:
        copy.wait()


def place(offsets, z, pieces, z_count, kept=()):
    x_count, rows, columns = pieces[0].shape
    qkv_width = QUERY_WIDTH + 2 * KEY_WIDTH
    shapes = [
        (z_count, x_count, rows, qkv_width),
        (z_count, x_count, rows // 2, 2 * (columns - qkv_width)),
    ]
    first_kept = 1 + len(pieces)
    return pl.pallas_call(
        functools.partial(place_kernel, offsets),
        out_shape=[jax.ShapeDtypeStruct(shape, BF16) for shape in shapes],
        in_specs=[pl.BlockSpec(memory_space=pltpu.SMEM)]
        + [pl.BlockSpec(memory_space=pl.ANY)] * len(pieces)
        + [pl.BlockSpec(memory_space=pltpu.VMEM)] * len(kept),
        out_specs=[pl.BlockSpec(memory_space=pltpu.VMEM)] * len(shapes),
        scratch_shapes=[pltpu.SemaphoreType.DMA((3 * len(offsets),))],
        input_output_aliases={first_kept + i: i for i in range(len(kept))},
        compiler_params=pltpu.CompilerParams(vmem_limit_bytes=VMEM_LIMIT),
    )(z.astype(jnp.int32).reshape(1), *pieces, *kept)


def call(kernel, outs, args):
    return pl.pallas_call(
        kernel,
        out_shape=[jax.ShapeDtypeStruct(shape, dtype) for shape, dtype in outs],
        in_specs=[pl.BlockSpec(memory_space=pltpu.VMEM)] * len(args),
        out_specs=[pl.BlockSpec(memory_space=pltpu.VMEM)] * len(outs),
        compiler_params=pltpu.CompilerParams(vmem_limit_bytes=VMEM_LIMIT),
    )(*args)


def step(kernel, section, arrived, fixed, read, kept):
    args = (section, arrived, *fixed, *read, *kept)
    outs = [arrived, *kept]
    first_kept = len(args) - len(kept)
    made = pl.pallas_call(
        kernel,
        out_shape=[jax.ShapeDtypeStruct(t.shape, t.dtype) for t in outs],
        in_specs=[pl.BlockSpec(memory_space=pltpu.SMEM)]
        + [pl.BlockSpec(memory_space=pltpu.VMEM)] * (len(args) - 1),
        out_specs=[pl.BlockSpec(memory_space=pltpu.VMEM)] * len(outs),
        input_output_aliases={first_kept + i: 1 + i for i in range(len(kept))},
        compiler_params=pltpu.CompilerParams(vmem_limit_bytes=VMEM_LIMIT),
    )(*args)
    return made[0], tuple(made[1:])


def z_route(replicas, distance):
    return [(i, (i + distance * X_CHIPS) % replicas) for i in range(replicas)]


def x_route(replicas, distance):
    return [
        (i, i // X_CHIPS * X_CHIPS + (i % X_CHIPS + distance) % X_CHIPS) for i in range(replicas)
    ]


def gather_shards(shard, replica, replicas):
    rows, columns = shard.shape
    z_count = replicas // X_CHIPS
    x = replica % X_CHIPS
    along_z = functools.partial(z_route, replicas)
    along_x = functools.partial(x_route, replicas)
    far = lax.ppermute(shard, "dp", along_x(2))
    right = lax.ppermute(shard, "dp", along_x(1))
    left = lax.ppermute(shard, "dp", along_x(-1))
    line = jnp.zeros((X_CHIPS, rows, columns), shard.dtype)
    for turn, data in ((0, shard), (-1, right), (1, left), (2, far)):
        line = lax.dynamic_update_slice(line, data[None], ((x + turn) % X_CHIPS, 0, 0))
    ahead = behind = line
    pieces = [(0, line)]
    late = None
    middle = X_CHIPS // 2
    for step in range(1, z_count // 2):
        ahead = lax.ppermute(ahead, "dp", along_z(1))
        behind = lax.ppermute(behind, "dp", along_z(-1))
        pieces += [(-step, ahead), (step, behind)]
        if step == LATE_ROUND:
            late = ahead
        if step == PLACE_ROUND:
            early = [data for _, data in pieces]
            placed = place([offset for offset, _ in pieces], replica // X_CHIPS, early, z_count)
            pieces = []
        if step == PLACE_ROUND + 1:
            ahead, behind, *placed = lax.optimization_barrier((ahead, behind, *placed))
    upper = lax.ppermute(ahead[:middle], "dp", along_z(1))
    lower = lax.ppermute(behind[middle:], "dp", along_z(-1))
    pieces.append((z_count // 2, jnp.concatenate([upper, lower], axis=0)))
    return pieces, placed, late


def sum_over_replicas(parts, replica, replicas):
    count, rows, columns = parts.shape
    blocks = replicas // count
    groups = [list(range(i, i + count)) for i in range(0, replicas, count)]

    def trade(t):
        return lax.all_to_all(t, "dp", 0, 0, axis_index_groups=groups, tiled=True)

    total = jnp.sum(trade(parts).astype(F32), axis=0).astype(BF16)
    came = [total]
    for distance in range(1, blocks):
        route = [(i, (i + distance * count) % replicas) for i in range(replicas)]
        came.insert(0, lax.ppermute(total, "dp", route))
    first = blocks - 1 - replica // count
    ordered = lax.dynamic_slice_in_dim(jnp.stack(came + came), first, blocks, 0)
    total = jnp.sum(ordered.astype(F32), axis=0).astype(BF16)
    whole = trade(jnp.broadcast_to(total[None], parts.shape)).astype(F32)
    return whole.transpose(1, 0, 2).reshape(rows, count * columns)


def exchange_tokens(source_tokens, send_counts, replica, replicas, section, sections, stream_count, late):
    slot_count = source_tokens.shape[0] // replicas
    width = source_tokens.shape[1] // sections
    share = lax.dynamic_slice_in_dim(source_tokens, section * width, width, 1)
    share, _ = lax.optimization_barrier((share, late))
    sent_counts = lax.dynamic_index_in_dim(send_counts, replica, 0, keepdims=False)
    send_start = jnp.cumsum(sent_counts) - sent_counts
    slot_ids = jnp.arange(slot_count, dtype=jnp.int32)
    occupied = slot_ids[None, :] < sent_counts[:, None]
    pick_rows = jnp.where(occupied, send_start[:, None] + slot_ids[None, :], -1).reshape(-1)
    own_rows = jnp.arange(source_tokens.shape[0], dtype=jnp.int32)
    choose = (pick_rows[:, None] == own_rows[None, :]).astype(BF16)
    packed = dot(choose, share).astype(BF16).reshape(replicas, slot_count, width)
    arrived = lax.all_to_all(packed, "dp", split_axis=0, concat_axis=0, tiled=True)
    incoming = lax.dynamic_index_in_dim(send_counts, replica, 1, keepdims=False)
    end_rows = jnp.cumsum(incoming)
    starts = end_rows - incoming
    places = jnp.arange(stream_count, dtype=jnp.int32)
    slot_place = starts[:, None] + slot_ids[None, :]
    slot_place = jnp.where(slot_ids[None, :] < incoming[:, None], slot_place, -1).reshape(-1)
    choose = (places[:, None] == slot_place[None, :]).astype(BF16)
    stream = dot(choose, arrived.reshape(replicas * slot_count, width)).astype(BF16)
    reach = 1
    while reach < sections:
        route = [(i + reach, i) for i in range(0, sections, 2 * reach)]
        stream = jnp.concatenate([stream, lax.ppermute(stream, "section", route)], axis=1)
        reach *= 2
    return stream, places < end_rows[replicas - 1]


def layout(segments, filled):
    micro_count, token_count = segments.shape
    tokens = micro_count * token_count
    segment = segments.reshape(tokens)
    places = jnp.arange(tokens, dtype=jnp.int32)
    sequence = places // token_count
    same = (segment[:, None] == segment[None, :]) & (sequence[:, None] == sequence[None, :])
    before = places[None, :] < places[:, None]
    position = jnp.sum(jnp.where(same & before, 1.0, 0.0).astype(F32), axis=1)
    alone = places[None, :] == places[:, None]
    allowed = (before & same & filled[:, None] & filled[None, :]) | alone
    half = HEAD_SIZE // 2
    frequency = ROPE_BASE ** (-2.0 * jnp.arange(half, dtype=F32) / HEAD_SIZE)
    angles = position[:, None] * frequency[None, :]
    cosine, sine = jnp.cos(angles), jnp.sin(angles)
    heads = LANES // HEAD_SIZE
    return (
        jnp.concatenate([cosine, cosine] * heads, axis=1),
        jnp.concatenate([-sine, sine] * heads, axis=1),
        allowed.astype(F32),
    )


def local(
    source_tokens,
    send_counts,
    doc_segments,
    out_cotangent,
    norm_gain,
    query_weight,
    frozen_key_matrix,
    frozen_value_matrix,
    out_weight,
    adapter_down,
    adapter_up_maps,
):
    replicas = lax.axis_size("dp")
    sections = lax.axis_size("section")
    replica = lax.axis_index("dp")
    section = lax.axis_index("section")
    features = source_tokens.shape[1]
    tokens = doc_segments.shape[0] * doc_segments.shape[1]

    half = out_weight.shape[2] // 2
    out_rows = jnp.concatenate([out_weight[0, :, :half], out_weight[0, :, half:]], axis=0)
    shard = jnp.concatenate(
        [query_weight[0], frozen_key_matrix[0], frozen_value_matrix[0], out_rows], axis=1
    )
    shards, placed, late = gather_shards(shard, replica, replicas)
    stream, filled = exchange_tokens(
        source_tokens, send_counts, replica, replicas, section, sections, tokens, late
    )
    cosine, sine, allowed = layout(doc_segments, filled)
    gain = norm_gain[0].reshape(1, features)
    tables = jnp.stack([cosine, sine, allowed])
    down = adapter_down[0].transpose(0, 2, 1).reshape(2 * RANK, features)
    up = adapter_up_maps[0]
    up = jnp.concatenate(
        [
            jnp.pad(up[:, :QUERY_WIDTH], ((0, RANK), (0, 0))),
            jnp.pad(up[:, QUERY_WIDTH:], ((RANK, 0), (0, 0))),
        ],
        axis=1,
    )

    saved_shapes = [
        ((tokens, features), BF16),
        ((tokens, QUERY_WIDTH), BF16),
        ((tokens, KEY_WIDTH), BF16),
        ((tokens, KEY_WIDTH), BF16),
        ((tokens, QUERY_HEADS * tokens), BF16),
        ((tokens, 2 * RANK), BF16),
        ((tokens, features), BF16),
    ]
    stream, tables, gain, down, up, *pieces = lax.optimization_barrier(
        (stream, tables, gain, down, up, *[data for _, data in shards])
    )
    z_count = replicas // X_CHIPS
    offsets = [offset for offset, _ in shards]
    wqkv, wout = place(offsets, replica // X_CHIPS, pieces, z_count, placed)
    wqkv = wqkv.reshape(-1, wqkv.shape[-1])
    wout = wout.reshape(-1, wout.shape[-1])
    fixed = (tables, gain, down, up, wqkv, wout)
    has_turn = section.astype(jnp.int32).reshape(1)
    x = stream
    saved = tuple(jnp.zeros(shape, dtype) for shape, dtype in saved_shapes)
    turned = turn_weights(lambda at: at != 0, has_turn, fixed[4:])
    for turn in range(sections):
        if turn == 2:
            turned = turn_weights(lambda at: at == 0, has_turn, fixed[4:], turned)
        last = turn + 1 == sections
        kernel = functools.partial(forward_kernel, turn, last)
        y, saved = step(kernel, has_turn, x, fixed, (), saved)
        if not last:
            x = lax.ppermute(y, "section", [(turn, turn + 1)])

    held, (low, normed) = saved[:5], saved[5:]
    c = out_cotangent
    kept = (
        jnp.zeros((tokens, QUERY_WIDTH), BF16),
        jnp.zeros((tokens, KEY_WIDTH), BF16),
        jnp.zeros((tokens, 2 * RANK), BF16),
    )
    for turn in range(sections - 1, -1, -1):
        kernel = functools.partial(backward_kernel, turn, turn == 0)
        if turn > 0:
            back, kept = step(kernel, has_turn, c, (*fixed[:4], *turned), held, kept)
        else:
            back, kept = step(kernel, has_turn, c, (tables, up, turned[1]), held[2:], kept)
        if turn > 0:
            c = lax.ppermute(back, "section", [(turn, turn - 1)])

    (grads,) = call(
        grads_kernel,
        [((SUM_GROUP, 3 * RANK, features // SUM_GROUP), BF16)],
        (normed, low, kept[0], kept[1], kept[2]),
    )
    grads = sum_over_replicas(grads, replica, replicas)
    down_grads = grads[: 2 * RANK].reshape(2, RANK, features).transpose(0, 2, 1)
    up_grads = grads[2 * RANK :, : QUERY_WIDTH + KEY_WIDTH]
    return (down_grads[None], up_grads[None])


def solution(mesh):
    placed = (
        P("dp", None),
        P(),
        P("dp", None),
        P("dp", None),
        P("section", None),
        P("section", "dp", None),
        P("section", "dp", None),
        P("section", "dp", None),
        P("section", "dp", None),
        P("section", None, None, None),
        P("section", None, None),
    )
    return jax.shard_map(
        local,
        mesh=mesh,
        in_specs=placed,
        out_specs=(P("section", None, None, None), P("section", None, None)),
        check_vma=False,
    )
```

```python
import functools

import jax
import jax.numpy as jnp
from jax import lax
from jax.experimental import pallas as pl
from jax.experimental.pallas import tpu as pltpu
from jax.sharding import PartitionSpec as P

QUERY_HEADS = 16
KEY_VALUE_HEADS = 4
GROUP = QUERY_HEADS // KEY_VALUE_HEADS
HEAD_SIZE = 64
QUERY_WIDTH = QUERY_HEADS * HEAD_SIZE
KEY_WIDTH = KEY_VALUE_HEADS * HEAD_SIZE
RANK = 16
LANES = 128

ROPE_BASE = 500000.0
ADAPTER_SCALE = 2.0
NORM_EPS = 1e-05
SCORE_SCALE = HEAD_SIZE ** (-0.5)

X_CHIPS = 4
SUM_GROUP = 16

F32 = jnp.float32
BF16 = jnp.bfloat16
VMEM_LIMIT = 24 * 1024 * 1024
LATE_ROUND = 1
PLACE_ROUND = 5


def dot(a, b):
    return jnp.dot(a, b, preferred_element_type=F32)


def dot_nt(a, b):
    return lax.dot_general(a, b, (((1,), (1,)), ((), ())), preferred_element_type=F32)


def dot_tn(a, b):
    return lax.dot_general(a, b, (((0,), (0,)), ((), ())), preferred_element_type=F32)


def lanes_of(rows, width):
    return lax.broadcasted_iota(jnp.int32, (rows, width), 1)


def rope(t, cosine, signed_sine):
    rows, width = t.shape
    copies = width // LANES
    wide_cos = jnp.concatenate([cosine] * copies, axis=1)
    wide_sin = jnp.concatenate([signed_sine] * copies, axis=1)
    half = HEAD_SIZE // 2
    leading = (lanes_of(rows, width) % HEAD_SIZE) < half
    partner = jnp.where(leading, pltpu.roll(t, width - half, 1), pltpu.roll(t, half, 1))
    return t * wide_cos + partner * wide_sin


def expand(turned, head):
    rows, width = turned[0].shape
    block = lanes_of(rows, width) // HEAD_SIZE
    zero = jnp.zeros((), turned[0].dtype)
    parts = [
        jnp.where(block == g, turned[(g - head) % KEY_VALUE_HEADS], zero) for g in range(GROUP)
    ]
    return jnp.concatenate(parts, axis=0)


def turns_of(t):
    width = t.shape[1]
    wide = t.astype(F32)
    return [t] + [
        pltpu.roll(wide, j * HEAD_SIZE, 1).astype(t.dtype) for j in range(1, KEY_VALUE_HEADS)
    ]


def fold(products):
    rows = products[0].shape[0] // GROUP
    width = products[0].shape[1]
    block = lanes_of(rows, width) // HEAD_SIZE
    total = None
    for h, product in enumerate(products):
        diagonal = None
        for g in range(GROUP):
            part = jnp.where(block == g, product[g * rows : (g + 1) * rows], 0.0)
            diagonal = part if diagonal is None else diagonal + part
        pair = diagonal + pltpu.roll(diagonal, HEAD_SIZE, 1)
        whole = pair + pltpu.roll(pair, 2 * HEAD_SIZE, 1)
        kept = jnp.where(block == h, whole, 0.0)
        total = kept if total is None else total + kept
    return total


def load(copies):
    for copy in copies:
        copy.start()


def forward_kernel(turn, last, turn_ref, x_ref, *refs):
    fixed, y_ref, kept = refs[:6], refs[13], refs[14:21]

    @pl.when(turn_ref[0] == turn)
    def _():
        forward_step(last, x_ref, *fixed, y_ref, *kept)


def forward_step(
    last,
    x_ref, tables, gain, down, up, wqkv, wout,
    y_ref, kept_x_ref, q_ref, k_ref, v_ref, p_ref, low_ref, n_ref,
):
    width = GROUP * HEAD_SIZE
    head_at = [slice(h * width, (h + 1) * width) for h in range(KEY_VALUE_HEADS)]
    cosine, sine = tables[0], tables[1]
    allowed = tables[2] > 0.0
    x = x_ref[...]
    kept_x_ref[...] = x
    hidden = x.astype(F32)
    energy = jnp.mean(hidden * hidden, axis=-1, keepdims=True)
    n = (hidden * lax.rsqrt(energy + NORM_EPS) * gain[...]).astype(BF16)
    n_ref[...] = n
    low = dot_nt(n, down[...]).astype(BF16)
    low_ref[...] = low
    kv = dot(n, wqkv[:, QUERY_WIDTH:])
    k = rope(kv[:, :KEY_WIDTH], cosine, sine).astype(BF16)
    k_ref[...] = k
    v = kv[:, KEY_WIDTH:] + ADAPTER_SCALE * dot(low, up[:, QUERY_WIDTH:])
    v = v.astype(BF16)
    v_ref[...] = v
    k_turns, v_turns = turns_of(k), turns_of(v)
    tokens = hidden.shape[0]
    blended = []
    for h, at in enumerate(head_at):
        q = dot(n, wqkv[:, at]) + ADAPTER_SCALE * dot(low, up[:, at])
        q = rope(q, cosine, sine).astype(BF16)
        q_ref[:, at] = q
        scores = dot_nt(q, expand(k_turns, h)) * SCORE_SCALE
        shares = []
        for g in range(GROUP):
            weights = jnp.where(allowed, jnp.exp(scores[:, g * tokens : (g + 1) * tokens]), 0.0)
            shares.append((weights / jnp.sum(weights, axis=-1, keepdims=True)).astype(BF16))
        shares = jnp.concatenate(shares, axis=1)
        p_ref[:, h * GROUP * tokens : (h + 1) * GROUP * tokens] = shares
        if not last:
            blended.append(dot(shares, expand(v_turns, h)).astype(BF16))
    if not last:
        y_ref[...] = (hidden + dot(jnp.concatenate(blended, axis=1), wout[...])).astype(BF16)


def backward_kernel(turn, first, turn_ref, c_ref, *refs):
    out_ref, kept = refs[-4], refs[-3:]

    @pl.when(turn_ref[0] == turn)
    def _():
        if first:
            tables, up, wout, k_ref, v_ref, p_ref = refs[:6]
            fixed, held = (tables, None, None, up, None, wout), (None, None, k_ref, v_ref, p_ref)
        else:
            fixed, held = refs[:6], refs[6:11]
        backward_step(first, c_ref, *fixed, *held, out_ref, *kept)


def backward_step(
    first,
    c_ref, tables, gain, down, up, wqkv, wout,
    x_ref, q_ref, k_ref, v_ref, p_ref,
    out_ref, dq_ref, dv_ref, dlow_ref,
):
    width = GROUP * HEAD_SIZE
    head_at = [slice(h * width, (h + 1) * width) for h in range(KEY_VALUE_HEADS)]
    cosine, sine = tables[0], tables[1]
    k_turns, v_turns = turns_of(k_ref[...]), turns_of(v_ref[...])
    c = c_ref[...]
    tokens = c.shape[0]
    dn = None
    dlow = None
    dk_products, dv_products = [], []
    for h, at in enumerate(head_at):
        dblended = dot(c, wout[:, at]).astype(BF16)
        shares = p_ref[:, h * GROUP * tokens : (h + 1) * GROUP * tokens]
        dshares = dot_nt(dblended, expand(v_turns, h))
        dscores = []
        for g in range(GROUP):
            span = slice(g * tokens, (g + 1) * tokens)
            p = shares[:, span].astype(F32)
            dp = dshares[:, span]
            pdp = p * dp
            dscores.append(
                ((pdp - p * jnp.sum(pdp, axis=-1, keepdims=True)) * SCORE_SCALE).astype(BF16)
            )
        dscores = jnp.concatenate(dscores, axis=1)
        dq = dot(dscores, expand(k_turns, h))
        dq = rope(dq, cosine, -sine).astype(BF16)
        dq_ref[:, at] = dq
        part = dot_nt(dq, up[:, at])
        dlow = part if dlow is None else dlow + part
        dv_products.append(dot_tn(shares, dblended))
        if not first:
            dk_products.append(dot_tn(dscores, q_ref[:, at]))
            part = dot(dq, wqkv[at, :])
            dn = part if dn is None else dn + part
    dv = fold(dv_products).astype(BF16)
    dv_ref[...] = dv
    dlow = (ADAPTER_SCALE * (dlow + dot_nt(dv, up[:, QUERY_WIDTH:]))).astype(BF16)
    dlow_ref[...] = dlow
    if first:
        return
    dk = rope(fold(dk_products), cosine, -sine).astype(BF16)
    dn = dn + dot(jnp.concatenate([dk, dv], axis=1), wqkv[QUERY_WIDTH:, :])
    dn = dn + dot(dlow, down[...])
    hidden = x_ref[...].astype(F32)
    energy = jnp.mean(hidden * hidden, axis=-1, keepdims=True)
    scale = lax.rsqrt(energy + NORM_EPS)
    dy = dn * gain[...]
    along = jnp.mean(hidden * dy, axis=-1, keepdims=True)
    dh = scale * dy - hidden * (scale * scale * scale * along)
    out_ref[...] = (c.astype(F32) + dh).astype(BF16)


def turn_kernel(act, turn_ref, wqkv, wout, *refs):
    wqkv_turned, wout_turned = refs[-2:]

    @pl.when(act(turn_ref[0]))
    def _():
        wqkv_turned[...] = wqkv[...].T
        wout_turned[...] = wout[...].T


def turn_weights(act, section, weights, kept=()):
    return pl.pallas_call(
        functools.partial(turn_kernel, act),
        out_shape=[jax.ShapeDtypeStruct(t.shape[::-1], t.dtype) for t in weights],
        in_specs=[pl.BlockSpec(memory_space=pltpu.SMEM)]
        + [pl.BlockSpec(memory_space=pltpu.VMEM)] * (len(weights) + len(kept)),
        out_specs=[pl.BlockSpec(memory_space=pltpu.VMEM)] * len(weights),
        input_output_aliases={1 + len(weights) + i: i for i in range(len(kept))},
        compiler_params=pltpu.CompilerParams(vmem_limit_bytes=VMEM_LIMIT),
    )(section, *weights, *kept)


def grads_kernel(n_ref, low_ref, dq_ref, dv_ref, dlow_ref, g_ref):
    part = g_ref.shape[2]
    down = dot_tn(dlow_ref[...], n_ref[...]).astype(BF16)
    low = low_ref[...]
    up_q = ADAPTER_SCALE * dot_tn(low, dq_ref[...])[:RANK]
    up_v = ADAPTER_SCALE * dot_tn(low, dv_ref[...])[RANK : 2 * RANK]
    spare = jnp.zeros((RANK, g_ref.shape[0] * part - QUERY_WIDTH - KEY_WIDTH), F32)
    up = jnp.concatenate([up_q, up_v, spare], axis=1).astype(BF16)
    for i in range(g_ref.shape[0]):
        at = slice(i * part, (i + 1) * part)
        g_ref[i, 0 : 2 * RANK, :] = down[:, at]
        g_ref[i, 2 * RANK : 3 * RANK, :] = up[:, at]


def place_kernel(offsets, at_ref, *refs):
    qkv, out, sems = refs[-3:]
    z_count, _, rows, qkv_width = qkv.shape
    half, width = rows // 2, out.shape[3] // 2
    rest = pl.ds(qkv_width, width)
    ends = []
    for piece, offset in zip(refs, offsets):
        z_at = lax.rem(at_ref[0] + (offset + z_count), z_count)
        ends += [
            (piece.at[:, :, pl.ds(0, qkv_width)], qkv.at[z_at]),
            (piece.at[:, pl.ds(0, half), rest], out.at[z_at, :, :, pl.ds(0, width)]),
            (piece.at[:, pl.ds(half, half), rest], out.at[z_at, :, :, pl.ds(width, width)]),
        ]
    copies = [pltpu.make_async_copy(a, b, sems.at[i]) for i, (a, b) in enumerate(ends)]
    for copy in copies:
        copy.start()
    for copy in copies:
        copy.wait()


def place(offsets, z, pieces, z_count, kept=()):
    x_count, rows, columns = pieces[0].shape
    qkv_width = QUERY_WIDTH + 2 * KEY_WIDTH
    shapes = [
        (z_count, x_count, rows, qkv_width),
        (z_count, x_count, rows // 2, 2 * (columns - qkv_width)),
    ]
    first_kept = 1 + len(pieces)
    return pl.pallas_call(
        functools.partial(place_kernel, offsets),
        out_shape=[jax.ShapeDtypeStruct(shape, BF16) for shape in shapes],
        in_specs=[pl.BlockSpec(memory_space=pltpu.SMEM)]
        + [pl.BlockSpec(memory_space=pl.ANY)] * len(pieces)
        + [pl.BlockSpec(memory_space=pltpu.VMEM)] * len(kept),
        out_specs=[pl.BlockSpec(memory_space=pltpu.VMEM)] * len(shapes),
        scratch_shapes=[pltpu.SemaphoreType.DMA((3 * len(offsets),))],
        input_output_aliases={first_kept + i: i for i in range(len(kept))},
        compiler_params=pltpu.CompilerParams(vmem_limit_bytes=VMEM_LIMIT),
    )(z.astype(jnp.int32).reshape(1), *pieces, *kept)


def call(kernel, outs, args):
    return pl.pallas_call(
        kernel,
        out_shape=[jax.ShapeDtypeStruct(shape, dtype) for shape, dtype in outs],
        in_specs=[pl.BlockSpec(memory_space=pltpu.VMEM)] * len(args),
        out_specs=[pl.BlockSpec(memory_space=pltpu.VMEM)] * len(outs),
        compiler_params=pltpu.CompilerParams(vmem_limit_bytes=VMEM_LIMIT),
    )(*args)


def step(kernel, section, arrived, fixed, read, kept):
    args = (section, arrived, *fixed, *read, *kept)
    outs = [arrived, *kept]
    first_kept = len(args) - len(kept)
    made = pl.pallas_call(
        kernel,
        out_shape=[jax.ShapeDtypeStruct(t.shape, t.dtype) for t in outs],
        in_specs=[pl.BlockSpec(memory_space=pltpu.SMEM)]
        + [pl.BlockSpec(memory_space=pltpu.VMEM)] * (len(args) - 1),
        out_specs=[pl.BlockSpec(memory_space=pltpu.VMEM)] * len(outs),
        input_output_aliases={first_kept + i: 1 + i for i in range(len(kept))},
        compiler_params=pltpu.CompilerParams(vmem_limit_bytes=VMEM_LIMIT),
    )(*args)
    return made[0], tuple(made[1:])


def z_route(replicas, distance):
    return [(i, (i + distance * X_CHIPS) % replicas) for i in range(replicas)]


def x_route(replicas, distance):
    return [
        (i, i // X_CHIPS * X_CHIPS + (i % X_CHIPS + distance) % X_CHIPS) for i in range(replicas)
    ]


def gather_shards(shard, replica, replicas):
    rows, columns = shard.shape
    z_count = replicas // X_CHIPS
    x = replica % X_CHIPS
    along_z = functools.partial(z_route, replicas)
    along_x = functools.partial(x_route, replicas)
    far = lax.ppermute(shard, "dp", along_x(2))
    right = lax.ppermute(shard, "dp", along_x(1))
    left = lax.ppermute(shard, "dp", along_x(-1))
    line = jnp.zeros((X_CHIPS, rows, columns), shard.dtype)
    for turn, data in ((0, shard), (-1, right), (1, left), (2, far)):
        line = lax.dynamic_update_slice(line, data[None], ((x + turn) % X_CHIPS, 0, 0))
    ahead = behind = line
    pieces = [(0, line)]
    late = None
    middle = X_CHIPS // 2
    for step in range(1, z_count // 2):
        ahead = lax.ppermute(ahead, "dp", along_z(1))
        behind = lax.ppermute(behind, "dp", along_z(-1))
        pieces += [(-step, ahead), (step, behind)]
        if step == LATE_ROUND:
            late = ahead
        if step == PLACE_ROUND:
            early = [data for _, data in pieces]
            placed = place([offset for offset, _ in pieces], replica // X_CHIPS, early, z_count)
            pieces = []
        if step == PLACE_ROUND + 1:
            ahead, behind, *placed = lax.optimization_barrier((ahead, behind, *placed))
    upper = lax.ppermute(ahead[:middle], "dp", along_z(1))
    lower = lax.ppermute(behind[middle:], "dp", along_z(-1))
    pieces.append((z_count // 2, jnp.concatenate([upper, lower], axis=0)))
    return pieces, placed, late


def sum_over_replicas(parts, replicas):
    count, rows, columns = parts.shape
    blocks = replicas // count
    groups = [list(range(i, i + count)) for i in range(0, replicas, count)]

    def trade(t):
        return lax.all_to_all(t, "dp", 0, 0, axis_index_groups=groups, tiled=True)

    total = jnp.sum(trade(parts).astype(F32), axis=0).astype(BF16)
    for pair in (lambda block: block ^ 1, lambda block: blocks - 1 - block):
        route = [(i, pair(i // count) * count + i % count) for i in range(replicas)]
        other = lax.ppermute(total, "dp", route)
        total = (total.astype(F32) + other.astype(F32)).astype(BF16)
    whole = trade(jnp.broadcast_to(total[None], parts.shape)).astype(F32)
    return whole.transpose(1, 0, 2).reshape(rows, count * columns)


def exchange_tokens(source_tokens, send_counts, replica, replicas, section, sections, stream_count, late):
    slot_count = source_tokens.shape[0] // replicas
    width = source_tokens.shape[1] // sections
    share = lax.dynamic_slice_in_dim(source_tokens, section * width, width, 1)
    share, _ = lax.optimization_barrier((share, late))
    sent_counts = lax.dynamic_index_in_dim(send_counts, replica, 0, keepdims=False)
    send_start = jnp.cumsum(sent_counts) - sent_counts
    slot_ids = jnp.arange(slot_count, dtype=jnp.int32)
    occupied = slot_ids[None, :] < sent_counts[:, None]
    pick_rows = jnp.where(occupied, send_start[:, None] + slot_ids[None, :], -1).reshape(-1)
    own_rows = jnp.arange(source_tokens.shape[0], dtype=jnp.int32)
    choose = (pick_rows[:, None] == own_rows[None, :]).astype(BF16)
    packed = dot(choose, share).astype(BF16).reshape(replicas, slot_count, width)
    arrived = lax.all_to_all(packed, "dp", split_axis=0, concat_axis=0, tiled=True)
    incoming = lax.dynamic_index_in_dim(send_counts, replica, 1, keepdims=False)
    end_rows = jnp.cumsum(incoming)
    starts = end_rows - incoming
    places = jnp.arange(stream_count, dtype=jnp.int32)
    slot_place = starts[:, None] + slot_ids[None, :]
    slot_place = jnp.where(slot_ids[None, :] < incoming[:, None], slot_place, -1).reshape(-1)
    choose = (places[:, None] == slot_place[None, :]).astype(BF16)
    stream = dot(choose, arrived.reshape(replicas * slot_count, width)).astype(BF16)
    reach = 1
    while reach < sections:
        route = [(i + reach, i) for i in range(0, sections, 2 * reach)]
        stream = jnp.concatenate([stream, lax.ppermute(stream, "section", route)], axis=1)
        reach *= 2
    return stream, places < end_rows[replicas - 1]


def layout(segments, filled):
    micro_count, token_count = segments.shape
    tokens = micro_count * token_count
    segment = segments.reshape(tokens)
    places = jnp.arange(tokens, dtype=jnp.int32)
    sequence = places // token_count
    same = (segment[:, None] == segment[None, :]) & (sequence[:, None] == sequence[None, :])
    before = places[None, :] < places[:, None]
    position = jnp.sum(jnp.where(same & before, 1.0, 0.0).astype(F32), axis=1)
    alone = places[None, :] == places[:, None]
    allowed = (before & same & filled[:, None] & filled[None, :]) | alone
    half = HEAD_SIZE // 2
    frequency = ROPE_BASE ** (-2.0 * jnp.arange(half, dtype=F32) / HEAD_SIZE)
    angles = position[:, None] * frequency[None, :]
    cosine, sine = jnp.cos(angles), jnp.sin(angles)
    heads = LANES // HEAD_SIZE
    return (
        jnp.concatenate([cosine, cosine] * heads, axis=1),
        jnp.concatenate([-sine, sine] * heads, axis=1),
        allowed.astype(F32),
    )


def local(
    source_tokens,
    send_counts,
    doc_segments,
    out_cotangent,
    norm_gain,
    query_weight,
    frozen_key_matrix,
    frozen_value_matrix,
    out_weight,
    adapter_down,
    adapter_up_maps,
):
    replicas = lax.axis_size("dp")
    sections = lax.axis_size("section")
    replica = lax.axis_index("dp")
    section = lax.axis_index("section")
    features = source_tokens.shape[1]
    tokens = doc_segments.shape[0] * doc_segments.shape[1]

    half = out_weight.shape[2] // 2
    out_rows = jnp.concatenate([out_weight[0, :, :half], out_weight[0, :, half:]], axis=0)
    shard = jnp.concatenate(
        [query_weight[0], frozen_key_matrix[0], frozen_value_matrix[0], out_rows], axis=1
    )
    shards, placed, late = gather_shards(shard, replica, replicas)
    stream, filled = exchange_tokens(
        source_tokens, send_counts, replica, replicas, section, sections, tokens, late
    )
    cosine, sine, allowed = layout(doc_segments, filled)
    gain = norm_gain[0].reshape(1, features)
    tables = jnp.stack([cosine, sine, allowed])
    down = adapter_down[0].transpose(0, 2, 1).reshape(2 * RANK, features)
    up = adapter_up_maps[0]
    up = jnp.concatenate(
        [
            jnp.pad(up[:, :QUERY_WIDTH], ((0, RANK), (0, 0))),
            jnp.pad(up[:, QUERY_WIDTH:], ((RANK, 0), (0, 0))),
        ],
        axis=1,
    )

    saved_shapes = [
        ((tokens, features), BF16),
        ((tokens, QUERY_WIDTH), BF16),
        ((tokens, KEY_WIDTH), BF16),
        ((tokens, KEY_WIDTH), BF16),
        ((tokens, QUERY_HEADS * tokens), BF16),
        ((tokens, 2 * RANK), BF16),
        ((tokens, features), BF16),
    ]
    stream, tables, gain, down, up, *pieces = lax.optimization_barrier(
        (stream, tables, gain, down, up, *[data for _, data in shards])
    )
    z_count = replicas // X_CHIPS
    offsets = [offset for offset, _ in shards]
    wqkv, wout = place(offsets, replica // X_CHIPS, pieces, z_count, placed)
    wqkv = wqkv.reshape(-1, wqkv.shape[-1])
    wout = wout.reshape(-1, wout.shape[-1])
    fixed = (tables, gain, down, up, wqkv, wout)
    has_turn = section.astype(jnp.int32).reshape(1)
    x = stream
    saved = tuple(jnp.zeros(shape, dtype) for shape, dtype in saved_shapes)
    turned = turn_weights(lambda at: at != 0, has_turn, fixed[4:])
    for turn in range(sections):
        if turn == 2:
            turned = turn_weights(lambda at: at == 0, has_turn, fixed[4:], turned)
        last = turn + 1 == sections
        kernel = functools.partial(forward_kernel, turn, last)
        y, saved = step(kernel, has_turn, x, fixed, (), saved)
        if not last:
            x = lax.ppermute(y, "section", [(turn, turn + 1)])

    held, (low, normed) = saved[:5], saved[5:]
    c = out_cotangent
    kept = (
        jnp.zeros((tokens, QUERY_WIDTH), BF16),
        jnp.zeros((tokens, KEY_WIDTH), BF16),
        jnp.zeros((tokens, 2 * RANK), BF16),
    )
    for turn in range(sections - 1, -1, -1):
        kernel = functools.partial(backward_kernel, turn, turn == 0)
        if turn > 0:
            back, kept = step(kernel, has_turn, c, (*fixed[:4], *turned), held, kept)
        else:
            back, kept = step(kernel, has_turn, c, (tables, up, turned[1]), held[2:], kept)
        if turn > 0:
            c = lax.ppermute(back, "section", [(turn, turn - 1)])

    (grads,) = call(
        grads_kernel,
        [((SUM_GROUP, 3 * RANK, features // SUM_GROUP), BF16)],
        (normed, low, kept[0], kept[1], kept[2]),
    )
    grads = sum_over_replicas(grads, replicas)
    down_grads = grads[: 2 * RANK].reshape(2, RANK, features).transpose(0, 2, 1)
    up_grads = grads[2 * RANK :, : QUERY_WIDTH + KEY_WIDTH]
    return (down_grads[None], up_grads[None])


def solution(mesh):
    placed = (
        P("dp", None),
        P(),
        P("dp", None),
        P("dp", None),
        P("section", None),
        P("section", "dp", None),
        P("section", "dp", None),
        P("section", "dp", None),
        P("section", "dp", None),
        P("section", None, None, None),
        P("section", None, None),
    )
    return jax.shard_map(
        local,
        mesh=mesh,
        in_specs=placed,
        out_specs=(P("section", None, None, None), P("section", None, None)),
        check_vma=False,
    )
```
